256 devices in a mesh: ch: 4 (over z_hi, core), ha: 16 (over z_lo, x), dp: 4 (over y).
Axes of the slice: x: 4, y: 4, z: 8 (z_hi: 2, z_lo: 4; z = z_hi * 4 + z_lo), core: 2. Of those that a mesh axis runs over, the one named last changes fastest.
Arguments:
- features: bfloat16 [384, 4, 4, 32, 128], P('ch', 'dp', None, 'ha'), may hold values from -26 to 26
- frame_count: int32 [4], P('dp'), may hold values from 1 to 4, as said below
- norm1_gain: float32 [384], P('ch'), may hold values from 0.5 to 2
- norm1_shift: float32 [384], P('ch'), may hold values from -3 to 3
- qkv_weight: bfloat16 [384, 1152], replicated, may hold values from -0.51031036 to 0.51031036
- qkv_bias: float32 [1152], replicated, may hold values from -3 to 3
- out_weight: bfloat16 [384, 384], replicated, may hold values from -0.3125 to 0.3125
- out_bias: float32 [384], replicated, may hold values from -3 to 3
- norm2_gain: float32 [384], P('ch'), may hold values from 0.5 to 2
- norm2_shift: float32 [384], P('ch'), may hold values from -3 to 3
- conv_weight: bfloat16 [3, 3, 3, 384, 384], P(None, None, None, 'ch'), may hold values from -0.0625 to 0.0625
- conv_bias: float32 [384], P('ch'), may hold values from -3 to 3
- cotangent: bfloat16 [384, 4, 4, 32, 128], P('ch', 'dp', None, 'ha'), may hold values from -0.0234375 to 0.0234375
Outputs:
- mixed: bfloat16 [384, 4, 4, 32, 128], P('ch', 'dp', None, 'ha')
- weight_grad: float32 [3, 3, 3, 384, 384], P(None, None, None, 'ch')
The draws below stay inside these ranges and needn't reach their ends.
Inputs may be any that keep to these rules, and one draw needn't show every extreme that they name: `frame_count`: some clip has all 4 frames valid and some clip only one.
All inputs are finite; a program needn't handle non-finite values.
Results may differ from the reference program's by a relative error of at most 0.015.
Values may be sent and summed in bfloat16 or wider, within the bound.
No kernel may reach another device: no remote copies, remote signals or barrier semaphores. Data moves between devices by JAX's collectives and lax.ppermute only.
A program may use at most 64 MiB of HBM per device.

```python
import math
import jax
import jax.numpy as jnp
from jax import lax

C = 384
GROUPS = 32
FR = 4
W = 128
CLIPS = 4
HEIGHT = 32


def draw_features(key, part):
    first = jax.random.fold_in(jax.random.fold_in(key, 11), 0)
    shape = (C, CLIPS, FR, HEIGHT, W)
    height_pos = lax.broadcasted_iota(jnp.float32, shape, 3) / (HEIGHT - 1)
    ramp = 1.0 + 2.0 * height_pos
    return (jnp.clip(jax.random.normal(first, shape, jnp.float32), -5.0, 5.0) * ramp).astype(jnp.bfloat16)


def draw_frame_count(key, part):
    first, second = jax.random.split(jax.random.fold_in(key, 23))
    counts = jax.random.randint(first, (CLIPS,), 1, FR + 1)
    chosen = jax.random.randint(second, (), 0, CLIPS)
    other = (chosen + 1) % CLIPS
    places = jnp.arange(CLIPS)
    counts = jnp.where(places == chosen, FR, counts)
    counts = jnp.where(places == other, 1, counts)
    return counts.astype(jnp.int32)


def draw_qkv_weight(key, part):
    first, second, third = jax.random.split(jax.random.fold_in(key, 37), 3)
    query_w = jnp.clip(jax.random.normal(first, (C, C), jnp.float32), -5.0, 5.0) * (1.6 * C ** (-0.5))
    noise = jnp.clip(jax.random.normal(second, (C, C), jnp.float32), -5.0, 5.0)
    key_w = noise * (1.6 * C ** (-0.5))
    value_w = jnp.clip(jax.random.normal(third, (C, C), jnp.float32), -5.0, 5.0) * C ** (-0.5)
    return jnp.concatenate([query_w, key_w, value_w], axis=1).astype(jnp.bfloat16)


def shard_levels(rng, dims, pieces, least, largest):
    loudness, own = 1.0, jax.random.fold_in(rng, 6)
    for axis_at, blocks in pieces:
        draws = jnp.exp(jax.random.uniform(jax.random.fold_in(own, axis_at), (blocks,), jnp.float32, least / len(pieces), largest / len(pieces)))
        loudness = loudness * jnp.repeat(draws, dims[axis_at] // blocks).reshape([-1 if axis == axis_at else 1 for axis in range(len(dims))])
    return loudness


def gaussian(key, extent, width, most, cuts=(), dtype=jnp.bfloat16):
    drawn = jax.random.normal(key, extent, jnp.float32) * width
    if len(cuts) > 0:
        drawn = shard_levels(key, extent, cuts, -0.22, 0.18) * drawn
    return jnp.clip(drawn, min=-most, max=most).astype(dtype)


def setup_inputs(seed: int = 0) -> dict:
    seeds = jax.random.split(jax.random.key(seed), 14)
    features = draw_features(jax.random.fold_in(seeds[13], 71), 0)
    frame_count = draw_frame_count(jax.random.fold_in(seeds[13], 71), 0)
    norm1_gain = jnp.clip(jnp.exp(math.log(2.0) - 1.3862944 * jax.random.uniform(seeds[2], (C,), jnp.float32) ** shard_levels(seeds[2], (C,), ((0, 4),), -0.2, 0.2)), 0.5, 2.0)
    norm1_shift = gaussian(seeds[3], (C,), 0.5, 3.0, ((0, 4),), jnp.float32)
    qkv_weight = draw_qkv_weight(jax.random.fold_in(seeds[13], 71), 0)
    qkv_bias = gaussian(seeds[5], (3 * C,), 0.5, 3.0, (), jnp.float32)
    out_weight = gaussian(seeds[6], (C, C), C ** -0.5, 0.3125)
    out_bias = gaussian(seeds[7], (C,), 0.3, 3.0, (), jnp.float32)
    norm2_gain = jnp.clip(jnp.exp(math.log(2.0) - 1.3862944 * jax.random.uniform(seeds[8], (C,), jnp.float32) ** shard_levels(seeds[8], (C,), ((0, 4),), -0.2, 0.2)), 0.5, 2.0)
    norm2_shift = gaussian(seeds[9], (C,), 0.5, 3.0, ((0, 4),), jnp.float32)
    conv_weight = gaussian(seeds[10], (3, 3, 3, C, C), (27 * C) ** -0.5, 0.0625, ((3, 4),))
    conv_bias = gaussian(seeds[11], (C,), 0.3, 3.0, ((0, 4),), jnp.float32)
    cotangent = gaussian(seeds[12], (C, CLIPS, FR, HEIGHT, W), ((CLIPS * FR * HEIGHT * W) ** -0.5), 0.0234375, ((0, 4), (1, 4), (3, 16)))
    return dict(features=features, frame_count=frame_count, norm1_gain=norm1_gain, norm1_shift=norm1_shift, qkv_weight=qkv_weight, qkv_bias=qkv_bias, out_weight=out_weight, out_bias=out_bias, norm2_gain=norm2_gain, norm2_shift=norm2_shift, conv_weight=conv_weight, conv_bias=conv_bias, cotangent=cotangent)


EPS = 1e-06

def frame_mask(frame_count):
    position = lax.broadcasted_iota(jnp.int32, (frame_count.shape[0], FR), 1)
    return (position < frame_count[:, None].astype(jnp.int32)).astype(jnp.float32)

def group_norm(values, mask, count, gain, shift):
    data = values.astype(jnp.float32).reshape(GROUPS, C // GROUPS, CLIPS, FR, HEIGHT * W)
    first = jnp.einsum('gkbfp,bf->gb', data, mask)
    second = jnp.einsum('gkbfp,bf->gb', data * data, mask)
    mean = first / count[None, :]
    var = second / count[None, :] - mean * mean
    scale = lax.rsqrt(var + EPS)
    normed = (data - mean[:, None, :, None, None]) * scale[:, None, :, None, None]
    normed = normed.reshape(C, CLIPS, FR, HEIGHT, W)
    return normed * gain[:, None, None, None, None] + shift[:, None, None, None, None]

def reference(features, frame_count, norm1_gain, norm1_shift, qkv_weight, qkv_bias, out_weight, out_bias, norm2_gain, norm2_shift, conv_weight, conv_bias, cotangent):
    mask = frame_mask(frame_count)
    count = frame_count.astype(jnp.float32) * (C // GROUPS * HEIGHT * W)
    normed = group_norm(features, mask, count, norm1_gain, norm1_shift).astype(jnp.bfloat16)
    frame_tokens = HEIGHT * W
    block_rows = math.gcd(frame_tokens, 1024)
    items = jnp.moveaxis(normed.reshape(C, CLIPS * FR, frame_tokens), 1, 0)
    qkv_full = qkv_weight.astype(jnp.float32)

    def attend_frame(item):
        proj = jnp.dot(item.T.astype(jnp.float32), qkv_full, preferred_element_type=jnp.float32) + qkv_bias
        proj = proj.astype(jnp.bfloat16)
        queries = proj[:, :C]
        keys = proj[:, C:2 * C].astype(jnp.float32)
        values = proj[:, 2 * C:].astype(jnp.float32)

        def one_block(query):
            scores = jnp.dot(query.astype(jnp.float32), keys.T, preferred_element_type=jnp.float32) * C ** (-0.5)
            top = lax.optimization_barrier(jnp.max(scores, axis=1, keepdims=True))
            weights = jnp.exp(scores - top)
            total = lax.optimization_barrier(jnp.sum(weights, axis=1, keepdims=True))
            rounded = lax.optimization_barrier(weights.astype(jnp.bfloat16))
            out = jnp.dot(rounded.astype(jnp.float32), values, preferred_element_type=jnp.float32) / total
            return out.astype(jnp.bfloat16)
        blocks = lax.map(one_block, queries.reshape(frame_tokens // block_rows, block_rows, C))
        return blocks.reshape(frame_tokens, C)
    attended = lax.map(attend_frame, items)
    update = lax.dot_general(out_weight.astype(jnp.float32), attended.astype(jnp.float32), (((0,), (2,)), ((), ())), preferred_element_type=jnp.float32)
    update = (update + out_bias[:, None, None]).astype(jnp.bfloat16).reshape(C, CLIPS, FR, HEIGHT, W)
    hidden = (features.astype(jnp.float32) + update.astype(jnp.float32)).astype(jnp.bfloat16)
    gated = jax.nn.silu(group_norm(hidden, mask, count, norm2_gain, norm2_shift)).astype(jnp.bfloat16)
    padded = jnp.pad(gated.astype(jnp.float32), ((0, 0), (0, 0), (2, 0), (1, 1), (1, 1)))
    masked_cot = (cotangent * mask.astype(jnp.bfloat16)[None, :, :, None, None]).astype(jnp.float32)
    conv = jnp.zeros((C, CLIPS, FR, HEIGHT, W), jnp.float32)
    grads = []
    for kt in range(3):
        for ky in range(3):
            for kx in range(3):
                window = padded[:, :, kt:kt + FR, ky:ky + HEIGHT, kx:kx + W]
                conv = conv + lax.dot_general(conv_weight[kt, ky, kx].astype(jnp.float32), window, (((0,), (0,)), ((), ())), preferred_element_type=jnp.float32)
                grads.append(lax.dot_general(window, masked_cot, (((1, 2, 3, 4), (1, 2, 3, 4)), ((), ())), preferred_element_type=jnp.float32))
    weight_grad = jnp.stack(grads).reshape(3, 3, 3, C, C)
    mixed = mask[None, :, :, None, None] * (hidden.astype(jnp.float32) + conv + conv_bias[:, None, None, None, None])
    return (mixed.astype(jnp.bfloat16), weight_grad)
```

```python
import itertools
import jax
import jax.numpy as jnp
from jax import lax
from jax.experimental import pallas as pl
from jax.experimental.pallas import tpu as pltpu
from jax.sharding import Mesh, PartitionSpec as P

EPS = 1e-06
SIZES = {"zh": 2, "co": 2, "zl": 4, "x": 4, "y": 4}
BF, F32 = jnp.bfloat16, jnp.float32
VMEM = 56 * 1024 * 1024


def permute(value, axes, target):
    sizes = [SIZES[a] for a in axes]

    def flat(index):
        at = 0
        for i, n in zip(index, sizes):
            at = at * n + i
        return at

    pairs = []
    for index in itertools.product(*[range(n) for n in sizes]):
        to = target(*index)
        if to is not None:
            pairs.append((flat(index), flat(to)))
    return lax.ppermute(value, axes, pairs)


def ring(value, axis):
    return [value] + [permute(value, (axis,), lambda i: ((i + s) % 4,)) for s in (1, 2, 3)]


def halo(last, first):
    def up(zl, x):
        at = zl * 4 + x + 1
        return (at // 4, at % 4) if at < 16 else None

    def down(zl, x):
        at = zl * 4 + x - 1
        return (at // 4, at % 4) if at >= 0 else None

    return permute(last, ("zl", "x"), up), permute(first, ("zl", "x"), down)


def spread(value, axes, count):
    copies = jnp.broadcast_to(value[None], (count,) + value.shape)
    return lax.all_to_all(copies, axes, 0, 0, tiled=True)


def own_other(array, co):
    first, second = array[:, 0], array[:, 1]
    own = jnp.where(co == 0, first, second)
    other = jnp.where(co == 0, second, first)
    return own, other


def silu_norm(data, mean, scale, gain, shift):
    u = (data.astype(F32) - mean) * scale * gain + shift
    return u / (1.0 + jnp.exp(-u))


def shifted(g, kx):
    if kx == 1:
        return g
    lane = lax.broadcasted_iota(jnp.int32, g.shape, 1)
    if kx == 0:
        return jnp.where(lane == 0, 0.0, pltpu.roll(g, 1, 1))
    return jnp.where(lane == 127, 0.0, pltpu.roll(g, 127, 1))


def grad_kernel(hid, cot, mean, scale, gain, shift, out, gs, cs):
    cs[...] = jnp.zeros_like(cs)
    for s in range(4):
        for f in range(4):
            for r in range(2):
                at = f * 256 + r * 128
                to = f * 1024 + s * 256 + r * 128
                g = silu_norm(hid[s, :, at : at + 128], mean[s], scale[s], gain[...], shift[...])
                for kx in range(3):
                    gs[kx * 96 : kx * 96 + 96, to : to + 128] = shifted(g, kx).astype(BF)
            for ky in range(3):
                at = f * 512 + (2 - ky) * 128
                to = f * 1024 + s * 256
                cs[ky * 128 : ky * 128 + 96, to : to + 256] = cot[s, :, at : at + 256]
    out[27 * 96 :, :] = jnp.zeros((96, 96), BF)
    for kt in range(3):
        table = lax.dot_general(
            gs[:, : (2 + kt) * 1024],
            cs[:, (2 - kt) * 1024 :],
            (((1,), (1,)), ((), ())),
            preferred_element_type=F32,
        ).astype(BF)
        for ky in range(3):
            at = (kt * 9 + ky * 3) * 96
            out[at : at + 288, :] = table[:, ky * 128 : ky * 128 + 96]


def conv_kernel(hid, weight, mean, scale, gain, shift, rows, out, stack):
    stack[:, :512] = jnp.zeros((864, 512), BF)
    for f in range(4):
        for p in range(4):
            at = f * 512 + p * 128
            g = silu_norm(hid[:, at : at + 128], mean[...], scale[...], gain[...], shift[...])
            g = jnp.where(rows[:, at : at + 128] > 0.0, g, 0.0)
            for kx in range(3):
                piece = shifted(g, kx).astype(BF)
                for ky in range(3):
                    r = p - ky
                    if 0 <= r < 2:
                        to = 512 + f * 256 + r * 128
                        row = (ky * 3 + kx) * 96
                        stack[row : row + 96, to : to + 128] = piece
    total = jnp.zeros((384, 1024), F32)
    for kt in range(3):
        total = total + jnp.dot(
            weight[kt], stack[:, kt * 256 : kt * 256 + 1024], preferred_element_type=F32
        )
    out[...] = total.astype(BF)


def body(
    features,
    frame_count,
    norm1_gain,
    norm1_shift,
    qkv_weight,
    qkv_bias,
    out_weight,
    out_bias,
    norm2_gain,
    norm2_shift,
    conv_weight,
    conv_bias,
    cotangent,
):
    zh, co, zl = lax.axis_index("zh"), lax.axis_index("co"), lax.axis_index("zl")
    x, y = lax.axis_index("x"), lax.axis_index("y")
    ch = zh * 2 + co
    frames = features.reshape(96, 4, 256)
    valid = frame_count[0]
    mask = (lax.iota(jnp.int32, 4) < valid).astype(F32)
    count = valid.astype(F32) * (12 * 32 * 128)

    by_frame = jnp.repeat(frames.transpose(1, 0, 2), 2, axis=0)
    got = lax.all_to_all(by_frame, ("zh", "zl"), 0, 0, tiled=True)
    mine = got.reshape(2, 4, 96, 256).transpose(0, 2, 1, 3).reshape(192, 1024)
    parts = ring(mine, "x")
    others = [permute(p, ("co",), lambda i: (1 - i,)) for p in parts]

    data = frames.astype(F32).reshape(8, 12, 4, 256)
    first = jnp.einsum("gkfp,f->g", data, mask)
    second = jnp.einsum("gkfp,f->g", data * data, mask)
    packed = jnp.concatenate([first, second, norm1_gain, norm1_shift, jnp.zeros((48,), F32)])
    packed = spread(packed.reshape(2, 128), ("zh", "co", "zl", "x"), 64).reshape(4, 16, 256)
    sums = jnp.sum(packed[:, :, :16], axis=1)
    mean = sums[:, :8] / count
    var = sums[:, 8:] / count - mean * mean
    scale = lax.rsqrt(var + EPS)
    vectors = jnp.stack(
        [
            jnp.repeat(mean, 12, axis=1),
            jnp.repeat(scale, 12, axis=1),
            packed[:, 0, 16:112],
            packed[:, 0, 112:208],
        ]
    )
    vectors = vectors.reshape(8, 2, 96)
    own_vec, other_vec = own_other(vectors, co)
    own_vec, other_vec = own_vec.reshape(4, 192), other_vec.reshape(4, 192)

    def normalize(raw, vec):
        v = vec[:, :, None]
        return ((raw.astype(F32) - v[0]) * v[1] * v[2] + v[3]).astype(BF)

    weight_own, weight_other = own_other(qkv_weight.reshape(2, 2, 96, 1152), co)
    weight = jnp.concatenate(
        [weight_own.reshape(192, 1152), weight_other.reshape(192, 1152)], axis=0
    )
    tokens = jnp.concatenate(
        [
            normalize(jnp.concatenate(parts, axis=1), own_vec),
            normalize(jnp.concatenate(others, axis=1), other_vec),
        ],
        axis=0,
    )
    slot = (2 * (zl % 2) + co) * 256
    raw_own = lax.dynamic_slice(parts[0], (0, slot), (192, 256))
    raw_other = lax.dynamic_slice(others[0], (0, slot), (192, 256))
    mine_q = lax.dynamic_slice(tokens, (0, slot), (384, 256))
    queries = lax.dot_general(
        mine_q, weight[:, :384], (((0,), (0,)), ((), ())), preferred_element_type=F32
    )
    queries = (queries + qkv_bias[:384]).astype(BF)
    lifted = lax.dot_general(
        queries, weight[:, 384:768], (((1,), (1,)), ((), ())), preferred_element_type=F32
    ).astype(BF)
    offset = jnp.sum(queries.astype(F32) * qkv_bias[384:768], axis=1, keepdims=True)
    scores = jnp.dot(lifted, tokens, preferred_element_type=F32)
    scores = (scores + offset) * (384 ** (-0.5))
    top = jnp.max(scores, axis=1, keepdims=True)
    ew = jnp.exp(scores - top)
    total = jnp.sum(ew, axis=1, keepdims=True)
    mixed_tokens = lax.dot_general(
        ew.astype(BF), tokens, (((1,), (1,)), ((), ())), preferred_element_type=F32
    )
    mixed_tokens = (mixed_tokens / total).astype(BF)
    attended = jnp.dot(mixed_tokens, weight[:, 768:], preferred_element_type=F32)
    attended = (attended + qkv_bias[768:]).astype(BF)
    update = lax.dot_general(
        out_weight, attended, (((0,), (1,)), ((), ())), preferred_element_type=F32
    )
    update = (update + out_bias[:, None]).astype(BF)
    lower = jnp.where(co == 0, raw_own, raw_other).reshape(2, 96, 256)
    upper = jnp.where(co == 0, raw_other, raw_own).reshape(2, 96, 256)
    raw = jnp.stack([lower, upper], axis=1).reshape(384, 256)
    hidden_q = (raw.astype(F32) + update.astype(F32)).astype(BF)

    frame = 2 * zh + zl // 2
    pieces = []
    for k in range(4):
        piece = lax.dynamic_slice(hidden_q, ((frame ^ k) * 96, 0), (96, 256))

        def to_channels(zh, co, zl, k=k):
            c = (2 * zh + zl // 2) ^ k
            return (c // 2, c % 2, 2 * (zl % 2) + co)

        pieces.append(permute(piece, ("zh", "co", "zl"), to_channels))
    pieces = jnp.stack(pieces)
    hidden = jnp.stack(
        [lax.dynamic_index_in_dim(pieces, ch ^ g, 0, keepdims=False) for g in range(4)], axis=1
    )

    data = hidden_q.astype(F32).reshape(32, 12 * 256)
    live = (frame < valid).astype(F32)
    packed = jnp.concatenate([jnp.sum(data, axis=1), jnp.sum(data * data, axis=1)]) * live
    packed = jnp.concatenate([packed, jnp.zeros((64,), F32)]).reshape(1, 128)
    packed = spread(packed, ("zh", "co", "zl", "x"), 64)
    sums = jnp.sum(packed, axis=(0, 1))[:64].reshape(2, 4, 8)
    sums = lax.dynamic_index_in_dim(sums, ch, 1, keepdims=False)
    mean = sums[0] / count
    var = sums[1] / count - mean * mean
    packed = jnp.concatenate([mean, lax.rsqrt(var + EPS), jnp.zeros((112,), F32)]).reshape(1, 128)
    packed = jnp.concatenate(ring(packed, "y"), axis=0)
    means = jnp.repeat(packed[:, :8], 12, axis=1)[:, :, None]
    scales = jnp.repeat(packed[:, 8:16], 12, axis=1)[:, :, None]

    masked = (cotangent.reshape(96, 4, 256) * mask.astype(BF)[None, :, None]).reshape(96, 1024)
    blocks = jnp.stack(
        [
            permute(
                masked,
                ("zh", "co", "y"),
                lambda zh, co, y: (((y + k) % 4) // 2, (y + k) % 2, 2 * zh + co),
            )
            for k in range(4)
        ]
    )
    blocks = jnp.concatenate([blocks, blocks], axis=0)
    blocks = lax.dynamic_slice_in_dim(blocks, (ch - y + 4) % 4, 4, 0).reshape(4, 96, 4, 2, 128)
    before, after = halo(blocks[:, :, :, 1], blocks[:, :, :, 0])
    blocks = jnp.concatenate([before[:, :, :, None], blocks, after[:, :, :, None]], axis=3)
    blocks = blocks.reshape(4, 96, 2048)

    clips = jnp.stack(ring(hidden.reshape(96, 1024), "y"))
    gain, shift = norm2_gain[:, None], norm2_shift[:, None]
    params = pltpu.CompilerParams(vmem_limit_bytes=VMEM)
    table = pl.pallas_call(
        grad_kernel,
        out_shape=jax.ShapeDtypeStruct((2688, 96), BF),
        scratch_shapes=[pltpu.VMEM((288, 4096), BF), pltpu.VMEM((384, 4096), BF)],
        compiler_params=params,
        name="weight_grad",
    )(clips, blocks, means, scales, gain, shift)
    shares = lax.all_to_all(table.reshape(16, 168, 96), ("zl", "x"), 0, 0, tiled=True)
    share = jnp.sum(shares.astype(F32), axis=0).astype(BF)
    table = spread(share, ("zl", "x"), 16).reshape(2688, 96)
    tables = jnp.stack(ring(table, "y"))
    grad = jnp.concatenate(
        [lax.dynamic_index_in_dim(tables, (y - j) % 4, 0, keepdims=False)[:2592] for j in range(4)],
        axis=1,
    )
    weight_grad = grad.astype(F32).reshape(3, 3, 3, 96, 384)

    rows = hidden.reshape(96, 4, 2, 128)
    before, after = halo(rows[:, :, 1], rows[:, :, 0])
    rows = jnp.concatenate([before[:, :, None], rows, after[:, :, None]], axis=2)
    at = lax.iota(jnp.int32, 16) % 4
    place = zl * 4 + x
    inside = jnp.where(at == 0, place > 0, jnp.where(at == 3, place < 15, True))
    inside = jnp.repeat(inside.astype(F32), 128)[None, :]
    kernels = conv_weight.transpose(0, 4, 1, 2, 3).reshape(3, 384, 864)
    partial = pl.pallas_call(
        conv_kernel,
        out_shape=jax.ShapeDtypeStruct((384, 1024), BF),
        scratch_shapes=[pltpu.VMEM((864, 1536), BF)],
        compiler_params=params,
        name="convolution",
    )(rows.reshape(96, 2048), kernels, means[0], scales[0], gain, shift, inside)
    partial = partial.reshape(4, 96, 1024)
    conv = lax.dynamic_index_in_dim(partial, ch, 0, keepdims=False).astype(F32)
    for k in range(1, 4):
        piece = lax.dynamic_index_in_dim(partial, ch ^ k, 0, keepdims=False)
        piece = permute(
            piece, ("zh", "co"), lambda zh, co, k=k: (zh ^ (k >> 1), co ^ (k & 1))
        )
        conv = conv + piece.astype(F32)
    mixed = hidden.reshape(96, 1024).astype(F32) + conv + conv_bias[:, None]
    mixed = (mixed.reshape(96, 4, 256) * mask[None, :, None]).astype(BF)
    return mixed.reshape(96, 1, 4, 2, 128), weight_grad


def solution(mesh):
    cut = Mesh(mesh.devices.reshape(2, 2, 4, 4, 4), ("zh", "co", "zl", "x", "y"))
    ch, ha = ("zh", "co"), ("zl", "x")
    maps = P(ch, "y", None, ha, None)
    placed = (
        maps,
        P("y"),
        P(ch),
        P(ch),
        P(),
        P(),
        P(),
        P(),
        P(ch),
        P(ch),
        P(None, None, None, ch, None),
        P(ch),
        maps,
    )
    return jax.shard_map(
        body,
        mesh=cut,
        in_specs=placed,
        out_specs=(maps, P(None, None, None, ch, None)),
        check_vma=False,
    )
```

```python
import itertools
import jax
import jax.numpy as jnp
from jax import lax
from jax.experimental import pallas as pl
from jax.experimental.pallas import tpu as pltpu
from jax.sharding import Mesh, PartitionSpec as P

EPS = 1e-06
SIZES = {"zh": 2, "co": 2, "zl": 4, "x": 4, "y": 4}
BF, F32 = jnp.bfloat16, jnp.float32
VMEM = 56 * 1024 * 1024


def permute(value, axes, target):
    sizes = [SIZES[a] for a in axes]

    def flat(index):
        at = 0
        for i, n in zip(index, sizes):
            at = at * n + i
        return at

    pairs = []
    for index in itertools.product(*[range(n) for n in sizes]):
        to = target(*index)
        if to is not None:
            pairs.append((flat(index), flat(to)))
    return lax.ppermute(value, axes, pairs)


def ring(value, axis):
    return [value] + [permute(value, (axis,), lambda i: ((i + s) % 4,)) for s in (1, 2, 3)]


def halo(last, first):
    def up(zl, x):
        at = zl * 4 + x + 1
        return (at // 4, at % 4) if at < 16 else None

    def down(zl, x):
        at = zl * 4 + x - 1
        return (at // 4, at % 4) if at >= 0 else None

    return permute(last, ("zl", "x"), up), permute(first, ("zl", "x"), down)


def spread(value, axes, count):
    copies = jnp.broadcast_to(value[None], (count,) + value.shape)
    return lax.all_to_all(copies, axes, 0, 0, tiled=True)


def cost(flops, size):
    return pl.CostEstimate(flops=flops, bytes_accessed=size, transcendentals=0)


def column(rows, place):
    lane = lax.broadcasted_iota(jnp.int32, (96, 128), 1)
    return jnp.sum(jnp.where(lane == place, rows, 0.0), axis=1, keepdims=True)


def pack_kernel(valid, frames, gain, shift, out):
    first = jnp.zeros((96, 128), F32)
    second = jnp.zeros((96, 128), F32)
    for f in range(4):
        data = frames[:, f * 256 : f * 256 + 256].astype(F32)
        data = jnp.where(f < valid[0], data, 0.0)
        square = data * data
        first += data[:, :128] + data[:, 128:]
        second += square[:, :128] + square[:, 128:]
    row = lax.broadcasted_iota(jnp.int32, (96, 128), 0) // 12
    lane = lax.broadcasted_iota(jnp.int32, (96, 128), 1)
    first = jnp.sum(first, axis=1, keepdims=True)
    second = jnp.sum(second, axis=1, keepdims=True)
    sums = jnp.where(row == lane, first, jnp.where(row + 8 == lane, second, 0.0))
    sums = jnp.sum(sums, axis=0, keepdims=True)
    pad = jnp.zeros((1, 32), F32)
    rows = jnp.concatenate(
        [
            sums,
            jnp.concatenate([gain[...], pad], axis=1),
            jnp.concatenate([shift[...], pad], axis=1),
            jnp.zeros((1, 128), F32),
        ],
        axis=0,
    )
    out[...] = jnp.broadcast_to(rows[None], out.shape)


def attend_kernel(
    at,
    packed,
    own0,
    own1,
    own2,
    own3,
    other0,
    other1,
    other2,
    other3,
    qkv,
    qkv_bias,
    out_weight,
    out_bias,
    hidden,
    sums,
    tokens,
    scores,
):
    co, slot, valid, frame = at[0], at[1], at[2], at[3]
    count = valid.astype(F32) * (12 * 32 * 128)
    group = lax.broadcasted_iota(jnp.int32, (96, 128), 0) // 12
    entry = lax.broadcasted_iota(jnp.int32, (96, 128), 0)
    for which, parts in ((co, (own0, own1, own2, own3)), (1 - co, (other0, other1, other2, other3))):
        for zh in range(2):
            c = 2 * zh + which
            table = jnp.sum(packed[c], axis=0)
            mean = column(table[0:1], group) / count
            var = column(table[0:1], group + 8) / count - mean * mean
            scale = lax.rsqrt(var + EPS)
            gain = column(packed[c, 0, 1:2], entry)
            shift = column(packed[c, 0, 2:3], entry)
            rows = pl.ds(pl.multiple_of(c * 96, 32), 96)
            for s in range(4):
                data = parts[s][zh * 96 : zh * 96 + 96, :].astype(F32)
                data = (data - mean) * scale * gain + shift
                tokens[rows, s * 1024 : s * 1024 + 1024] = data.astype(BF)
    lanes = pl.ds(pl.multiple_of(slot, 256), 256)
    queries = lax.dot_general(
        tokens[:, lanes], qkv[:, :384], (((0,), (0,)), ((), ())), preferred_element_type=F32
    )
    queries = (queries + qkv_bias[:, :384]).astype(BF)
    lifted = lax.dot_general(
        queries, qkv[:, 384:768], (((1,), (1,)), ((), ())), preferred_element_type=F32
    ).astype(BF)
    offset = jnp.sum(queries.astype(F32) * qkv_bias[:, 384:768], axis=1, keepdims=True)
    top = jnp.full((256, 128), -jnp.inf, F32)
    for j in range(8):
        piece = jnp.dot(lifted, tokens[:, j * 512 : j * 512 + 512], preferred_element_type=F32)
        piece = (piece + offset) * (384 ** (-0.5))
        scores[:, j * 512 : j * 512 + 512] = piece
        for i in range(4):
            top = jnp.maximum(top, piece[:, i * 128 : i * 128 + 128])
    top = jnp.max(top, axis=1, keepdims=True)
    total = jnp.zeros((256, 128), F32)
    acc = jnp.zeros((256, 384), F32)
    for j in range(8):
        ew = jnp.exp(scores[:, j * 512 : j * 512 + 512] - top)
        for i in range(4):
            total += ew[:, i * 128 : i * 128 + 128]
        acc += lax.dot_general(
            ew.astype(BF),
            tokens[:, j * 512 : j * 512 + 512],
            (((1,), (1,)), ((), ())),
            preferred_element_type=F32,
        )
    total = jnp.sum(total, axis=1, keepdims=True)
    acc = (acc / total).astype(BF)
    attended = jnp.dot(acc, qkv[:, 768:], preferred_element_type=F32)
    attended = (attended + qkv_bias[:, 768:]).astype(BF)
    update = lax.dot_general(
        out_weight[...], attended, (((0,), (1,)), ((), ())), preferred_element_type=F32
    )
    hidden[...] = (update + out_bias[...]).astype(BF)
    for which, part in ((co, own0), (1 - co, other0)):
        for zh in range(2):
            rows = pl.ds(pl.multiple_of((2 * zh + which) * 96, 32), 96)
            raw = part[zh * 96 : zh * 96 + 96, lanes].astype(F32)
            hidden[rows, :] = (raw + hidden[rows, :].astype(F32)).astype(BF)
    data = jnp.where(frame < valid, hidden[...].astype(F32), 0.0)
    first = jnp.sum(data, axis=1, keepdims=True)
    second = jnp.sum(data * data, axis=1, keepdims=True)
    row = lax.broadcasted_iota(jnp.int32, (384, 128), 0) // 12
    lane = lax.broadcasted_iota(jnp.int32, (384, 128), 1)
    table = jnp.where(row == lane, first, jnp.where(row + 32 == lane, second, 0.0))
    table = jnp.sum(table, axis=0, keepdims=True)
    sums[...] = jnp.broadcast_to(table[None], sums.shape)


def gate_kernel(at, packed, piece0, piece1, piece2, piece3, gain, shift, gated, hidden, held):
    ch, valid = at[0], at[1]
    count = valid.astype(F32) * (12 * 32 * 128)
    table = jnp.sum(packed[...], axis=0)
    group = lax.broadcasted_iota(jnp.int32, (96, 128), 0) // 12 + ch * 8
    mean = column(table, group) / count
    var = column(table, group + 32) / count - mean * mean
    scale = lax.rsqrt(var + EPS)
    for k, piece in enumerate((piece0, piece1, piece2, piece3)):
        held[ch ^ k] = piece[...]
    for f in range(4):
        data = held[f]
        hidden[:, f * 256 : f * 256 + 256] = data
        u = (data.astype(F32) - mean) * scale * gain[...] + shift[...]
        gated[:, f * 256 : f * 256 + 256] = (u / (1.0 + jnp.exp(-u))).astype(BF)


def shifted(g, kx):
    if kx == 1:
        return g
    lane = lax.broadcasted_iota(jnp.int32, g.shape, 1)
    if kx == 0:
        return jnp.where(lane == 0, 0.0, pltpu.roll(g, 1, 1))
    return jnp.where(lane == 127, 0.0, pltpu.roll(g, 127, 1))


def grad_kernel(at, clip0, clip1, clip2, clip3, cot, before, after, out, gs, cs):
    gs[864:, :] = jnp.zeros((32, 4096), BF)
    for s, clip in enumerate((clip0, clip1, clip2, clip3)):
        for kt in range(2):
            gs[kt * 288 : kt * 288 + 288, s * 1024 : s * 1024 + (2 - kt) * 256] = jnp.zeros(
                (288, (2 - kt) * 256), BF
            )
        for b in range(8):
            g = clip[:, b * 128 : b * 128 + 128].astype(F32)
            for kx in range(3):
                piece = shifted(g, kx).astype(BF)
                for kt in range(3):
                    to = b * 128 + (2 - kt) * 256
                    if to < 1024:
                        row = (kt * 3 + kx) * 96
                        gs[row : row + 96, s * 1024 + to : s * 1024 + to + 128] = piece
        k = lax.rem(s + at[0], 4)
        cs[96:192, s * 1024 : s * 1024 + 1024] = cot[k]
        for f in range(4):
            to = s * 1024 + f * 256
            cs[0:96, to : to + 128] = cot[k, :, f * 256 + 128 : f * 256 + 256]
            cs[0:96, to + 128 : to + 256] = after[k, :, f * 128 : f * 128 + 128]
            cs[192:288, to : to + 128] = before[k, :, f * 128 : f * 128 + 128]
            cs[192:288, to + 128 : to + 256] = cot[k, :, f * 256 : f * 256 + 128]
    table = lax.dot_general(
        cs[...], gs[...], (((1,), (1,)), ((), ())), preferred_element_type=F32
    ).astype(BF)
    for t in range(18):
        for l in range(7):
            out[t * 7 + l] = table[t * 16 : t * 16 + 16, l * 128 : l * 128 + 128]
    out[126:] = jnp.zeros((2, 16, 128), BF)


def join_kernel(at, table0, table1, table2, table3, out, held):
    for s, table in enumerate((table0, table1, table2, table3)):
        held[lax.rem(at[0] - s + 4, 4)] = table[...]
    for ky in range(3):
        for l in range(7):
            blocks = [
                held[j, (ky * 6 + t) * 7 + l] for j in range(4) for t in range(6)
            ]
            flipped = jnp.concatenate(blocks, axis=0).astype(F32).T
            lane = l * 128
            while lane < min(l * 128 + 128, 864):
                block = lane // 96
                end = min((block + 1) * 96, l * 128 + 128)
                row = ((block // 3 * 3 + ky) * 3 + block % 3) * 96 + lane % 96
                out[row : row + end - lane, :] = flipped[lane - l * 128 : end - l * 128, :]
                lane = end


def conv_kernel(clip, before, after, weight, out, stack):
    stack[:, :512] = jnp.zeros((864, 512), BF)
    for f in range(4):
        for p in range(4):
            if p == 0:
                g = before[:, f * 128 : f * 128 + 128]
            elif p == 3:
                g = after[:, f * 128 : f * 128 + 128]
            else:
                g = clip[:, f * 256 + p * 128 - 128 : f * 256 + p * 128]
            g = g.astype(F32)
            for kx in range(3):
                piece = shifted(g, kx).astype(BF)
                for ky in range(3):
                    r = p - ky
                    if 0 <= r < 2:
                        to = 512 + f * 256 + r * 128
                        row = (ky * 3 + kx) * 96
                        stack[row : row + 96, to : to + 128] = piece
    total = jnp.zeros((384, 1024), F32)
    for kt in range(3):
        total = total + jnp.dot(
            weight[kt], stack[:, kt * 256 : kt * 256 + 1024], preferred_element_type=F32
        )
    out[...] = total.astype(BF).reshape(4, 96, 1024)


def body(
    features,
    frame_count,
    norm1_gain,
    norm1_shift,
    qkv_weight,
    qkv_bias,
    out_weight,
    out_bias,
    norm2_gain,
    norm2_shift,
    conv_weight,
    conv_bias,
    cotangent,
):
    zh, co, zl = lax.axis_index("zh"), lax.axis_index("co"), lax.axis_index("zl")
    x, y = lax.axis_index("x"), lax.axis_index("y")
    ch = zh * 2 + co
    params = pltpu.CompilerParams(vmem_limit_bytes=VMEM)
    scalars = pl.BlockSpec(memory_space=pltpu.SMEM)
    whole = pl.BlockSpec(memory_space=pltpu.VMEM)
    frames = features.reshape(96, 4, 256)
    valid = frame_count[0]
    mask = (lax.iota(jnp.int32, 4) < valid).astype(F32)

    by_frame = jnp.repeat(frames.transpose(1, 0, 2), 2, axis=0)
    got = lax.all_to_all(by_frame, ("zh", "zl"), 0, 0, tiled=True)
    mine = got.reshape(2, 4, 96, 256).transpose(0, 2, 1, 3).reshape(192, 1024)
    parts = ring(mine, "x")
    others = [permute(p, ("co",), lambda i: (1 - i,)) for p in parts]

    packed = pl.pallas_call(
        pack_kernel,
        out_shape=jax.ShapeDtypeStruct((64, 4, 128), F32),
        in_specs=[scalars, whole, whole, whole],
        out_specs=whole,
        compiler_params=params,
        cost_estimate=cost(10**6, 200000),
        name="pack",
    )(frame_count, frames.reshape(96, 1024), norm1_gain[None], norm1_shift[None])
    packed = lax.all_to_all(packed, ("zh", "co", "zl", "x"), 0, 0, tiled=True)

    frame = 2 * zh + zl // 2
    at = jnp.stack([co, (2 * (zl % 2) + co) * 256, valid, frame]).astype(jnp.int32)
    hidden_q, packed = pl.pallas_call(
        attend_kernel,
        out_shape=(
            jax.ShapeDtypeStruct((384, 256), BF),
            jax.ShapeDtypeStruct((64, 1, 128), F32),
        ),
        in_specs=[scalars] + [whole] * 13,
        out_specs=(whole, whole),
        scratch_shapes=[pltpu.VMEM((384, 4096), BF), pltpu.VMEM((256, 4096), F32)],
        compiler_params=params,
        cost_estimate=cost(4 * 10**9, 20 * 10**6),
        name="attention",
    )(
        at,
        packed.reshape(4, 16, 4, 128),
        *parts,
        *others,
        qkv_weight,
        qkv_bias[None],
        out_weight,
        out_bias[:, None],
    )

    pieces = []
    for k in range(4):
        piece = lax.dynamic_slice(hidden_q, ((frame ^ k) * 96, 0), (96, 256))

        def to_channels(zh, co, zl, k=k):
            c = (2 * zh + zl // 2) ^ k
            return (c // 2, c % 2, 2 * (zl % 2) + co)

        pieces.append(permute(piece, ("zh", "co", "zl"), to_channels))

    packed = lax.all_to_all(packed, ("zh", "co", "zl", "x"), 0, 0, tiled=True)
    gated, hidden = pl.pallas_call(
        gate_kernel,
        out_shape=(jax.ShapeDtypeStruct((96, 1024), BF), jax.ShapeDtypeStruct((96, 1024), BF)),
        in_specs=[scalars] + [whole] * 7,
        out_specs=(whole, whole),
        scratch_shapes=[pltpu.VMEM((4, 96, 256), BF)],
        compiler_params=params,
        cost_estimate=cost(10**7, 10**6),
        name="gate",
    )(
        jnp.stack([ch, valid]).astype(jnp.int32),
        packed,
        *pieces,
        norm2_gain[:, None],
        norm2_shift[:, None],
    )

    masked = (cotangent.reshape(96, 4, 256) * mask.astype(BF)[None, :, None]).reshape(96, 1024)
    masked, _ = lax.optimization_barrier((masked, mine))
    blocks = jnp.stack(
        [
            permute(
                masked,
                ("zh", "co", "y"),
                lambda zh, co, y: (((y + k) % 4) // 2, (y + k) % 2, 2 * zh + co),
            )
            for k in range(4)
        ]
    )
    lines = blocks.reshape(4, 96, 4, 2, 128)
    before, after = halo(
        lines[:, :, :, 1].reshape(4, 96, 512), lines[:, :, :, 0].reshape(4, 96, 512)
    )

    clips = ring(gated, "y")
    table = pl.pallas_call(
        grad_kernel,
        out_shape=jax.ShapeDtypeStruct((128, 16, 128), BF),
        in_specs=[scalars] + [whole] * 7,
        out_specs=whole,
        scratch_shapes=[pltpu.VMEM((896, 4096), BF), pltpu.VMEM((288, 4096), BF)],
        compiler_params=params,
        cost_estimate=cost(4 * 10**9, 20 * 10**6),
        name="weight_grad",
    )((ch - y + 4).astype(jnp.int32)[None], *clips, blocks, before, after)
    shares = lax.all_to_all(table.reshape(16, 8, 16, 128), ("zl", "x"), 0, 0, tiled=True)
    share = jnp.sum(shares.astype(F32), axis=0).astype(BF)
    table = spread(share, ("zl", "x"), 16).reshape(128, 16, 128)
    weight_grad = pl.pallas_call(
        join_kernel,
        out_shape=jax.ShapeDtypeStruct((2592, 384), F32),
        in_specs=[scalars] + [whole] * 4,
        out_specs=whole,
        scratch_shapes=[pltpu.VMEM((4, 128, 16, 128), BF)],
        compiler_params=params,
        cost_estimate=cost(10**6, 6 * 10**6),
        name="join",
    )(y.astype(jnp.int32)[None], *ring(table, "y"))
    weight_grad = weight_grad.reshape(3, 3, 3, 96, 384)

    rows = gated.reshape(96, 4, 2, 128)
    before, after = halo(rows[:, :, 1].reshape(96, 512), rows[:, :, 0].reshape(96, 512))
    kernels = conv_weight.transpose(0, 4, 1, 2, 3).reshape(3, 384, 864)
    partial = pl.pallas_call(
        conv_kernel,
        out_shape=jax.ShapeDtypeStruct((4, 96, 1024), BF),
        scratch_shapes=[pltpu.VMEM((864, 1536), BF)],
        compiler_params=params,
        cost_estimate=cost(3 * 10**9, 12 * 10**6),
        name="convolution",
    )(gated, before, after, kernels)
    conv = lax.dynamic_index_in_dim(partial, ch, 0, keepdims=False).astype(F32)
    for k in range(1, 4):
        piece = lax.dynamic_index_in_dim(partial, ch ^ k, 0, keepdims=False)
        piece = permute(
            piece, ("zh", "co"), lambda zh, co, k=k: (zh ^ (k >> 1), co ^ (k & 1))
        )
        conv = conv + piece.astype(F32)
    mixed = hidden.astype(F32) + conv + conv_bias[:, None]
    mixed = (mixed.reshape(96, 4, 256) * mask[None, :, None]).astype(BF)
    return mixed.reshape(96, 1, 4, 2, 128), weight_grad


def solution(mesh):
    cut = Mesh(mesh.devices.reshape(2, 2, 4, 4, 4), ("zh", "co", "zl", "x", "y"))
    ch, ha = ("zh", "co"), ("zl", "x")
    maps = P(ch, "y", None, ha, None)
    placed = (
        maps,
        P("y"),
        P(ch),
        P(ch),
        P(),
        P(),
        P(),
        P(),
        P(ch),
        P(ch),
        P(None, None, None, ch, None),
        P(ch),
        maps,
    )
    return jax.shard_map(
        body,
        mesh=cut,
        in_specs=placed,
        out_specs=(maps, P(None, None, None, ch, None)),
        check_vma=False,
    )
```

```python
import itertools
import jax
import jax.numpy as jnp
from jax import lax
from jax.experimental import pallas as pl
from jax.experimental.pallas import tpu as pltpu
from jax.sharding import Mesh, PartitionSpec as P

EPS = 1e-06
SIZES = {"zh": 2, "co": 2, "zl": 4, "x": 4, "y": 4}
BF, F32 = jnp.bfloat16, jnp.float32
VMEM = 56 * 1024 * 1024


def permute(value, axes, target):
    sizes = [SIZES[a] for a in axes]

    def flat(index):
        at = 0
        for i, n in zip(index, sizes):
            at = at * n + i
        return at

    pairs = []
    for index in itertools.product(*[range(n) for n in sizes]):
        to = target(*index)
        if to is not None:
            pairs.append((flat(index), flat(to)))
    return lax.ppermute(value, axes, pairs)


def ring(value, axis):
    return [value] + [permute(value, (axis,), lambda i: ((i + s) % 4,)) for s in (1, 2, 3)]


def halo(last, first):
    def up(zl, x):
        at = zl * 4 + x + 1
        return (at // 4, at % 4) if at < 16 else None

    def down(zl, x):
        at = zl * 4 + x - 1
        return (at // 4, at % 4) if at >= 0 else None

    return permute(last, ("zl", "x"), up), permute(first, ("zl", "x"), down)


def spread(value, axes, count):
    copies = jnp.broadcast_to(value[None], (count,) + value.shape)
    return lax.all_to_all(copies, axes, 0, 0, tiled=True)


def cost(flops, size):
    return pl.CostEstimate(flops=flops, bytes_accessed=size, transcendentals=0)


def column(rows, place):
    lane = lax.broadcasted_iota(jnp.int32, (96, 128), 1)
    return jnp.sum(jnp.where(lane == place, rows, 0.0), axis=1, keepdims=True)


def pack_kernel(valid, frames, gain, shift, out):
    first = jnp.zeros((96, 128), F32)
    second = jnp.zeros((96, 128), F32)
    for f in range(4):
        data = frames[:, f * 256 : f * 256 + 256]
        out[2 * f, :96] = data
        out[2 * f + 1, :96] = data
        data = jnp.where(f < valid[0], data.astype(F32), 0.0)
        square = data * data
        first += data[:, :128] + data[:, 128:]
        second += square[:, :128] + square[:, 128:]
    row = lax.broadcasted_iota(jnp.int32, (96, 128), 0) // 12
    lane = lax.broadcasted_iota(jnp.int32, (96, 128), 1)
    first = jnp.sum(first, axis=1, keepdims=True)
    second = jnp.sum(second, axis=1, keepdims=True)
    sums = jnp.where(row + 96 == lane, first, jnp.where(row + 104 == lane, second, 0.0))
    sums = jnp.sum(sums, axis=0, keepdims=True)
    left = jnp.concatenate([gain[...], jnp.zeros((1, 32), F32)], axis=1) + sums
    right = jnp.concatenate([shift[...], jnp.zeros((1, 32), F32)], axis=1)
    rest = jnp.concatenate([left, right], axis=1)
    rows = []
    for _ in range(3):
        rounded = rest.astype(BF).astype(F32)
        rows.append(rounded)
        rest = rest - rounded
    rows = jnp.concatenate(rows + [jnp.zeros((13, 256), F32)], axis=0).astype(BF)
    for z in range(8):
        out[z, 96:] = rows


def attend_kernel(
    at,
    own0,
    own1,
    own2,
    own3,
    other0,
    other1,
    other2,
    other3,
    qkv,
    qkv_bias,
    out_weight,
    out_bias,
    hidden,
    sums,
    tokens,
    scores,
):
    co, slot, valid, frame = at[0], at[1], at[2], at[3]
    count = valid.astype(F32) * (12 * 32 * 128)
    group = lax.broadcasted_iota(jnp.int32, (96, 128), 0) // 12
    entry = lax.broadcasted_iota(jnp.int32, (96, 128), 0)
    for which, parts in ((co, (own0, own1, own2, own3)), (1 - co, (other0, other1, other2, other3))):
        for zh in range(2):
            tables = []
            for s in range(4):
                for zl in range(4):
                    rows = parts[s][zh * 4 + zl, 96:].astype(F32)
                    tables.append(rows[0:1] + rows[1:2] + rows[2:3])
            table = tables[0]
            for other in tables[1:]:
                table = table + other
            left, right = tables[0][:, :128], tables[0][:, 128:]
            mean = column(table[:, :128], group + 96) / count
            var = column(table[:, :128], group + 104) / count - mean * mean
            scale = lax.rsqrt(var + EPS)
            gain = column(left, entry)
            shift = column(right, entry)
            rows = pl.ds(pl.multiple_of((2 * zh + which) * 96, 32), 96)
            for s in range(4):
                for zl in range(4):
                    data = parts[s][zh * 4 + zl, :96].astype(F32)
                    data = (data - mean) * scale * gain + shift
                    to = s * 1024 + zl * 256
                    tokens[rows, to : to + 256] = data.astype(BF)
    lanes = pl.ds(pl.multiple_of(slot * 256, 256), 256)
    queries = lax.dot_general(
        tokens[:, lanes], qkv[:, :384], (((0,), (0,)), ((), ())), preferred_element_type=F32
    )
    queries = (queries + qkv_bias[:, :384]).astype(BF)
    lifted = lax.dot_general(
        queries, qkv[:, 384:768], (((1,), (1,)), ((), ())), preferred_element_type=F32
    ).astype(BF)
    offset = jnp.sum(queries.astype(F32) * qkv_bias[:, 384:768], axis=1, keepdims=True)
    top = jnp.full((256, 128), -jnp.inf, F32)
    for j in range(8):
        piece = jnp.dot(lifted, tokens[:, j * 512 : j * 512 + 512], preferred_element_type=F32)
        piece = (piece + offset) * (384 ** (-0.5))
        scores[:, j * 512 : j * 512 + 512] = piece
        for i in range(4):
            top = jnp.maximum(top, piece[:, i * 128 : i * 128 + 128])
    top = jnp.max(top, axis=1, keepdims=True)
    total = jnp.zeros((256, 128), F32)
    acc = jnp.zeros((256, 384), F32)
    for j in range(8):
        ew = jnp.exp(scores[:, j * 512 : j * 512 + 512] - top)
        for i in range(4):
            total += ew[:, i * 128 : i * 128 + 128]
        acc += lax.dot_general(
            ew.astype(BF),
            tokens[:, j * 512 : j * 512 + 512],
            (((1,), (1,)), ((), ())),
            preferred_element_type=F32,
        )
    total = jnp.sum(total, axis=1, keepdims=True)
    acc = (acc / total).astype(BF)
    attended = jnp.dot(acc, qkv[:, 768:], preferred_element_type=F32)
    attended = (attended + qkv_bias[:, 768:]).astype(BF)
    update = lax.dot_general(
        out_weight[...], attended, (((0,), (1,)), ((), ())), preferred_element_type=F32
    )
    hidden[...] = (update + out_bias[...]).astype(BF)
    for which, part in ((co, own0), (1 - co, other0)):
        for zh in range(2):
            rows = pl.ds(pl.multiple_of((2 * zh + which) * 96, 32), 96)
            raw = part[zh * 4 + slot, :96].astype(F32)
            hidden[rows, :] = (raw + hidden[rows, :].astype(F32)).astype(BF)
    data = jnp.where(frame < valid, hidden[...].astype(F32), 0.0)
    first = jnp.sum(data, axis=1, keepdims=True)
    second = jnp.sum(data * data, axis=1, keepdims=True)
    row = lax.broadcasted_iota(jnp.int32, (384, 128), 0) // 12
    lane = lax.broadcasted_iota(jnp.int32, (384, 128), 1)
    table = jnp.where(row == lane, first, jnp.where(row + 32 == lane, second, 0.0))
    table = jnp.sum(table, axis=0, keepdims=True)
    sums[...] = jnp.broadcast_to(table[None], sums.shape)


def gate_kernel(at, packed, piece0, piece1, piece2, piece3, gain, shift, gated, hidden, held):
    ch, valid = at[0], at[1]
    count = valid.astype(F32) * (12 * 32 * 128)
    table = jnp.sum(packed[...], axis=0)
    group = lax.broadcasted_iota(jnp.int32, (96, 128), 0) // 12 + ch * 8
    mean = column(table, group) / count
    var = column(table, group + 32) / count - mean * mean
    scale = lax.rsqrt(var + EPS)
    for k, piece in enumerate((piece0, piece1, piece2, piece3)):
        held[ch ^ k] = piece[...]
    for f in range(4):
        data = held[f]
        hidden[:, f * 256 : f * 256 + 256] = data
        u = (data.astype(F32) - mean) * scale * gain[...] + shift[...]
        gated[:, f * 256 : f * 256 + 256] = (u / (1.0 + jnp.exp(-u))).astype(BF)


def shifted(g, kx):
    if kx == 1:
        return g
    lane = lax.broadcasted_iota(jnp.int32, g.shape, 1)
    if kx == 0:
        return jnp.where(lane == 0, 0.0, pltpu.roll(g, 1, 1))
    return jnp.where(lane == 127, 0.0, pltpu.roll(g, 127, 1))


def grad_kernel(
    at,
    clip0,
    clip1,
    clip2,
    clip3,
    near,
    near_before,
    near_after,
    far,
    far_before,
    far_after,
    out,
    gs,
    cs,
    cot,
    before,
    after,
):
    for to, first, second in (
        (cot, near, far),
        (before, near_before, far_before),
        (after, near_after, far_after),
    ):
        to[0:2] = first[...]
        to[2:4] = second[...]
    gs[864:, :] = jnp.zeros((32, 4096), BF)
    for s, gated in enumerate((clip0, clip1, clip2, clip3)):
        for kt in range(2):
            gs[kt * 288 : kt * 288 + 288, s * 1024 : s * 1024 + (2 - kt) * 256] = jnp.zeros(
                (288, (2 - kt) * 256), BF
            )
        for b in range(8):
            g = gated[:, b * 128 : b * 128 + 128].astype(F32)
            for kx in range(3):
                piece = shifted(g, kx).astype(BF)
                for kt in range(3):
                    to = b * 128 + (2 - kt) * 256
                    if to < 1024:
                        row = (kt * 3 + kx) * 96
                        gs[row : row + 96, s * 1024 + to : s * 1024 + to + 128] = piece
        clip = lax.rem(at[0] - s + 4, 4)
        k = jnp.where(lax.rem(clip, 2) == at[1], 0, 2) + (clip // 2 ^ at[2])
        cs[96:192, s * 1024 : s * 1024 + 1024] = cot[k]
        for f in range(4):
            to = s * 1024 + f * 256
            cs[0:96, to : to + 128] = cot[k, :, f * 256 + 128 : f * 256 + 256]
            cs[0:96, to + 128 : to + 256] = after[k, :, f * 128 : f * 128 + 128]
            cs[192:288, to : to + 128] = before[k, :, f * 128 : f * 128 + 128]
            cs[192:288, to + 128 : to + 256] = cot[k, :, f * 256 : f * 256 + 128]
    table = lax.dot_general(
        cs[...], gs[...], (((1,), (1,)), ((), ())), preferred_element_type=F32
    ).astype(BF)
    for t in range(18):
        for l in range(7):
            out[t * 7 + l] = table[t * 16 : t * 16 + 16, l * 128 : l * 128 + 128]
    out[126:] = jnp.zeros((2, 16, 128), BF)


def join_kernel(at, table0, table1, table2, table3, out, held):
    for s, table in enumerate((table0, table1, table2, table3)):
        held[lax.rem(at[0] - s + 4, 4)] = table[...]
    for ky in range(3):
        for l in range(7):
            blocks = [
                held[j, (ky * 6 + t) * 7 + l] for j in range(4) for t in range(6)
            ]
            flipped = jnp.concatenate(blocks, axis=0).astype(F32).T
            lane = l * 128
            while lane < min(l * 128 + 128, 864):
                block = lane // 96
                end = min((block + 1) * 96, l * 128 + 128)
                row = ((block // 3 * 3 + ky) * 3 + block % 3) * 96 + lane % 96
                out[row : row + end - lane, :] = flipped[lane - l * 128 : end - l * 128, :]
                lane = end


def conv_kernel(clip, before, after, weight, out, stack):
    stack[:, :512] = jnp.zeros((864, 512), BF)
    for f in range(4):
        for p in range(4):
            if p == 0:
                g = before[:, f * 128 : f * 128 + 128]
            elif p == 3:
                g = after[:, f * 128 : f * 128 + 128]
            else:
                g = clip[:, f * 256 + p * 128 - 128 : f * 256 + p * 128]
            g = g.astype(F32)
            for kx in range(3):
                piece = shifted(g, kx).astype(BF)
                for ky in range(3):
                    r = p - ky
                    if 0 <= r < 2:
                        to = 512 + f * 256 + r * 128
                        row = (ky * 3 + kx) * 96
                        stack[row : row + 96, to : to + 128] = piece
    total = jnp.zeros((384, 1024), F32)
    for kt in range(3):
        total = total + jnp.dot(
            weight[kt], stack[:, kt * 256 : kt * 256 + 1024], preferred_element_type=F32
        )
    out[...] = total.astype(BF).reshape(4, 96, 1024)


def body(
    features,
    frame_count,
    norm1_gain,
    norm1_shift,
    qkv_weight,
    qkv_bias,
    out_weight,
    out_bias,
    norm2_gain,
    norm2_shift,
    conv_weight,
    conv_bias,
    cotangent,
):
    zh, co, zl = lax.axis_index("zh"), lax.axis_index("co"), lax.axis_index("zl")
    x, y = lax.axis_index("x"), lax.axis_index("y")
    ch = zh * 2 + co
    params = pltpu.CompilerParams(vmem_limit_bytes=VMEM)
    scalars = pl.BlockSpec(memory_space=pltpu.SMEM)
    whole = pl.BlockSpec(memory_space=pltpu.VMEM)
    valid = frame_count[0]
    mask = (lax.iota(jnp.int32, 4) < valid).astype(F32)

    by_frame = pl.pallas_call(
        pack_kernel,
        out_shape=jax.ShapeDtypeStruct((8, 112, 256), BF),
        in_specs=[scalars, whole, whole, whole],
        out_specs=whole,
        compiler_params=params,
        cost_estimate=cost(10**6, 200000),
        name="pack",
    )(frame_count, features.reshape(96, 1024), norm1_gain[None], norm1_shift[None])
    mine = lax.all_to_all(by_frame, ("zh", "zl"), 0, 0, tiled=True)
    parts = ring(mine, "x")
    others = [permute(p, ("co",), lambda i: (1 - i,)) for p in parts]

    frame = 2 * zh + zl // 2
    at = jnp.stack([co, 2 * (zl % 2) + co, valid, frame]).astype(jnp.int32)
    hidden_q, packed = pl.pallas_call(
        attend_kernel,
        out_shape=(
            jax.ShapeDtypeStruct((384, 256), BF),
            jax.ShapeDtypeStruct((64, 1, 128), F32),
        ),
        in_specs=[scalars] + [whole] * 12,
        out_specs=(whole, whole),
        scratch_shapes=[pltpu.VMEM((384, 4096), BF), pltpu.VMEM((256, 4096), F32)],
        compiler_params=params,
        cost_estimate=cost(4 * 10**9, 20 * 10**6),
        name="attention",
    )(
        at,
        *parts,
        *others,
        qkv_weight,
        qkv_bias[None],
        out_weight,
        out_bias[:, None],
    )

    pieces = []
    for k in range(4):
        piece = lax.dynamic_slice(hidden_q, ((frame ^ k) * 96, 0), (96, 256))

        def to_channels(zh, co, zl, k=k):
            c = (2 * zh + zl // 2) ^ k
            return (c // 2, c % 2, 2 * (zl % 2) + co)

        pieces.append(permute(piece, ("zh", "co", "zl"), to_channels))

    masked = (cotangent.reshape(96, 4, 256) * mask.astype(BF)[None, :, None]).reshape(96, 1024)
    masked, _ = lax.optimization_barrier((masked, parts[1]))
    blocks = jnp.stack(
        [
            permute(
                masked,
                ("zh", "co", "y"),
                lambda zh, co, y: ((y // 2 + k) % 2, y % 2, 2 * zh + co),
            )
            for k in range(2)
        ]
    )
    lines = blocks.reshape(2, 96, 4, 2, 128)
    before, after = halo(
        lines[:, :, :, 1].reshape(2, 96, 512), lines[:, :, :, 0].reshape(2, 96, 512)
    )
    near = (blocks, before, after)
    far = [permute(v, ("co",), lambda i: (1 - i,)) for v in near]

    packed = lax.all_to_all(packed, ("zh", "co", "zl", "x"), 0, 0, tiled=True)
    packed, near, far = lax.optimization_barrier((packed, near, far))
    gated, hidden = pl.pallas_call(
        gate_kernel,
        out_shape=(jax.ShapeDtypeStruct((96, 1024), BF), jax.ShapeDtypeStruct((96, 1024), BF)),
        in_specs=[scalars] + [whole] * 7,
        out_specs=(whole, whole),
        scratch_shapes=[pltpu.VMEM((4, 96, 256), BF)],
        compiler_params=params,
        cost_estimate=cost(10**7, 10**6),
        name="gate",
    )(
        jnp.stack([ch, valid]).astype(jnp.int32),
        packed,
        *pieces,
        norm2_gain[:, None],
        norm2_shift[:, None],
    )

    rows = gated.reshape(96, 4, 2, 128)
    above, below = halo(rows[:, :, 1].reshape(96, 512), rows[:, :, 0].reshape(96, 512))
    clips = ring(gated, "y")
    kernels = conv_weight.transpose(0, 4, 1, 2, 3).reshape(3, 384, 864)
    clips, above, below, kernels = lax.optimization_barrier((clips, above, below, kernels))
    table = pl.pallas_call(
        grad_kernel,
        out_shape=jax.ShapeDtypeStruct((128, 16, 128), BF),
        in_specs=[scalars] + [whole] * 10,
        out_specs=whole,
        scratch_shapes=[
            pltpu.VMEM((896, 4096), BF),
            pltpu.VMEM((288, 4096), BF),
            pltpu.VMEM((4, 96, 1024), BF),
            pltpu.VMEM((4, 96, 512), BF),
            pltpu.VMEM((4, 96, 512), BF),
        ],
        compiler_params=params,
        cost_estimate=cost(4 * 10**9, 20 * 10**6),
        name="weight_grad",
    )(jnp.stack([y, co, zh]).astype(jnp.int32), *clips, *near, *far)
    table, above, below = lax.optimization_barrier((table, above, below))
    shares = lax.all_to_all(table.reshape(16, 8, 16, 128), ("zl", "x"), 0, 0, tiled=True)
    partial = pl.pallas_call(
        conv_kernel,
        out_shape=jax.ShapeDtypeStruct((4, 96, 1024), BF),
        scratch_shapes=[pltpu.VMEM((864, 1536), BF)],
        compiler_params=params,
        cost_estimate=cost(3 * 10**9, 12 * 10**6),
        name="convolution",
    )(clips[0], above, below, kernels)
    shares, partial = lax.optimization_barrier((shares, partial))
    share = jnp.sum(shares.astype(F32), axis=0).astype(BF)
    table = spread(share, ("zl", "x"), 16).reshape(128, 16, 128)
    weight_grad = pl.pallas_call(
        join_kernel,
        out_shape=jax.ShapeDtypeStruct((2592, 384), F32),
        in_specs=[scalars] + [whole] * 4,
        out_specs=whole,
        scratch_shapes=[pltpu.VMEM((4, 128, 16, 128), BF)],
        compiler_params=params,
        cost_estimate=cost(10**6, 6 * 10**6),
        name="join",
    )(y.astype(jnp.int32)[None], *ring(table, "y"))
    weight_grad = weight_grad.reshape(3, 3, 3, 96, 384)

    conv = lax.dynamic_index_in_dim(partial, ch, 0, keepdims=False).astype(F32)
    for k in range(1, 4):
        piece = lax.dynamic_index_in_dim(partial, ch ^ k, 0, keepdims=False)
        piece = permute(
            piece, ("zh", "co"), lambda zh, co, k=k: (zh ^ (k >> 1), co ^ (k & 1))
        )
        conv = conv + piece.astype(F32)
    mixed = hidden.astype(F32) + conv + conv_bias[:, None]
    mixed = (mixed.reshape(96, 4, 256) * mask[None, :, None]).astype(BF)
    return mixed.reshape(96, 1, 4, 2, 128), weight_grad


def solution(mesh):
    cut = Mesh(mesh.devices.reshape(2, 2, 4, 4, 4), ("zh", "co", "zl", "x", "y"))
    ch, ha = ("zh", "co"), ("zl", "x")
    maps = P(ch, "y", None, ha, None)
    placed = (
        maps,
        P("y"),
        P(ch),
        P(ch),
        P(),
        P(),
        P(),
        P(),
        P(ch),
        P(ch),
        P(None, None, None, ch, None),
        P(ch),
        maps,
    )
    return jax.shard_map(
        body,
        mesh=cut,
        in_specs=placed,
        out_specs=(maps, P(None, None, None, ch, None)),
        check_vma=False,
    )
```

```python
import itertools
import jax
import jax.numpy as jnp
from jax import lax
from jax.experimental import pallas as pl
from jax.experimental.pallas import tpu as pltpu
from jax.sharding import Mesh, PartitionSpec as P

EPS = 1e-06
SIZES = {"zh": 2, "co": 2, "zl": 4, "x": 4, "y": 4}
BF, F32 = jnp.bfloat16, jnp.float32
VMEM = 56 * 1024 * 1024


def permute(value, axes, target):
    sizes = [SIZES[a] for a in axes]

    def flat(index):
        at = 0
        for i, n in zip(index, sizes):
            at = at * n + i
        return at

    pairs = []
    for index in itertools.product(*[range(n) for n in sizes]):
        to = target(*index)
        if to is not None:
            pairs.append((flat(index), flat(to)))
    return lax.ppermute(value, axes, pairs)


def ring(value, axis):
    return [value] + [permute(value, (axis,), lambda i: ((i + s) % 4,)) for s in (1, 2, 3)]


def halo(last, first):
    def up(zl, x):
        at = zl * 4 + x + 1
        return (at // 4, at % 4) if at < 16 else None

    def down(zl, x):
        at = zl * 4 + x - 1
        return (at // 4, at % 4) if at >= 0 else None

    return permute(last, ("zl", "x"), up), permute(first, ("zl", "x"), down)


def spread(value, axes, count):
    copies = jnp.broadcast_to(value[None], (count,) + value.shape)
    return lax.all_to_all(copies, axes, 0, 0, tiled=True)


def cost(flops, size):
    return pl.CostEstimate(flops=flops, bytes_accessed=size, transcendentals=0)


def column(rows, place):
    lane = lax.broadcasted_iota(jnp.int32, (96, 128), 1)
    return jnp.sum(jnp.where(lane == place, rows, 0.0), axis=1, keepdims=True)


def pack_kernel(valid, frames, gain, shift, out):
    first = jnp.zeros((96, 128), F32)
    second = jnp.zeros((96, 128), F32)
    for f in range(4):
        data = frames[:, f * 256 : f * 256 + 256]
        out[2 * f, :96] = data
        out[2 * f + 1, :96] = data
        data = jnp.where(f < valid[0], data.astype(F32), 0.0)
        square = data * data
        first += data[:, :128] + data[:, 128:]
        second += square[:, :128] + square[:, 128:]
    row = lax.broadcasted_iota(jnp.int32, (96, 128), 0) // 12
    lane = lax.broadcasted_iota(jnp.int32, (96, 128), 1)
    first = jnp.sum(first, axis=1, keepdims=True)
    second = jnp.sum(second, axis=1, keepdims=True)
    sums = jnp.where(row + 96 == lane, first, jnp.where(row + 104 == lane, second, 0.0))
    sums = jnp.sum(sums, axis=0, keepdims=True)
    left = jnp.concatenate([gain[...], jnp.zeros((1, 32), F32)], axis=1) + sums
    right = jnp.concatenate([shift[...], jnp.zeros((1, 32), F32)], axis=1)
    rest = jnp.concatenate([left, right], axis=1)
    rows = []
    for _ in range(3):
        rounded = rest.astype(BF).astype(F32)
        rows.append(rounded)
        rest = rest - rounded
    rows = jnp.concatenate(rows + [jnp.zeros((13, 256), F32)], axis=0).astype(BF)
    for z in range(8):
        out[z, 96:] = rows


def attend_kernel(
    at,
    own0,
    own1,
    own2,
    own3,
    other0,
    other1,
    other2,
    other3,
    qkv,
    qkv_bias,
    out_weight,
    out_bias,
    hidden,
    sums,
    tokens,
    scores,
):
    co, slot, valid, frame = at[0], at[1], at[2], at[3]
    count = valid.astype(F32) * (12 * 32 * 128)
    group = lax.broadcasted_iota(jnp.int32, (96, 128), 0) // 12
    entry = lax.broadcasted_iota(jnp.int32, (96, 128), 0)
    for which, parts in ((co, (own0, own1, own2, own3)), (1 - co, (other0, other1, other2, other3))):
        for zh in range(2):
            tables = []
            for s in range(4):
                for zl in range(4):
                    rows = parts[s][zh * 4 + zl, 96:].astype(F32)
                    tables.append(rows[0:1] + rows[1:2] + rows[2:3])
            table = tables[0]
            for other in tables[1:]:
                table = table + other
            left, right = tables[0][:, :128], tables[0][:, 128:]
            mean = column(table[:, :128], group + 96) / count
            var = column(table[:, :128], group + 104) / count - mean * mean
            scale = lax.rsqrt(var + EPS)
            gain = column(left, entry)
            shift = column(right, entry)
            rows = pl.ds(pl.multiple_of((2 * zh + which) * 96, 32), 96)
            for s in range(4):
                for zl in range(4):
                    data = parts[s][zh * 4 + zl, :96].astype(F32)
                    data = (data - mean) * scale * gain + shift
                    to = s * 1024 + zl * 256
                    tokens[rows, to : to + 256] = data.astype(BF)
    lanes = pl.ds(pl.multiple_of(slot * 256, 256), 256)
    queries = lax.dot_general(
        tokens[:, lanes], qkv[:, :384], (((0,), (0,)), ((), ())), preferred_element_type=F32
    )
    queries = (queries + qkv_bias[:, :384]).astype(BF)
    lifted = lax.dot_general(
        queries, qkv[:, 384:768], (((1,), (1,)), ((), ())), preferred_element_type=F32
    ).astype(BF)
    offset = jnp.sum(queries.astype(F32) * qkv_bias[:, 384:768], axis=1, keepdims=True)
    top = jnp.full((256, 128), -jnp.inf, F32)
    for j in range(8):
        piece = jnp.dot(lifted, tokens[:, j * 512 : j * 512 + 512], preferred_element_type=F32)
        piece = (piece + offset) * (384 ** (-0.5))
        scores[:, j * 512 : j * 512 + 512] = piece
        for i in range(4):
            top = jnp.maximum(top, piece[:, i * 128 : i * 128 + 128])
    top = jnp.max(top, axis=1, keepdims=True)
    total = jnp.zeros((256, 128), F32)
    acc = jnp.zeros((256, 384), F32)
    for j in range(8):
        ew = jnp.exp(scores[:, j * 512 : j * 512 + 512] - top)
        for i in range(4):
            total += ew[:, i * 128 : i * 128 + 128]
        acc += lax.dot_general(
            ew.astype(BF),
            tokens[:, j * 512 : j * 512 + 512],
            (((1,), (1,)), ((), ())),
            preferred_element_type=F32,
        )
    total = jnp.sum(total, axis=1, keepdims=True)
    acc = (acc / total).astype(BF)
    attended = jnp.dot(acc, qkv[:, 768:], preferred_element_type=F32)
    attended = (attended + qkv_bias[:, 768:]).astype(BF)
    update = lax.dot_general(
        out_weight[...], attended, (((0,), (1,)), ((), ())), preferred_element_type=F32
    )
    hidden[...] = (update + out_bias[...]).astype(BF)
    for which, part in ((co, own0), (1 - co, other0)):
        for zh in range(2):
            rows = pl.ds(pl.multiple_of((2 * zh + which) * 96, 32), 96)
            raw = part[zh * 4 + slot, :96].astype(F32)
            hidden[rows, :] = (raw + hidden[rows, :].astype(F32)).astype(BF)
    data = jnp.where(frame < valid, hidden[...].astype(F32), 0.0)
    first = jnp.sum(data, axis=1, keepdims=True)
    second = jnp.sum(data * data, axis=1, keepdims=True)
    row = lax.broadcasted_iota(jnp.int32, (384, 128), 0) // 12
    lane = lax.broadcasted_iota(jnp.int32, (384, 128), 1)
    table = jnp.where(row == lane, first, jnp.where(row + 32 == lane, second, 0.0))
    table = jnp.sum(table, axis=0, keepdims=True)
    sums[...] = jnp.broadcast_to(table[None], sums.shape)


def gate_kernel(at, packed, piece0, piece1, piece2, piece3, gain, shift, gated, hidden, held):
    ch, valid = at[0], at[1]
    count = valid.astype(F32) * (12 * 32 * 128)
    table = jnp.sum(packed[...], axis=0, keepdims=True)
    group = lax.broadcasted_iota(jnp.int32, (96, 128), 0) // 12 + ch * 8
    mean = column(table, group) / count
    var = column(table, group + 32) / count - mean * mean
    scale = lax.rsqrt(var + EPS)
    for k, piece in enumerate((piece0, piece1, piece2, piece3)):
        held[ch ^ k] = piece[...]
    for f in range(4):
        data = held[f]
        hidden[:, f * 256 : f * 256 + 256] = data
        u = (data.astype(F32) - mean) * scale * gain[...] + shift[...]
        gated[:, f * 256 : f * 256 + 256] = (u / (1.0 + jnp.exp(-u))).astype(BF)


def shifted(g, kx):
    if kx == 1:
        return g
    lane = lax.broadcasted_iota(jnp.int32, g.shape, 1)
    if kx == 0:
        return jnp.where(lane == 0, 0.0, pltpu.roll(g, 1, 1))
    return jnp.where(lane == 127, 0.0, pltpu.roll(g, 127, 1))


def grad_kernel(
    at, clip0, clip1, clip2, clip3, near0, near1, far0, far1, out, gs, cs, cot, before, after
):
    for i, part in enumerate((near0, near1, far0, far1)):
        cot[i] = part[:, :1024]
        before[i] = part[:, 1024:1536]
        after[i] = part[:, 1536:]
    gs[864:, :] = jnp.zeros((32, 4096), BF)
    for s, gated in enumerate((clip0, clip1, clip2, clip3)):
        for kt in range(2):
            gs[kt * 288 : kt * 288 + 288, s * 1024 : s * 1024 + (2 - kt) * 256] = jnp.zeros(
                (288, (2 - kt) * 256), BF
            )
        for b in range(8):
            g = gated[:, b * 128 : b * 128 + 128].astype(F32)
            for kx in range(3):
                piece = shifted(g, kx).astype(BF)
                for kt in range(3):
                    to = b * 128 + (2 - kt) * 256
                    if to < 1024:
                        row = (kt * 3 + kx) * 96
                        gs[row : row + 96, s * 1024 + to : s * 1024 + to + 128] = piece
        clip = lax.rem(at[0] - s + 4, 4)
        k = jnp.where(lax.rem(clip, 2) == at[1], 0, 2) + (clip // 2 ^ at[2])
        cs[96:192, s * 1024 : s * 1024 + 1024] = cot[k]
        for f in range(4):
            to = s * 1024 + f * 256
            cs[0:96, to : to + 128] = cot[k, :, f * 256 + 128 : f * 256 + 256]
            cs[0:96, to + 128 : to + 256] = after[k, :, f * 128 : f * 128 + 128]
            cs[192:288, to : to + 128] = before[k, :, f * 128 : f * 128 + 128]
            cs[192:288, to + 128 : to + 256] = cot[k, :, f * 256 : f * 256 + 128]
    table = lax.dot_general(
        cs[...], gs[...], (((1,), (1,)), ((), ())), preferred_element_type=F32
    ).astype(BF)
    for t in range(18):
        for l in range(7):
            out[t * 7 + l] = table[t * 16 : t * 16 + 16, l * 128 : l * 128 + 128]
    out[126:] = jnp.zeros((2, 16, 128), BF)


def join_kernel(at, table0, table1, table2, table3, out, held):
    for s, table in enumerate((table0, table1, table2, table3)):
        held[lax.rem(at[0] - s + 4, 4)] = table[...]
    for ky in range(3):
        for l in range(7):
            blocks = [
                held[j, (ky * 6 + t) * 7 + l] for j in range(4) for t in range(6)
            ]
            flipped = jnp.concatenate(blocks, axis=0).astype(F32).T
            lane = l * 128
            while lane < min(l * 128 + 128, 864):
                block = lane // 96
                end = min((block + 1) * 96, l * 128 + 128)
                row = ((block // 3 * 3 + ky) * 3 + block % 3) * 96 + lane % 96
                out[row : row + end - lane, :] = flipped[lane - l * 128 : end - l * 128, :]
                lane = end


def conv_kernel(at, clip, before, after, weight, keep, send, stack, held):
    stack[:, :512] = jnp.zeros((864, 512), BF)
    for f in range(4):
        for p in range(4):
            if p == 0:
                g = before[:, f * 128 : f * 128 + 128]
            elif p == 3:
                g = after[:, f * 128 : f * 128 + 128]
            else:
                g = clip[:, f * 256 + p * 128 - 128 : f * 256 + p * 128]
            g = g.astype(F32)
            for kx in range(3):
                piece = shifted(g, kx).astype(BF)
                for ky in range(3):
                    r = p - ky
                    if 0 <= r < 2:
                        to = 512 + f * 256 + r * 128
                        row = (ky * 3 + kx) * 96
                        stack[row : row + 96, to : to + 128] = piece
    total = jnp.zeros((384, 1024), F32)
    for kt in range(3):
        total = total + jnp.dot(
            weight[kt], stack[:, kt * 256 : kt * 256 + 1024], preferred_element_type=F32
        )
    held[...] = total.astype(BF).reshape(4, 96, 1024)
    for zh in range(2):
        keep[zh] = held[2 * zh + at[0]]
        send[zh] = held[2 * zh + 1 - at[0]]


def body(
    features,
    frame_count,
    norm1_gain,
    norm1_shift,
    qkv_weight,
    qkv_bias,
    out_weight,
    out_bias,
    norm2_gain,
    norm2_shift,
    conv_weight,
    conv_bias,
    cotangent,
):
    zh, co, zl = lax.axis_index("zh"), lax.axis_index("co"), lax.axis_index("zl")
    x, y = lax.axis_index("x"), lax.axis_index("y")
    ch = zh * 2 + co
    params = pltpu.CompilerParams(vmem_limit_bytes=VMEM)
    scalars = pl.BlockSpec(memory_space=pltpu.SMEM)
    whole = pl.BlockSpec(memory_space=pltpu.VMEM)
    valid = frame_count[0]
    mask = (lax.iota(jnp.int32, 4) < valid).astype(F32)

    by_frame = pl.pallas_call(
        pack_kernel,
        out_shape=jax.ShapeDtypeStruct((8, 112, 256), BF),
        in_specs=[scalars, whole, whole, whole],
        out_specs=whole,
        compiler_params=params,
        cost_estimate=cost(10**6, 200000),
        name="pack",
    )(frame_count, features.reshape(96, 1024), norm1_gain[None], norm1_shift[None])
    mine = lax.all_to_all(by_frame, ("zh", "zl"), 0, 0, tiled=True)
    parts = ring(mine, "x")
    others = [permute(p, ("co",), lambda i: (1 - i,)) for p in parts]

    masked = (cotangent.reshape(96, 4, 256) * mask.astype(BF)[None, :, None]).reshape(96, 1024)
    lines = masked.reshape(96, 4, 2, 128)
    before, after = halo(lines[:, :, 1].reshape(96, 512), lines[:, :, 0].reshape(96, 512))
    bundle = jnp.concatenate([masked, before, after], axis=1)
    bundle, _ = lax.optimization_barrier((bundle, parts[1]))
    near = [
        permute(
            bundle, ("zh", "co", "y"), lambda zh, co, y: ((y // 2 + k) % 2, y % 2, 2 * zh + co)
        )
        for k in range(2)
    ]

    frame = 2 * zh + zl // 2
    at = jnp.stack([co, 2 * (zl % 2) + co, valid, frame]).astype(jnp.int32)
    hidden_q, packed = pl.pallas_call(
        attend_kernel,
        out_shape=(
            jax.ShapeDtypeStruct((384, 256), BF),
            jax.ShapeDtypeStruct((16, 1, 128), F32),
        ),
        in_specs=[scalars] + [whole] * 12,
        out_specs=(whole, whole),
        scratch_shapes=[pltpu.VMEM((384, 4096), BF), pltpu.VMEM((256, 4096), F32)],
        compiler_params=params,
        cost_estimate=cost(4 * 10**9, 20 * 10**6),
        name="attention",
    )(
        at,
        *parts,
        *others,
        qkv_weight,
        qkv_bias[None],
        out_weight,
        out_bias[:, None],
    )

    pieces = []
    for k in range(4):
        piece = lax.dynamic_slice(hidden_q, ((frame ^ k) * 96, 0), (96, 256))

        def to_channels(zh, co, zl, k=k):
            c = (2 * zh + zl // 2) ^ k
            return (c // 2, c % 2, 2 * (zl % 2) + co)

        pieces.append(permute(piece, ("zh", "co", "zl"), to_channels))

    packed = lax.all_to_all(packed, ("zh", "co", "zl"), 0, 0, tiled=True)
    packed = jnp.sum(packed, axis=0)
    packed, near, pieces = lax.optimization_barrier((packed, near, pieces))
    packed = jnp.concatenate(ring(packed, "x"), axis=0)
    far = [permute(v, ("co",), lambda i: (1 - i,)) for v in near]
    gated, hidden = pl.pallas_call(
        gate_kernel,
        out_shape=(jax.ShapeDtypeStruct((96, 1024), BF), jax.ShapeDtypeStruct((96, 1024), BF)),
        in_specs=[scalars] + [whole] * 7,
        out_specs=(whole, whole),
        scratch_shapes=[pltpu.VMEM((4, 96, 256), BF)],
        compiler_params=params,
        cost_estimate=cost(10**7, 10**6),
        name="gate",
    )(
        jnp.stack([ch, valid]).astype(jnp.int32),
        packed,
        *pieces,
        norm2_gain[:, None],
        norm2_shift[:, None],
    )

    rows = gated.reshape(96, 4, 2, 128)
    above, below = halo(rows[:, :, 1].reshape(96, 512), rows[:, :, 0].reshape(96, 512))
    clips = ring(gated, "y")
    clips, above, below = lax.optimization_barrier((clips, above, below))
    table = pl.pallas_call(
        grad_kernel,
        out_shape=jax.ShapeDtypeStruct((128, 16, 128), BF),
        in_specs=[scalars] + [whole] * 8,
        out_specs=whole,
        scratch_shapes=[
            pltpu.VMEM((896, 4096), BF),
            pltpu.VMEM((288, 4096), BF),
            pltpu.VMEM((4, 96, 1024), BF),
            pltpu.VMEM((4, 96, 512), BF),
            pltpu.VMEM((4, 96, 512), BF),
        ],
        compiler_params=params,
        cost_estimate=cost(4 * 10**9, 20 * 10**6),
        name="weight_grad",
    )(jnp.stack([y, co, zh]).astype(jnp.int32), *clips, *near, *far)
    table, conv_weight = lax.optimization_barrier((table, conv_weight))
    kernels = conv_weight.transpose(0, 4, 1, 2, 3).reshape(3, 384, 864)
    shares = lax.all_to_all(table.reshape(16, 8, 16, 128), ("zl", "x"), 0, 0, tiled=True)
    keep, send = pl.pallas_call(
        conv_kernel,
        out_shape=(jax.ShapeDtypeStruct((2, 96, 1024), BF),) * 2,
        in_specs=[scalars] + [whole] * 4,
        out_specs=(whole, whole),
        scratch_shapes=[pltpu.VMEM((864, 1536), BF), pltpu.VMEM((4, 96, 1024), BF)],
        compiler_params=params,
        cost_estimate=cost(3 * 10**9, 12 * 10**6),
        name="convolution",
    )(co.astype(jnp.int32)[None], clips[0], above, below, kernels)
    send = permute(send, ("co",), lambda i: (1 - i,))
    summed = keep.astype(F32) + send.astype(F32)
    near = lax.dynamic_index_in_dim(summed, zh, 0, keepdims=False)
    far = lax.dynamic_index_in_dim(summed, 1 - zh, 0, keepdims=False).astype(BF)
    shares, near, far = lax.optimization_barrier((shares, near, far))
    share = jnp.sum(shares.astype(F32), axis=0).astype(BF)
    table = spread(share, ("zl", "x"), 16).reshape(128, 16, 128)
    table, near, far = lax.optimization_barrier((table, near, far))
    weight_grad = pl.pallas_call(
        join_kernel,
        out_shape=jax.ShapeDtypeStruct((2592, 384), F32),
        in_specs=[scalars] + [whole] * 4,
        out_specs=whole,
        scratch_shapes=[pltpu.VMEM((4, 128, 16, 128), BF)],
        compiler_params=params,
        cost_estimate=cost(10**6, 6 * 10**6),
        name="join",
    )(y.astype(jnp.int32)[None], *ring(table, "y"))
    weight_grad = weight_grad.reshape(3, 3, 3, 96, 384)

    conv = near + permute(far, ("zh",), lambda i: (1 - i,)).astype(F32)
    mixed = hidden.astype(F32) + conv + conv_bias[:, None]
    mixed = (mixed.reshape(96, 4, 256) * mask[None, :, None]).astype(BF)
    return mixed.reshape(96, 1, 4, 2, 128), weight_grad


def solution(mesh):
    cut = Mesh(mesh.devices.reshape(2, 2, 4, 4, 4), ("zh", "co", "zl", "x", "y"))
    ch, ha = ("zh", "co"), ("zl", "x")
    maps = P(ch, "y", None, ha, None)
    placed = (
        maps,
        P("y"),
        P(ch),
        P(ch),
        P(),
        P(),
        P(),
        P(),
        P(ch),
        P(ch),
        P(None, None, None, ch, None),
        P(ch),
        maps,
    )
    return jax.shard_map(
        body,
        mesh=cut,
        in_specs=placed,
        out_specs=(maps, P(None, None, None, ch, None)),
        check_vma=False,
    )
```

```python
import itertools
import jax
import jax.numpy as jnp
from jax import lax
from jax.experimental import pallas as pl
from jax.experimental.pallas import tpu as pltpu
from jax.sharding import Mesh, PartitionSpec as P

EPS = 1e-06
SIZES = {"zh": 2, "co": 2, "zl": 4, "x": 4, "y": 4}
BF, F32 = jnp.bfloat16, jnp.float32
VMEM = 56 * 1024 * 1024


def permute(value, axes, target):
    sizes = [SIZES[a] for a in axes]

    def flat(index):
        at = 0
        for i, n in zip(index, sizes):
            at = at * n + i
        return at

    pairs = []
    for index in itertools.product(*[range(n) for n in sizes]):
        to = target(*index)
        if to is not None:
            pairs.append((flat(index), flat(to)))
    return lax.ppermute(value, axes, pairs)


def ring(value, axis):
    return [value] + [permute(value, (axis,), lambda i: ((i + s) % 4,)) for s in (1, 2, 3)]


def halo(last, first):
    def up(zl, x):
        at = zl * 4 + x + 1
        return (at // 4, at % 4) if at < 16 else None

    def down(zl, x):
        at = zl * 4 + x - 1
        return (at // 4, at % 4) if at >= 0 else None

    return permute(last, ("zl", "x"), up), permute(first, ("zl", "x"), down)


def spread(value, axes, count):
    copies = jnp.broadcast_to(value[None], (count,) + value.shape)
    return lax.all_to_all(copies, axes, 0, 0, tiled=True)


def cost(flops, size):
    return pl.CostEstimate(flops=flops, bytes_accessed=size, transcendentals=0)


def column(rows, place):
    lane = lax.broadcasted_iota(jnp.int32, (96, 128), 1)
    return jnp.sum(jnp.where(lane == place, rows, 0.0), axis=1, keepdims=True)


def pack_kernel(valid, frames, gain, shift, out):
    first = jnp.zeros((96, 128), F32)
    second = jnp.zeros((96, 128), F32)
    for f in range(4):
        data = frames[:, f * 256 : f * 256 + 256]
        out[2 * f, :96] = data
        out[2 * f + 1, :96] = data
        data = jnp.where(f < valid[0], data.astype(F32), 0.0)
        square = data * data
        first += data[:, :128] + data[:, 128:]
        second += square[:, :128] + square[:, 128:]
    row = lax.broadcasted_iota(jnp.int32, (96, 128), 0) // 12
    lane = lax.broadcasted_iota(jnp.int32, (96, 128), 1)
    first = jnp.sum(first, axis=1, keepdims=True)
    second = jnp.sum(second, axis=1, keepdims=True)
    sums = jnp.where(row + 96 == lane, first, jnp.where(row + 104 == lane, second, 0.0))
    sums = jnp.sum(sums, axis=0, keepdims=True)
    left = jnp.concatenate([gain[...], jnp.zeros((1, 32), F32)], axis=1) + sums
    right = jnp.concatenate([shift[...], jnp.zeros((1, 32), F32)], axis=1)
    rest = jnp.concatenate([left, right], axis=1)
    rows = []
    for _ in range(3):
        rounded = rest.astype(BF).astype(F32)
        rows.append(rounded)
        rest = rest - rounded
    rows = jnp.concatenate(rows + [jnp.zeros((13, 256), F32)], axis=0).astype(BF)
    for z in range(8):
        out[z, 96:] = rows


def attend_kernel(
    at,
    own0,
    own1,
    own2,
    own3,
    other0,
    other1,
    other2,
    other3,
    qkv,
    qkv_bias,
    out_weight,
    out_bias,
    piece0,
    piece1,
    piece2,
    piece3,
    sums,
    tokens,
    scores,
    hidden,
):
    co, slot, valid, frame = at[0], at[1], at[2], at[3]
    count = valid.astype(F32) * (12 * 32 * 128)
    group = lax.broadcasted_iota(jnp.int32, (96, 128), 0) // 12
    entry = lax.broadcasted_iota(jnp.int32, (96, 128), 0)
    for which, parts in ((co, (own0, own1, own2, own3)), (1 - co, (other0, other1, other2, other3))):
        for zh in range(2):
            tables = []
            for s in range(4):
                for zl in range(4):
                    rows = parts[s][zh * 4 + zl, 96:].astype(F32)
                    tables.append(rows[0:1] + rows[1:2] + rows[2:3])
            table = tables[0]
            for other in tables[1:]:
                table = table + other
            left, right = tables[0][:, :128], tables[0][:, 128:]
            mean = column(table[:, :128], group + 96) / count
            var = column(table[:, :128], group + 104) / count - mean * mean
            scale = lax.rsqrt(var + EPS)
            gain = column(left, entry)
            shift = column(right, entry)
            rows = pl.ds(pl.multiple_of((2 * zh + which) * 96, 32), 96)
            for s in range(4):
                for zl in range(4):
                    data = parts[s][zh * 4 + zl, :96].astype(F32)
                    data = (data - mean) * scale * gain + shift
                    to = s * 1024 + zl * 256
                    tokens[rows, to : to + 256] = data.astype(BF)
    lanes = pl.ds(pl.multiple_of(slot * 256, 256), 256)
    queries = lax.dot_general(
        tokens[:, lanes], qkv[:, :384], (((0,), (0,)), ((), ())), preferred_element_type=F32
    )
    queries = (queries + qkv_bias[:, :384]).astype(BF)
    lifted = lax.dot_general(
        queries, qkv[:, 384:768], (((1,), (1,)), ((), ())), preferred_element_type=F32
    ).astype(BF)
    offset = jnp.sum(queries.astype(F32) * qkv_bias[:, 384:768], axis=1, keepdims=True)
    top = jnp.full((256, 128), -jnp.inf, F32)
    for j in range(8):
        piece = jnp.dot(lifted, tokens[:, j * 512 : j * 512 + 512], preferred_element_type=F32)
        piece = (piece + offset) * (384 ** (-0.5))
        scores[:, j * 512 : j * 512 + 512] = piece
        for i in range(4):
            top = jnp.maximum(top, piece[:, i * 128 : i * 128 + 128])
    top = jnp.max(top, axis=1, keepdims=True)
    total = jnp.zeros((256, 128), F32)
    acc = jnp.zeros((256, 384), F32)
    for j in range(8):
        ew = jnp.exp(scores[:, j * 512 : j * 512 + 512] - top)
        for i in range(4):
            total += ew[:, i * 128 : i * 128 + 128]
        acc += lax.dot_general(
            ew.astype(BF),
            tokens[:, j * 512 : j * 512 + 512],
            (((1,), (1,)), ((), ())),
            preferred_element_type=F32,
        )
    total = jnp.sum(total, axis=1, keepdims=True)
    acc = (acc / total).astype(BF)
    attended = jnp.dot(acc, qkv[:, 768:], preferred_element_type=F32)
    attended = (attended + qkv_bias[:, 768:]).astype(BF)
    update = lax.dot_general(
        out_weight[...], attended, (((0,), (1,)), ((), ())), preferred_element_type=F32
    )
    hidden[...] = (update + out_bias[...]).astype(BF)
    for which, part in ((co, own0), (1 - co, other0)):
        for zh in range(2):
            rows = pl.ds(pl.multiple_of((2 * zh + which) * 96, 32), 96)
            raw = part[zh * 4 + slot, :96].astype(F32)
            hidden[rows, :] = (raw + hidden[rows, :].astype(F32)).astype(BF)
    for k, piece in enumerate((piece0, piece1, piece2, piece3)):
        piece[...] = hidden[pl.ds(pl.multiple_of((frame ^ k) * 96, 32), 96), :]
    data = jnp.where(frame < valid, hidden[...].astype(F32), 0.0)
    first = jnp.sum(data, axis=1, keepdims=True)
    second = jnp.sum(data * data, axis=1, keepdims=True)
    row = lax.broadcasted_iota(jnp.int32, (384, 128), 0) // 12
    lane = lax.broadcasted_iota(jnp.int32, (384, 128), 1)
    table = jnp.where(row == lane, first, jnp.where(row + 32 == lane, second, 0.0))
    table = jnp.sum(table, axis=0, keepdims=True)
    table = table + jnp.where(lane[0:1] == 64, valid.astype(F32) / 64.0, 0.0)
    sums[...] = jnp.broadcast_to(table[None], sums.shape)


def arrange_kernel(at, piece0, piece1, piece2, piece3, whole, last, leading, held):
    for k, piece in enumerate((piece0, piece1, piece2, piece3)):
        held[at[0] ^ k] = piece[...]
    for f in range(4):
        data = held[f]
        whole[:, f * 256 : f * 256 + 256] = data
        leading[:, f * 128 : f * 128 + 128] = data[:, :128]
        last[:, f * 128 : f * 128 + 128] = data[:, 128:]


def clip_columns(table, ch):
    group = lax.broadcasted_iota(jnp.int32, (96, 128), 0) // 12 + ch * 8
    count = column(table, 64) * (12 * 32 * 128)
    mean = column(table, group) / count
    var = column(table, group + 32) / count - mean * mean
    return mean, lax.rsqrt(var + EPS)


def gate(data, columns, gain, shift):
    mean, scale = columns
    u = (data.astype(F32) - mean) * scale * gain[...] + shift[...]
    return u / (1.0 + jnp.exp(-u))


def shifted(g, kx):
    if kx == 1:
        return g
    lane = lax.broadcasted_iota(jnp.int32, g.shape, 1)
    if kx == 0:
        return jnp.where(lane == 0, 0.0, pltpu.roll(g, 1, 1))
    return jnp.where(lane == 127, 0.0, pltpu.roll(g, 127, 1))


def grad_kernel(
    at,
    table,
    clip0,
    clip1,
    clip2,
    clip3,
    near0,
    near1,
    far0,
    far1,
    gain,
    shift,
    out,
    gs,
    cs,
    cot,
    before,
    after,
):
    for i, part in enumerate((near0, near1, far0, far1)):
        cot[i] = part[:, :1024]
        before[i] = part[:, 1024:1536]
        after[i] = part[:, 1536:]
    gs[864:, :] = jnp.zeros((32, 4096), BF)
    for s, hidden in enumerate((clip0, clip1, clip2, clip3)):
        columns = clip_columns(table[s : s + 1], at[3])
        for kt in range(2):
            gs[kt * 288 : kt * 288 + 288, s * 1024 : s * 1024 + (2 - kt) * 256] = jnp.zeros(
                (288, (2 - kt) * 256), BF
            )
        for b in range(8):
            g = gate(hidden[:, b * 128 : b * 128 + 128], columns, gain, shift)
            for kx in range(3):
                piece = shifted(g, kx).astype(BF)
                for kt in range(3):
                    to = b * 128 + (2 - kt) * 256
                    if to < 1024:
                        row = (kt * 3 + kx) * 96
                        gs[row : row + 96, s * 1024 + to : s * 1024 + to + 128] = piece
        clip = lax.rem(at[0] - s + 4, 4)
        k = jnp.where(lax.rem(clip, 2) == at[1], 0, 2) + (clip // 2 ^ at[2])
        cs[96:192, s * 1024 : s * 1024 + 1024] = cot[k]
        for f in range(4):
            to = s * 1024 + f * 256
            cs[0:96, to : to + 128] = cot[k, :, f * 256 + 128 : f * 256 + 256]
            cs[0:96, to + 128 : to + 256] = after[k, :, f * 128 : f * 128 + 128]
            cs[192:288, to : to + 128] = before[k, :, f * 128 : f * 128 + 128]
            cs[192:288, to + 128 : to + 256] = cot[k, :, f * 256 : f * 256 + 128]
    grads = lax.dot_general(
        cs[...], gs[...], (((1,), (1,)), ((), ())), preferred_element_type=F32
    ).astype(BF)
    for t in range(18):
        for l in range(7):
            out[t * 7 + l] = grads[t * 16 : t * 16 + 16, l * 128 : l * 128 + 128]
    out[126:] = jnp.zeros((2, 16, 128), BF)


def join_kernel(at, table0, table1, table2, table3, out, held):
    for s, table in enumerate((table0, table1, table2, table3)):
        held[lax.rem(at[0] - s + 4, 4)] = table[...]
    for ky in range(3):
        for l in range(7):
            blocks = [
                held[j, (ky * 6 + t) * 7 + l] for j in range(4) for t in range(6)
            ]
            flipped = jnp.concatenate(blocks, axis=0).astype(F32).T
            lane = l * 128
            while lane < min(l * 128 + 128, 864):
                block = lane // 96
                end = min((block + 1) * 96, l * 128 + 128)
                row = ((block // 3 * 3 + ky) * 3 + block % 3) * 96 + lane % 96
                out[row : row + end - lane, :] = flipped[lane - l * 128 : end - l * 128, :]
                lane = end


def conv_kernel(at, table, clip, before, after, weight, gain, shift, keep, send, stack, held):
    stack[:, :512] = jnp.zeros((864, 512), BF)
    columns = clip_columns(table[0:1], at[1])
    for f in range(4):
        for p in range(4):
            if p == 0:
                g = before[:, f * 128 : f * 128 + 128]
            elif p == 3:
                g = after[:, f * 128 : f * 128 + 128]
            else:
                g = clip[:, f * 256 + p * 128 - 128 : f * 256 + p * 128]
            g = gate(g, columns, gain, shift)
            if p == 0:
                g = jnp.where(at[2] > 0, g, 0.0)
            elif p == 3:
                g = jnp.where(at[2] < 15, g, 0.0)
            for kx in range(3):
                piece = shifted(g, kx).astype(BF)
                for ky in range(3):
                    r = p - ky
                    if 0 <= r < 2:
                        to = 512 + f * 256 + r * 128
                        row = (ky * 3 + kx) * 96
                        stack[row : row + 96, to : to + 128] = piece
    total = jnp.zeros((384, 1024), F32)
    for kt in range(3):
        total = total + jnp.dot(
            weight[kt], stack[:, kt * 256 : kt * 256 + 1024], preferred_element_type=F32
        )
    held[...] = total.astype(BF).reshape(4, 96, 1024)
    for zh in range(2):
        keep[zh] = held[2 * zh + at[0]]
        send[zh] = held[2 * zh + 1 - at[0]]


def body(
    features,
    frame_count,
    norm1_gain,
    norm1_shift,
    qkv_weight,
    qkv_bias,
    out_weight,
    out_bias,
    norm2_gain,
    norm2_shift,
    conv_weight,
    conv_bias,
    cotangent,
):
    zh, co, zl = lax.axis_index("zh"), lax.axis_index("co"), lax.axis_index("zl")
    x, y = lax.axis_index("x"), lax.axis_index("y")
    ch = zh * 2 + co
    params = pltpu.CompilerParams(vmem_limit_bytes=VMEM)
    scalars = pl.BlockSpec(memory_space=pltpu.SMEM)
    whole = pl.BlockSpec(memory_space=pltpu.VMEM)
    valid = frame_count[0]
    mask = (lax.iota(jnp.int32, 4) < valid).astype(F32)

    by_frame = pl.pallas_call(
        pack_kernel,
        out_shape=jax.ShapeDtypeStruct((8, 112, 256), BF),
        in_specs=[scalars, whole, whole, whole],
        out_specs=whole,
        compiler_params=params,
        cost_estimate=cost(10**6, 200000),
        name="pack",
    )(frame_count, features.reshape(96, 1024), norm1_gain[None], norm1_shift[None])
    mine = lax.all_to_all(by_frame, ("zh", "zl"), 0, 0, tiled=True)
    masked = (cotangent.reshape(96, 4, 256) * mask.astype(BF)[None, :, None]).reshape(96, 1024)
    lines = masked.reshape(96, 4, 2, 128)
    before, after = halo(lines[:, :, 1].reshape(96, 512), lines[:, :, 0].reshape(96, 512))
    bundle = jnp.concatenate([masked, before, after], axis=1)
    mine, bundle = lax.optimization_barrier((mine, bundle))
    parts = ring(mine, "x")
    others = [permute(p, ("co",), lambda i: (1 - i,)) for p in parts]

    bundle, _ = lax.optimization_barrier((bundle, parts[1]))
    near = [
        permute(
            bundle, ("zh", "co", "y"), lambda zh, co, y: ((y // 2 + k) % 2, y % 2, 2 * zh + co)
        )
        for k in range(2)
    ]

    frame = 2 * zh + zl // 2
    at = jnp.stack([co, 2 * (zl % 2) + co, valid, frame]).astype(jnp.int32)
    *pieces, packed = pl.pallas_call(
        attend_kernel,
        out_shape=(jax.ShapeDtypeStruct((96, 256), BF),) * 4
        + (jax.ShapeDtypeStruct((64, 1, 128), F32),),
        in_specs=[scalars] + [whole] * 12,
        out_specs=(whole,) * 5,
        scratch_shapes=[
            pltpu.VMEM((384, 4096), BF),
            pltpu.VMEM((256, 4096), F32),
            pltpu.VMEM((384, 256), BF),
        ],
        compiler_params=params,
        cost_estimate=cost(4 * 10**9, 20 * 10**6),
        name="attention",
    )(
        at,
        *parts,
        *others,
        qkv_weight,
        qkv_bias[None],
        out_weight,
        out_bias[:, None],
    )

    near, pieces = lax.optimization_barrier((near, pieces))
    far = [permute(v, ("co",), lambda i: (1 - i,)) for v in near]

    for k in range(4):

        def to_channels(zh, co, zl, k=k):
            c = (2 * zh + zl // 2) ^ k
            return (c // 2, c % 2, 2 * (zl % 2) + co)

        pieces[k] = permute(pieces[k], ("zh", "co", "zl"), to_channels)
    packed = lax.all_to_all(packed, ("zh", "co", "zl", "x"), 0, 0, tiled=True)
    packed = jnp.sum(packed, axis=0)
    packed, far, pieces = lax.optimization_barrier((packed, far, pieces))
    hidden, last, leading = pl.pallas_call(
        arrange_kernel,
        out_shape=(
            jax.ShapeDtypeStruct((96, 1024), BF),
            jax.ShapeDtypeStruct((96, 512), BF),
            jax.ShapeDtypeStruct((96, 512), BF),
        ),
        in_specs=[scalars] + [whole] * 4,
        out_specs=(whole,) * 3,
        scratch_shapes=[pltpu.VMEM((4, 96, 256), BF)],
        compiler_params=params,
        cost_estimate=cost(10**6, 10**6),
        name="arrange",
    )(ch.astype(jnp.int32)[None], *pieces)
    packed, hidden = lax.optimization_barrier((packed, hidden))
    clips = ring(hidden, "y")

    table2 = jnp.concatenate(ring(packed, "y"), axis=0)
    gain, shift = norm2_gain[:, None], norm2_shift[:, None]

    table = pl.pallas_call(
        grad_kernel,
        out_shape=jax.ShapeDtypeStruct((128, 16, 128), BF),
        in_specs=[scalars] + [whole] * 11,
        out_specs=whole,
        scratch_shapes=[
            pltpu.VMEM((896, 4096), BF),
            pltpu.VMEM((288, 4096), BF),
            pltpu.VMEM((4, 96, 1024), BF),
            pltpu.VMEM((4, 96, 512), BF),
            pltpu.VMEM((4, 96, 512), BF),
        ],
        compiler_params=params,
        cost_estimate=cost(4 * 10**9, 20 * 10**6),
        name="weight_grad",
    )(jnp.stack([y, co, zh, ch]).astype(jnp.int32), table2, *clips, *near, *far, gain, shift)
    table, conv_weight, last, leading = lax.optimization_barrier((table, conv_weight, last, leading))
    above, below = halo(last, leading)
    kernels = conv_weight.transpose(0, 4, 1, 2, 3).reshape(3, 384, 864)
    shares = lax.all_to_all(table.reshape(16, 8, 16, 128), ("zl", "x"), 0, 0, tiled=True)
    keep, send = pl.pallas_call(
        conv_kernel,
        out_shape=(jax.ShapeDtypeStruct((2, 96, 1024), BF),) * 2,
        in_specs=[scalars] + [whole] * 7,
        out_specs=(whole, whole),
        scratch_shapes=[pltpu.VMEM((864, 1536), BF), pltpu.VMEM((4, 96, 1024), BF)],
        compiler_params=params,
        cost_estimate=cost(3 * 10**9, 12 * 10**6),
        name="convolution",
    )(
        jnp.stack([co, ch, zl * 4 + x]).astype(jnp.int32),
        table2,
        clips[0],
        above,
        below,
        kernels,
        gain,
        shift,
    )
    send = permute(send, ("co",), lambda i: (1 - i,))
    summed = keep.astype(F32) + send.astype(F32)
    near = lax.dynamic_index_in_dim(summed, zh, 0, keepdims=False)
    far = lax.dynamic_index_in_dim(summed, 1 - zh, 0, keepdims=False).astype(BF)
    shares, near, far = lax.optimization_barrier((shares, near, far))
    share = jnp.sum(shares.astype(F32), axis=0).astype(BF)
    table = spread(share, ("zl", "x"), 16).reshape(128, 16, 128)
    table, near, far = lax.optimization_barrier((table, near, far))
    weight_grad = pl.pallas_call(
        join_kernel,
        out_shape=jax.ShapeDtypeStruct((2592, 384), F32),
        in_specs=[scalars] + [whole] * 4,
        out_specs=whole,
        scratch_shapes=[pltpu.VMEM((4, 128, 16, 128), BF)],
        compiler_params=params,
        cost_estimate=cost(10**6, 6 * 10**6),
        name="join",
    )(y.astype(jnp.int32)[None], *ring(table, "y"))
    weight_grad = weight_grad.reshape(3, 3, 3, 96, 384)

    conv = near + permute(far, ("zh",), lambda i: (1 - i,)).astype(F32)
    mixed = hidden.astype(F32) + conv + conv_bias[:, None]
    mixed = (mixed.reshape(96, 4, 256) * mask[None, :, None]).astype(BF)
    return mixed.reshape(96, 1, 4, 2, 128), weight_grad


def solution(mesh):
    cut = Mesh(mesh.devices.reshape(2, 2, 4, 4, 4), ("zh", "co", "zl", "x", "y"))
    ch, ha = ("zh", "co"), ("zl", "x")
    maps = P(ch, "y", None, ha, None)
    placed = (
        maps,
        P("y"),
        P(ch),
        P(ch),
        P(),
        P(),
        P(),
        P(),
        P(ch),
        P(ch),
        P(None, None, None, ch, None),
        P(ch),
        maps,
    )
    return jax.shard_map(
        body,
        mesh=cut,
        in_specs=placed,
        out_specs=(maps, P(None, None, None, ch, None)),
        check_vma=False,
    )
```

```python
import itertools
import jax
import jax.numpy as jnp
from jax import lax
from jax.experimental import pallas as pl
from jax.experimental.pallas import tpu as pltpu
from jax.sharding import Mesh, PartitionSpec as P

EPS = 1e-06
SIZES = {"zh": 2, "co": 2, "zl": 4, "x": 4, "y": 4}
BF, F32 = jnp.bfloat16, jnp.float32
VMEM = 56 * 1024 * 1024


def permute(value, axes, target):
    sizes = [SIZES[a] for a in axes]

    def flat(index):
        at = 0
        for i, n in zip(index, sizes):
            at = at * n + i
        return at

    pairs = []
    for index in itertools.product(*[range(n) for n in sizes]):
        to = target(*index)
        if to is not None:
            pairs.append((flat(index), flat(to)))
    return lax.ppermute(value, axes, pairs)


def ring(value, axis):
    return [value] + [permute(value, (axis,), lambda i: ((i + s) % 4,)) for s in (1, 2, 3)]


def halo(last, first):
    def up(zl, x):
        at = zl * 4 + x + 1
        return (at // 4, at % 4) if at < 16 else None

    def down(zl, x):
        at = zl * 4 + x - 1
        return (at // 4, at % 4) if at >= 0 else None

    return permute(last, ("zl", "x"), up), permute(first, ("zl", "x"), down)


def spread(value, axes, count):
    copies = jnp.broadcast_to(value[None], (count,) + value.shape)
    return lax.all_to_all(copies, axes, 0, 0, tiled=True)


def cost(flops, size):
    return pl.CostEstimate(flops=flops, bytes_accessed=size, transcendentals=0)


def column(rows, place):
    lane = lax.broadcasted_iota(jnp.int32, (96, 128), 1)
    return jnp.sum(jnp.where(lane == place, rows, 0.0), axis=1, keepdims=True)


def pack_kernel(valid, frames, gain, shift, out):
    first = jnp.zeros((96, 128), F32)
    second = jnp.zeros((96, 128), F32)
    for f in range(4):
        data = frames[:, f * 256 : f * 256 + 256]
        out[2 * f, :96] = data
        out[2 * f + 1, :96] = data
        data = jnp.where(f < valid[0], data.astype(F32), 0.0)
        square = data * data
        first += data[:, :128] + data[:, 128:]
        second += square[:, :128] + square[:, 128:]
    row = lax.broadcasted_iota(jnp.int32, (96, 128), 0) // 12
    lane = lax.broadcasted_iota(jnp.int32, (96, 128), 1)
    first = jnp.sum(first, axis=1, keepdims=True)
    second = jnp.sum(second, axis=1, keepdims=True)
    sums = jnp.where(row + 96 == lane, first, jnp.where(row + 104 == lane, second, 0.0))
    sums = jnp.sum(sums, axis=0, keepdims=True)
    left = jnp.concatenate([gain[...], jnp.zeros((1, 32), F32)], axis=1) + sums
    right = jnp.concatenate([shift[...], jnp.zeros((1, 32), F32)], axis=1)
    rest = jnp.concatenate([left, right], axis=1)
    rows = []
    for _ in range(3):
        rounded = rest.astype(BF).astype(F32)
        rows.append(rounded)
        rest = rest - rounded
    rows = jnp.concatenate(rows + [jnp.zeros((13, 256), F32)], axis=0).astype(BF)
    for z in range(8):
        out[z, 96:] = rows


def attend_kernel(
    at,
    own0,
    own1,
    own2,
    own3,
    other0,
    other1,
    other2,
    other3,
    qkv,
    qkv_bias,
    out_weight,
    out_bias,
    piece0,
    piece1,
    piece2,
    piece3,
    tokens,
    scores,
    hidden,
):
    co, slot, valid, frame = at[0], at[1], at[2], at[3]
    count = valid.astype(F32) * (12 * 32 * 128)
    group = lax.broadcasted_iota(jnp.int32, (96, 128), 0) // 12
    entry = lax.broadcasted_iota(jnp.int32, (96, 128), 0)
    for which, parts in ((co, (own0, own1, own2, own3)), (1 - co, (other0, other1, other2, other3))):
        for zh in range(2):
            tables = []
            for s in range(4):
                for zl in range(4):
                    rows = parts[s][zh * 4 + zl, 96:].astype(F32)
                    tables.append(rows[0:1] + rows[1:2] + rows[2:3])
            table = tables[0]
            for other in tables[1:]:
                table = table + other
            left, right = tables[0][:, :128], tables[0][:, 128:]
            mean = column(table[:, :128], group + 96) / count
            var = column(table[:, :128], group + 104) / count - mean * mean
            scale = lax.rsqrt(var + EPS)
            gain = column(left, entry)
            shift = column(right, entry)
            rows = pl.ds(pl.multiple_of((2 * zh + which) * 96, 32), 96)
            for s in range(4):
                for zl in range(4):
                    data = parts[s][zh * 4 + zl, :96].astype(F32)
                    data = (data - mean) * scale * gain + shift
                    to = s * 1024 + zl * 256
                    tokens[rows, to : to + 256] = data.astype(BF)
    lanes = pl.ds(pl.multiple_of(slot * 256, 256), 256)
    queries = lax.dot_general(
        tokens[:, lanes], qkv[:, :384], (((0,), (0,)), ((), ())), preferred_element_type=F32
    )
    queries = (queries + qkv_bias[:, :384]).astype(BF)
    lifted = lax.dot_general(
        queries, qkv[:, 384:768], (((1,), (1,)), ((), ())), preferred_element_type=F32
    ).astype(BF)
    offset = jnp.sum(queries.astype(F32) * qkv_bias[:, 384:768], axis=1, keepdims=True)
    top = jnp.full((256, 128), -jnp.inf, F32)
    for j in range(8):
        piece = jnp.dot(lifted, tokens[:, j * 512 : j * 512 + 512], preferred_element_type=F32)
        piece = (piece + offset) * (384 ** (-0.5))
        scores[:, j * 512 : j * 512 + 512] = piece
        for i in range(4):
            top = jnp.maximum(top, piece[:, i * 128 : i * 128 + 128])
    top = jnp.max(top, axis=1, keepdims=True)
    total = jnp.zeros((256, 128), F32)
    acc = jnp.zeros((256, 384), F32)
    for j in range(8):
        ew = jnp.exp(scores[:, j * 512 : j * 512 + 512] - top)
        for i in range(4):
            total += ew[:, i * 128 : i * 128 + 128]
        acc += lax.dot_general(
            ew.astype(BF),
            tokens[:, j * 512 : j * 512 + 512],
            (((1,), (1,)), ((), ())),
            preferred_element_type=F32,
        )
    total = jnp.sum(total, axis=1, keepdims=True)
    acc = (acc / total).astype(BF)
    attended = jnp.dot(acc, qkv[:, 768:], preferred_element_type=F32)
    attended = (attended + qkv_bias[:, 768:]).astype(BF)
    update = lax.dot_general(
        out_weight[...], attended, (((0,), (1,)), ((), ())), preferred_element_type=F32
    )
    hidden[...] = (update + out_bias[...]).astype(BF)
    for which, part in ((co, own0), (1 - co, other0)):
        for zh in range(2):
            rows = pl.ds(pl.multiple_of((2 * zh + which) * 96, 32), 96)
            raw = part[zh * 4 + slot, :96].astype(F32)
            hidden[rows, :] = (raw + hidden[rows, :].astype(F32)).astype(BF)
    for k, piece in enumerate((piece0, piece1, piece2, piece3)):
        piece[...] = hidden[pl.ds(pl.multiple_of((frame ^ k) * 96, 32), 96), :]


def arrange_kernel(at, piece0, piece1, piece2, piece3, whole, last, leading, sums, held):
    for k, piece in enumerate((piece0, piece1, piece2, piece3)):
        held[at[0] ^ k] = piece[...]
    valid = at[1]
    first = jnp.zeros((96, 128), F32)
    second = jnp.zeros((96, 128), F32)
    for f in range(4):
        data = held[f]
        whole[:, f * 256 : f * 256 + 256] = data
        leading[:, f * 128 : f * 128 + 128] = data[:, :128]
        last[:, f * 128 : f * 128 + 128] = data[:, 128:]
        data = jnp.where(f < valid, data.astype(F32), 0.0)
        square = data * data
        first += data[:, :128] + data[:, 128:]
        second += square[:, :128] + square[:, 128:]
    first = jnp.sum(first, axis=1, keepdims=True)
    second = jnp.sum(second, axis=1, keepdims=True)
    row = lax.broadcasted_iota(jnp.int32, (96, 128), 0) // 12
    lane = lax.broadcasted_iota(jnp.int32, (96, 128), 1)
    table = jnp.where(row == lane, first, jnp.where(row + 8 == lane, second, 0.0))
    table = jnp.sum(table, axis=0, keepdims=True)
    sums[...] = table + jnp.where(lane[0:1] == 64, valid.astype(F32) / 16.0, 0.0)


def clip_columns(table):
    group = lax.broadcasted_iota(jnp.int32, (96, 128), 0) // 12
    count = column(table, 64) * (12 * 32 * 128)
    mean = column(table, group) / count
    var = column(table, group + 8) / count - mean * mean
    return mean, lax.rsqrt(var + EPS)


def gate(data, columns, gain, shift):
    mean, scale = columns
    u = (data.astype(F32) - mean) * scale * gain[...] + shift[...]
    return u / (1.0 + jnp.exp(-u))


def shifted(g, kx):
    if kx == 1:
        return g
    lane = lax.broadcasted_iota(jnp.int32, g.shape, 1)
    if kx == 0:
        return jnp.where(lane == 0, 0.0, pltpu.roll(g, 1, 1))
    return jnp.where(lane == 127, 0.0, pltpu.roll(g, 127, 1))


def grad_kernel(
    at,
    table,
    clip0,
    clip1,
    clip2,
    clip3,
    near0,
    near1,
    far0,
    far1,
    gain,
    shift,
    out,
    gs,
    cs,
    cot,
    before,
    after,
):
    for i, part in enumerate((near0, near1, far0, far1)):
        cot[i] = part[:, :1024]
        before[i] = part[:, 1024:1536]
        after[i] = part[:, 1536:]
    gs[864:, :] = jnp.zeros((32, 4096), BF)
    for s, hidden in enumerate((clip0, clip1, clip2, clip3)):
        columns = clip_columns(table[s : s + 1])
        for kt in range(2):
            gs[kt * 288 : kt * 288 + 288, s * 1024 : s * 1024 + (2 - kt) * 256] = jnp.zeros(
                (288, (2 - kt) * 256), BF
            )
        for b in range(8):
            g = gate(hidden[:, b * 128 : b * 128 + 128], columns, gain, shift)
            for kx in range(3):
                piece = shifted(g, kx).astype(BF)
                for kt in range(3):
                    to = b * 128 + (2 - kt) * 256
                    if to < 1024:
                        row = (kt * 3 + kx) * 96
                        gs[row : row + 96, s * 1024 + to : s * 1024 + to + 128] = piece
        clip = lax.rem(at[0] - s + 4, 4)
        k = jnp.where(lax.rem(clip, 2) == at[1], 0, 2) + (clip // 2 ^ at[2])
        cs[96:192, s * 1024 : s * 1024 + 1024] = cot[k]
        for f in range(4):
            to = s * 1024 + f * 256
            cs[0:96, to : to + 128] = cot[k, :, f * 256 + 128 : f * 256 + 256]
            cs[0:96, to + 128 : to + 256] = after[k, :, f * 128 : f * 128 + 128]
            cs[192:288, to : to + 128] = before[k, :, f * 128 : f * 128 + 128]
            cs[192:288, to + 128 : to + 256] = cot[k, :, f * 256 : f * 256 + 128]
    grads = lax.dot_general(
        cs[...], gs[...], (((1,), (1,)), ((), ())), preferred_element_type=F32
    ).astype(BF)
    for t in range(18):
        for l in range(7):
            out[t * 7 + l] = grads[t * 16 : t * 16 + 16, l * 128 : l * 128 + 128]
    out[126:] = jnp.zeros((2, 16, 128), BF)


def join_kernel(at, table0, table1, table2, table3, out, held):
    for s, table in enumerate((table0, table1, table2, table3)):
        held[lax.rem(at[0] - s + 4, 4)] = table[...]
    for ky in range(3):
        for l in range(7):
            blocks = [
                held[j, (ky * 6 + t) * 7 + l] for j in range(4) for t in range(6)
            ]
            flipped = jnp.concatenate(blocks, axis=0).astype(F32).T
            lane = l * 128
            while lane < min(l * 128 + 128, 864):
                block = lane // 96
                end = min((block + 1) * 96, l * 128 + 128)
                row = ((block // 3 * 3 + ky) * 3 + block % 3) * 96 + lane % 96
                out[row : row + end - lane, :] = flipped[lane - l * 128 : end - l * 128, :]
                lane = end


def conv_kernel(at, table, clip, before, after, weight, gain, shift, keep, send, stack, held):
    stack[:, :512] = jnp.zeros((864, 512), BF)
    columns = clip_columns(table[0:1])
    for f in range(4):
        for p in range(4):
            if p == 0:
                g = before[:, f * 128 : f * 128 + 128]
            elif p == 3:
                g = after[:, f * 128 : f * 128 + 128]
            else:
                g = clip[:, f * 256 + p * 128 - 128 : f * 256 + p * 128]
            g = gate(g, columns, gain, shift)
            if p == 0:
                g = jnp.where(at[1] > 0, g, 0.0)
            elif p == 3:
                g = jnp.where(at[1] < 15, g, 0.0)
            for kx in range(3):
                piece = shifted(g, kx).astype(BF)
                for ky in range(3):
                    r = p - ky
                    if 0 <= r < 2:
                        to = 512 + f * 256 + r * 128
                        row = (ky * 3 + kx) * 96
                        stack[row : row + 96, to : to + 128] = piece
    total = jnp.zeros((384, 1024), F32)
    for kt in range(3):
        total = total + jnp.dot(
            weight[kt], stack[:, kt * 256 : kt * 256 + 1024], preferred_element_type=F32
        )
    held[...] = total.astype(BF).reshape(4, 96, 1024)
    for zh in range(2):
        keep[zh] = held[2 * zh + at[0]]
        send[zh] = held[2 * zh + 1 - at[0]]


def body(
    features,
    frame_count,
    norm1_gain,
    norm1_shift,
    qkv_weight,
    qkv_bias,
    out_weight,
    out_bias,
    norm2_gain,
    norm2_shift,
    conv_weight,
    conv_bias,
    cotangent,
):
    zh, co, zl = lax.axis_index("zh"), lax.axis_index("co"), lax.axis_index("zl")
    x, y = lax.axis_index("x"), lax.axis_index("y")
    ch = zh * 2 + co
    params = pltpu.CompilerParams(vmem_limit_bytes=VMEM)
    scalars = pl.BlockSpec(memory_space=pltpu.SMEM)
    whole = pl.BlockSpec(memory_space=pltpu.VMEM)
    valid = frame_count[0]
    mask = (lax.iota(jnp.int32, 4) < valid).astype(F32)

    by_frame = pl.pallas_call(
        pack_kernel,
        out_shape=jax.ShapeDtypeStruct((8, 112, 256), BF),
        in_specs=[scalars, whole, whole, whole],
        out_specs=whole,
        compiler_params=params,
        cost_estimate=cost(10**6, 200000),
        name="pack",
    )(frame_count, features.reshape(96, 1024), norm1_gain[None], norm1_shift[None])
    mine = lax.all_to_all(by_frame, ("zh", "zl"), 0, 0, tiled=True)
    masked = (cotangent.reshape(96, 4, 256) * mask.astype(BF)[None, :, None]).reshape(96, 1024)
    lines = masked.reshape(96, 4, 2, 128)
    before, after = halo(lines[:, :, 1].reshape(96, 512), lines[:, :, 0].reshape(96, 512))
    bundle = jnp.concatenate([masked, before, after], axis=1)
    mine, bundle = lax.optimization_barrier((mine, bundle))
    parts = ring(mine, "x")
    others = [permute(p, ("co",), lambda i: (1 - i,)) for p in parts]

    bundle, _ = lax.optimization_barrier((bundle, parts[1]))
    near = [
        permute(
            bundle, ("zh", "co", "y"), lambda zh, co, y: ((y // 2 + k) % 2, y % 2, 2 * zh + co)
        )
        for k in range(2)
    ]

    frame = 2 * zh + zl // 2
    at = jnp.stack([co, 2 * (zl % 2) + co, valid, frame]).astype(jnp.int32)
    pieces = pl.pallas_call(
        attend_kernel,
        out_shape=[jax.ShapeDtypeStruct((96, 256), BF)] * 4,
        in_specs=[scalars] + [whole] * 12,
        out_specs=[whole] * 4,
        scratch_shapes=[
            pltpu.VMEM((384, 4096), BF),
            pltpu.VMEM((256, 4096), F32),
            pltpu.VMEM((384, 256), BF),
        ],
        compiler_params=params,
        cost_estimate=cost(4 * 10**9, 20 * 10**6),
        name="attention",
    )(
        at,
        *parts,
        *others,
        qkv_weight,
        qkv_bias[None],
        out_weight,
        out_bias[:, None],
    )

    near, pieces = lax.optimization_barrier((near, list(pieces)))
    far = [permute(v, ("co",), lambda i: (1 - i,)) for v in near]

    for k in range(4):

        def to_channels(zh, co, zl, k=k):
            c = (2 * zh + zl // 2) ^ k
            return (c // 2, c % 2, 2 * (zl % 2) + co)

        pieces[k] = permute(pieces[k], ("zh", "co", "zl"), to_channels)
    far, pieces = lax.optimization_barrier((far, pieces))
    hidden, last, leading, packed = pl.pallas_call(
        arrange_kernel,
        out_shape=(
            jax.ShapeDtypeStruct((96, 1024), BF),
            jax.ShapeDtypeStruct((96, 512), BF),
            jax.ShapeDtypeStruct((96, 512), BF),
            jax.ShapeDtypeStruct((1, 128), F32),
        ),
        in_specs=[scalars] + [whole] * 4,
        out_specs=(whole,) * 4,
        scratch_shapes=[pltpu.VMEM((4, 96, 256), BF)],
        compiler_params=params,
        cost_estimate=cost(10**6, 10**6),
        name="arrange",
    )(jnp.stack([ch, valid]).astype(jnp.int32), *pieces)
    clips = ring(hidden, "y")
    clips[1], last, leading = lax.optimization_barrier((clips[1], last, leading))
    above, below = halo(last, leading)

    packed = sum(ring(packed, "zl"))
    packed = sum(ring(packed, "x"))
    table2 = jnp.concatenate(ring(packed, "y"), axis=0)
    gain, shift = norm2_gain[:, None], norm2_shift[:, None]

    clips, above, below = lax.optimization_barrier((clips, above, below))
    table = pl.pallas_call(
        grad_kernel,
        out_shape=jax.ShapeDtypeStruct((128, 16, 128), BF),
        in_specs=[scalars] + [whole] * 11,
        out_specs=whole,
        scratch_shapes=[
            pltpu.VMEM((896, 4096), BF),
            pltpu.VMEM((288, 4096), BF),
            pltpu.VMEM((4, 96, 1024), BF),
            pltpu.VMEM((4, 96, 512), BF),
            pltpu.VMEM((4, 96, 512), BF),
        ],
        compiler_params=params,
        cost_estimate=cost(4 * 10**9, 20 * 10**6),
        name="weight_grad",
    )(jnp.stack([y, co, zh]).astype(jnp.int32), table2, *clips, *near, *far, gain, shift)
    table, conv_weight = lax.optimization_barrier((table, conv_weight))
    kernels = conv_weight.transpose(0, 4, 1, 2, 3).reshape(3, 384, 864)
    shares = lax.all_to_all(table.reshape(16, 8, 16, 128), ("zl", "x"), 0, 0, tiled=True)
    keep, send = pl.pallas_call(
        conv_kernel,
        out_shape=(jax.ShapeDtypeStruct((2, 96, 1024), BF),) * 2,
        in_specs=[scalars] + [whole] * 7,
        out_specs=(whole, whole),
        scratch_shapes=[pltpu.VMEM((864, 1536), BF), pltpu.VMEM((4, 96, 1024), BF)],
        compiler_params=params,
        cost_estimate=cost(3 * 10**9, 12 * 10**6),
        name="convolution",
    )(
        jnp.stack([co, zl * 4 + x]).astype(jnp.int32),
        table2,
        clips[0],
        above,
        below,
        kernels,
        gain,
        shift,
    )
    send = permute(send, ("co",), lambda i: (1 - i,))
    summed = keep.astype(F32) + send.astype(F32)
    near = lax.dynamic_index_in_dim(summed, zh, 0, keepdims=False)
    far = lax.dynamic_index_in_dim(summed, 1 - zh, 0, keepdims=False).astype(BF)
    shares, near, far = lax.optimization_barrier((shares, near, far))
    share = jnp.sum(shares.astype(F32), axis=0).astype(BF)
    table = spread(share, ("zl", "x"), 16).reshape(128, 16, 128)
    table, near, far = lax.optimization_barrier((table, near, far))
    weight_grad = pl.pallas_call(
        join_kernel,
        out_shape=jax.ShapeDtypeStruct((2592, 384), F32),
        in_specs=[scalars] + [whole] * 4,
        out_specs=whole,
        scratch_shapes=[pltpu.VMEM((4, 128, 16, 128), BF)],
        compiler_params=params,
        cost_estimate=cost(10**6, 6 * 10**6),
        name="join",
    )(y.astype(jnp.int32)[None], *ring(table, "y"))
    weight_grad = weight_grad.reshape(3, 3, 3, 96, 384)

    conv = near + permute(far, ("zh",), lambda i: (1 - i,)).astype(F32)
    mixed = hidden.astype(F32) + conv + conv_bias[:, None]
    mixed = (mixed.reshape(96, 4, 256) * mask[None, :, None]).astype(BF)
    return mixed.reshape(96, 1, 4, 2, 128), weight_grad


def solution(mesh):
    cut = Mesh(mesh.devices.reshape(2, 2, 4, 4, 4), ("zh", "co", "zl", "x", "y"))
    ch, ha = ("zh", "co"), ("zl", "x")
    maps = P(ch, "y", None, ha, None)
    placed = (
        maps,
        P("y"),
        P(ch),
        P(ch),
        P(),
        P(),
        P(),
        P(),
        P(ch),
        P(ch),
        P(None, None, None, ch, None),
        P(ch),
        maps,
    )
    return jax.shard_map(
        body,
        mesh=cut,
        in_specs=placed,
        out_specs=(maps, P(None, None, None, ch, None)),
        check_vma=False,
    )
```

```python
import itertools
import jax
import jax.numpy as jnp
from jax import lax
from jax.experimental import pallas as pl
from jax.experimental.pallas import tpu as pltpu
from jax.sharding import Mesh, PartitionSpec as P

EPS = 1e-06
SIZES = {"zh": 2, "co": 2, "zl": 4, "x": 4, "y": 4}
BF, F32 = jnp.bfloat16, jnp.float32
VMEM = 56 * 1024 * 1024


def permute(value, axes, target):
    sizes = [SIZES[a] for a in axes]

    def flat(index):
        at = 0
        for i, n in zip(index, sizes):
            at = at * n + i
        return at

    pairs = []
    for index in itertools.product(*[range(n) for n in sizes]):
        to = target(*index)
        if to is not None:
            pairs.append((flat(index), flat(to)))
    return lax.ppermute(value, axes, pairs)


def ring(value, axis):
    return [value] + [permute(value, (axis,), lambda i: ((i + s) % 4,)) for s in (1, 2, 3)]


def halo(last, first):
    def up(zl, x):
        at = zl * 4 + x + 1
        return (at // 4, at % 4) if at < 16 else None

    def down(zl, x):
        at = zl * 4 + x - 1
        return (at // 4, at % 4) if at >= 0 else None

    return permute(last, ("zl", "x"), up), permute(first, ("zl", "x"), down)


def spread(value, axes, count):
    copies = jnp.broadcast_to(value[None], (count,) + value.shape)
    return lax.all_to_all(copies, axes, 0, 0, tiled=True)


def cost(flops, size):
    return pl.CostEstimate(flops=flops, bytes_accessed=size, transcendentals=0)


def column(rows, place):
    lane = lax.broadcasted_iota(jnp.int32, (96, 128), 1)
    return jnp.sum(jnp.where(lane == place, rows, 0.0), axis=1, keepdims=True)


def pack_kernel(valid, frames, gain, shift, out):
    first = jnp.zeros((96, 128), F32)
    second = jnp.zeros((96, 128), F32)
    for f in range(4):
        data = frames[:, f * 256 : f * 256 + 256]
        out[2 * f, :96] = data
        out[2 * f + 1, :96] = data
        data = jnp.where(f < valid[0], data.astype(F32), 0.0)
        square = data * data
        first += data[:, :128] + data[:, 128:]
        second += square[:, :128] + square[:, 128:]
    row = lax.broadcasted_iota(jnp.int32, (96, 128), 0) // 12
    lane = lax.broadcasted_iota(jnp.int32, (96, 128), 1)
    first = jnp.sum(first, axis=1, keepdims=True)
    second = jnp.sum(second, axis=1, keepdims=True)
    sums = jnp.where(row + 96 == lane, first, jnp.where(row + 104 == lane, second, 0.0))
    sums = jnp.sum(sums, axis=0, keepdims=True)
    left = jnp.concatenate([gain[...], jnp.zeros((1, 32), F32)], axis=1) + sums
    right = jnp.concatenate([shift[...], jnp.zeros((1, 32), F32)], axis=1)
    rest = jnp.concatenate([left, right], axis=1)
    rows = []
    for _ in range(3):
        rounded = rest.astype(BF).astype(F32)
        rows.append(rounded)
        rest = rest - rounded
    rows = jnp.concatenate(rows + [jnp.zeros((13, 256), F32)], axis=0).astype(BF)
    for z in range(8):
        out[z, 96:] = rows


def attend_kernel(
    at,
    own0,
    own1,
    own2,
    own3,
    other0,
    other1,
    other2,
    other3,
    qkv,
    qkv_bias,
    out_weight,
    out_bias,
    piece0,
    piece1,
    piece2,
    piece3,
    tokens,
    scores,
    hidden,
):
    co, slot, valid, frame = at[0], at[1], at[2], at[3]
    count = valid.astype(F32) * (12 * 32 * 128)
    group = lax.broadcasted_iota(jnp.int32, (96, 128), 0) // 12
    entry = lax.broadcasted_iota(jnp.int32, (96, 128), 0)
    for which, parts in ((co, (own0, own1, own2, own3)), (1 - co, (other0, other1, other2, other3))):
        for zh in range(2):
            tables = []
            for s in range(4):
                for zl in range(4):
                    rows = parts[s][zh * 4 + zl, 96:].astype(F32)
                    tables.append(rows[0:1] + rows[1:2] + rows[2:3])
            table = tables[0]
            for other in tables[1:]:
                table = table + other
            left, right = tables[0][:, :128], tables[0][:, 128:]
            mean = column(table[:, :128], group + 96) / count
            var = column(table[:, :128], group + 104) / count - mean * mean
            scale = lax.rsqrt(var + EPS)
            gain = column(left, entry)
            shift = column(right, entry)
            rows = pl.ds(pl.multiple_of((2 * zh + which) * 96, 32), 96)
            for s in range(4):
                for zl in range(4):
                    data = parts[s][zh * 4 + zl, :96].astype(F32)
                    data = (data - mean) * scale * gain + shift
                    to = s * 1024 + zl * 256
                    tokens[rows, to : to + 256] = data.astype(BF)
    lanes = pl.ds(pl.multiple_of(slot * 256, 256), 256)
    queries = lax.dot_general(
        tokens[:, lanes], qkv[:, :384], (((0,), (0,)), ((), ())), preferred_element_type=F32
    )
    queries = (queries + qkv_bias[:, :384]).astype(BF)
    lifted = lax.dot_general(
        queries, qkv[:, 384:768], (((1,), (1,)), ((), ())), preferred_element_type=F32
    ).astype(BF)
    offset = jnp.sum(queries.astype(F32) * qkv_bias[:, 384:768], axis=1, keepdims=True)
    top = jnp.full((256, 128), -jnp.inf, F32)
    for j in range(8):
        piece = jnp.dot(lifted, tokens[:, j * 512 : j * 512 + 512], preferred_element_type=F32)
        piece = (piece + offset) * (384 ** (-0.5))
        scores[:, j * 512 : j * 512 + 512] = piece
        for i in range(4):
            top = jnp.maximum(top, piece[:, i * 128 : i * 128 + 128])
    top = jnp.max(top, axis=1, keepdims=True)
    total = jnp.zeros((256, 128), F32)
    acc = jnp.zeros((256, 384), F32)
    for j in range(8):
        ew = jnp.exp(scores[:, j * 512 : j * 512 + 512] - top)
        for i in range(4):
            total += ew[:, i * 128 : i * 128 + 128]
        acc += lax.dot_general(
            ew.astype(BF),
            tokens[:, j * 512 : j * 512 + 512],
            (((1,), (1,)), ((), ())),
            preferred_element_type=F32,
        )
    total = jnp.sum(total, axis=1, keepdims=True)
    acc = (acc / total).astype(BF)
    attended = jnp.dot(acc, qkv[:, 768:], preferred_element_type=F32)
    attended = (attended + qkv_bias[:, 768:]).astype(BF)
    update = lax.dot_general(
        out_weight[...], attended, (((0,), (1,)), ((), ())), preferred_element_type=F32
    )
    hidden[...] = (update + out_bias[...]).astype(BF)
    for which, part in ((co, own0), (1 - co, other0)):
        for zh in range(2):
            rows = pl.ds(pl.multiple_of((2 * zh + which) * 96, 32), 96)
            raw = part[zh * 4 + slot, :96].astype(F32)
            hidden[rows, :] = (raw + hidden[rows, :].astype(F32)).astype(BF)
    for k, piece in enumerate((piece0, piece1, piece2, piece3)):
        piece[...] = hidden[pl.ds(pl.multiple_of((frame ^ k) * 96, 32), 96), :]


def arrange_kernel(at, piece0, piece1, piece2, piece3, whole, last, leading, sums, held):
    for k, piece in enumerate((piece0, piece1, piece2, piece3)):
        held[at[0] ^ k] = piece[...]
    valid = at[1]
    first = jnp.zeros((96, 128), F32)
    second = jnp.zeros((96, 128), F32)
    for f in range(4):
        data = held[f]
        whole[:, f * 256 : f * 256 + 256] = data
        leading[:, f * 128 : f * 128 + 128] = data[:, :128]
        last[:, f * 128 : f * 128 + 128] = data[:, 128:]
        data = jnp.where(f < valid, data.astype(F32), 0.0)
        square = data * data
        first += data[:, :128] + data[:, 128:]
        second += square[:, :128] + square[:, 128:]
    first = jnp.sum(first, axis=1, keepdims=True)
    second = jnp.sum(second, axis=1, keepdims=True)
    row = lax.broadcasted_iota(jnp.int32, (96, 128), 0) // 12
    lane = lax.broadcasted_iota(jnp.int32, (96, 128), 1)
    table = jnp.where(row == lane, first, jnp.where(row + 8 == lane, second, 0.0))
    table = jnp.sum(table, axis=0, keepdims=True)
    table = table + jnp.where(lane[0:1] == 64, valid.astype(F32) / 16.0, 0.0)
    sums[...] = jnp.broadcast_to(table[None], sums.shape)


def clip_columns(table):
    group = lax.broadcasted_iota(jnp.int32, (96, 128), 0) // 12
    count = column(table, 64) * (12 * 32 * 128)
    mean = column(table, group) / count
    var = column(table, group + 8) / count - mean * mean
    return mean, lax.rsqrt(var + EPS)


def gate(data, columns, gain, shift):
    mean, scale = columns
    u = (data.astype(F32) - mean) * scale * gain[...] + shift[...]
    return u / (1.0 + jnp.exp(-u))


def shifted(g, kx):
    if kx == 1:
        return g
    lane = lax.broadcasted_iota(jnp.int32, g.shape, 1)
    if kx == 0:
        return jnp.where(lane == 0, 0.0, pltpu.roll(g, 1, 1))
    return jnp.where(lane == 127, 0.0, pltpu.roll(g, 127, 1))


def grad_kernel(at, table, clip0, clip1, clip2, clip3, cot, gain, shift, out, gs, cs):
    gs[864:, :] = jnp.zeros((32, 4096), BF)
    for s, hidden in enumerate((clip0, clip1, clip2, clip3)):
        clip = lax.rem(at[0] - s + 4, 4)
        columns = clip_columns(jnp.sum(table[:, clip], axis=0))
        for kt in range(2):
            gs[kt * 288 : kt * 288 + 288, s * 1024 : s * 1024 + (2 - kt) * 256] = jnp.zeros(
                (288, (2 - kt) * 256), BF
            )
        for b in range(8):
            g = gate(hidden[:, b * 128 : b * 128 + 128], columns, gain, shift)
            for kx in range(3):
                piece = shifted(g, kx).astype(BF)
                for kt in range(3):
                    to = b * 128 + (2 - kt) * 256
                    if to < 1024:
                        row = (kt * 3 + kx) * 96
                        gs[row : row + 96, s * 1024 + to : s * 1024 + to + 128] = piece
        cs[96:192, s * 1024 : s * 1024 + 1024] = cot[clip, :, :1024]
        for f in range(4):
            to = s * 1024 + f * 256
            above = cot[clip, :, 1024 + f * 128 : 1152 + f * 128]
            below = cot[clip, :, 1536 + f * 128 : 1664 + f * 128]
            cs[0:96, to : to + 128] = cot[clip, :, f * 256 + 128 : f * 256 + 256]
            cs[0:96, to + 128 : to + 256] = below
            cs[192:288, to : to + 128] = above
            cs[192:288, to + 128 : to + 256] = cot[clip, :, f * 256 : f * 256 + 128]
    grads = lax.dot_general(
        cs[...], gs[...], (((1,), (1,)), ((), ())), preferred_element_type=F32
    ).astype(BF)
    for t in range(18):
        for l in range(7):
            out[t * 7 + l] = grads[t * 16 : t * 16 + 16, l * 128 : l * 128 + 128]
    out[126:] = jnp.zeros((2, 16, 128), BF)


def join_kernel(tables, out):
    for ky in range(3):
        for l in range(7):
            tiles = [(ky * 6 + t) * 7 + l for t in range(6)]
            blocks = [tables[t // 8, j, t % 8] for j in range(4) for t in tiles]
            flipped = jnp.concatenate(blocks, axis=0).astype(F32).T
            lane = l * 128
            while lane < min(l * 128 + 128, 864):
                block = lane // 96
                end = min((block + 1) * 96, l * 128 + 128)
                row = ((block // 3 * 3 + ky) * 3 + block % 3) * 96 + lane % 96
                out[row : row + end - lane, :] = flipped[lane - l * 128 : end - l * 128, :]
                lane = end


def conv_kernel(at, table, clip, before, after, weight, gain, shift, keep, send, stack, held):
    stack[:, :512] = jnp.zeros((864, 512), BF)
    columns = clip_columns(jnp.sum(table[:, at[2]], axis=0))
    for f in range(4):
        for p in range(4):
            if p == 0:
                g = before[:, f * 128 : f * 128 + 128]
            elif p == 3:
                g = after[:, f * 128 : f * 128 + 128]
            else:
                g = clip[:, f * 256 + p * 128 - 128 : f * 256 + p * 128]
            g = gate(g, columns, gain, shift)
            if p == 0:
                g = jnp.where(at[1] > 0, g, 0.0)
            elif p == 3:
                g = jnp.where(at[1] < 15, g, 0.0)
            for kx in range(3):
                piece = shifted(g, kx).astype(BF)
                for ky in range(3):
                    r = p - ky
                    if 0 <= r < 2:
                        to = 512 + f * 256 + r * 128
                        row = (ky * 3 + kx) * 96
                        stack[row : row + 96, to : to + 128] = piece
    total = jnp.zeros((384, 1024), F32)
    for kt in range(3):
        total = total + jnp.dot(
            weight[kt], stack[:, kt * 256 : kt * 256 + 1024], preferred_element_type=F32
        )
    held[...] = total.astype(BF).reshape(4, 96, 1024)
    for zh in range(2):
        keep[zh] = held[2 * zh + at[0]]
        send[zh] = held[2 * zh + 1 - at[0]]


def body(
    features,
    frame_count,
    norm1_gain,
    norm1_shift,
    qkv_weight,
    qkv_bias,
    out_weight,
    out_bias,
    norm2_gain,
    norm2_shift,
    conv_weight,
    conv_bias,
    cotangent,
):
    zh, co, zl = lax.axis_index("zh"), lax.axis_index("co"), lax.axis_index("zl")
    x, y = lax.axis_index("x"), lax.axis_index("y")
    ch = zh * 2 + co
    params = pltpu.CompilerParams(vmem_limit_bytes=VMEM)
    scalars = pl.BlockSpec(memory_space=pltpu.SMEM)
    whole = pl.BlockSpec(memory_space=pltpu.VMEM)
    valid = frame_count[0]
    mask = (lax.iota(jnp.int32, 4) < valid).astype(F32)

    by_frame = pl.pallas_call(
        pack_kernel,
        out_shape=jax.ShapeDtypeStruct((8, 112, 256), BF),
        in_specs=[scalars, whole, whole, whole],
        out_specs=whole,
        compiler_params=params,
        cost_estimate=cost(10**6, 200000),
        name="pack",
    )(frame_count, features.reshape(96, 1024), norm1_gain[None], norm1_shift[None])
    mine = lax.all_to_all(by_frame, ("zh", "zl"), 0, 0, tiled=True)
    masked = (cotangent.reshape(96, 4, 256) * mask.astype(BF)[None, :, None]).reshape(96, 1024)
    lines = masked.reshape(96, 4, 2, 128)
    before, after = halo(lines[:, :, 1].reshape(96, 512), lines[:, :, 0].reshape(96, 512))
    bundle = jnp.concatenate([masked, before, after], axis=1)
    mine, bundle = lax.optimization_barrier((mine, bundle))
    parts = ring(mine, "x")
    others = [permute(p, ("co",), lambda i: (1 - i,)) for p in parts]

    bundle = permute(
        bundle, ("zh", "co", "y"), lambda zh, co, y: (y // 2, y % 2, 2 * zh + co)
    )
    bundle, _ = lax.optimization_barrier((bundle, others[1:]))
    blocks = lax.all_gather(bundle, ("zh", "co"), axis=0)

    frame = 2 * zh + zl // 2
    at = jnp.stack([co, 2 * (zl % 2) + co, valid, frame]).astype(jnp.int32)
    pieces = pl.pallas_call(
        attend_kernel,
        out_shape=[jax.ShapeDtypeStruct((96, 256), BF)] * 4,
        in_specs=[scalars] + [whole] * 12,
        out_specs=[whole] * 4,
        scratch_shapes=[
            pltpu.VMEM((384, 4096), BF),
            pltpu.VMEM((256, 4096), F32),
            pltpu.VMEM((384, 256), BF),
        ],
        compiler_params=params,
        cost_estimate=cost(4 * 10**9, 20 * 10**6),
        name="attention",
    )(
        at,
        *parts,
        *others,
        qkv_weight,
        qkv_bias[None],
        out_weight,
        out_bias[:, None],
    )

    pieces = list(pieces)

    for k in range(4):

        def to_channels(zh, co, zl, k=k):
            c = (2 * zh + zl // 2) ^ k
            return (c // 2, c % 2, 2 * (zl % 2) + co)

        pieces[k] = permute(pieces[k], ("zh", "co", "zl"), to_channels)
    hidden, last, leading, packed = pl.pallas_call(
        arrange_kernel,
        out_shape=(
            jax.ShapeDtypeStruct((96, 1024), BF),
            jax.ShapeDtypeStruct((96, 512), BF),
            jax.ShapeDtypeStruct((96, 512), BF),
            jax.ShapeDtypeStruct((64, 1, 128), F32),
        ),
        in_specs=[scalars] + [whole] * 4,
        out_specs=(whole,) * 4,
        scratch_shapes=[pltpu.VMEM((4, 96, 256), BF)],
        compiler_params=params,
        cost_estimate=cost(10**6, 10**6),
        name="arrange",
    )(jnp.stack([ch, valid]).astype(jnp.int32), *pieces)
    clips = ring(hidden, "y")

    packed = lax.all_to_all(packed, ("zl", "x", "y"), 0, 0, tiled=True)
    packed = packed.reshape(16, 4, 1, 128)
    gain, shift = norm2_gain[:, None], norm2_shift[:, None]

    table = pl.pallas_call(
        grad_kernel,
        out_shape=jax.ShapeDtypeStruct((128, 16, 128), BF),
        in_specs=[scalars] + [whole] * 8,
        out_specs=whole,
        scratch_shapes=[
            pltpu.VMEM((896, 4096), BF),
            pltpu.VMEM((288, 4096), BF),
        ],
        compiler_params=params,
        cost_estimate=cost(4 * 10**9, 20 * 10**6),
        name="weight_grad",
    )(y.astype(jnp.int32)[None], packed, *clips, blocks, gain, shift)
    table, conv_weight = lax.optimization_barrier((table, conv_weight))
    kernels = conv_weight.transpose(0, 4, 1, 2, 3).reshape(3, 384, 864)
    kernels, last, leading = lax.optimization_barrier((kernels, last, leading))
    above, below = halo(last, leading)
    shares = lax.all_to_all(table.reshape(16, 8, 16, 128), ("zl", "x"), 0, 0, tiled=True)
    keep, send = pl.pallas_call(
        conv_kernel,
        out_shape=(jax.ShapeDtypeStruct((2, 96, 1024), BF),) * 2,
        in_specs=[scalars] + [whole] * 7,
        out_specs=(whole, whole),
        scratch_shapes=[pltpu.VMEM((864, 1536), BF), pltpu.VMEM((4, 96, 1024), BF)],
        compiler_params=params,
        cost_estimate=cost(3 * 10**9, 12 * 10**6),
        name="convolution",
    )(
        jnp.stack([co, zl * 4 + x, y]).astype(jnp.int32),
        packed,
        clips[0],
        above,
        below,
        kernels,
        gain,
        shift,
    )
    send = permute(send, ("co",), lambda i: (1 - i,))
    summed = keep.astype(F32) + send.astype(F32)
    near = lax.dynamic_index_in_dim(summed, zh, 0, keepdims=False)
    far = lax.dynamic_index_in_dim(summed, 1 - zh, 0, keepdims=False).astype(BF)
    shares, near, far = lax.optimization_barrier((shares, near, far))
    share = jnp.sum(shares.astype(F32), axis=0).astype(BF)
    tables = spread(share, ("zl", "x", "y"), 64).reshape(16, 4, 8, 16, 128)
    weight_grad = pl.pallas_call(
        join_kernel,
        out_shape=jax.ShapeDtypeStruct((2592, 384), F32),
        compiler_params=params,
        cost_estimate=cost(10**6, 6 * 10**6),
        name="join",
    )(tables)
    weight_grad = weight_grad.reshape(3, 3, 3, 96, 384)

    conv = near + permute(far, ("zh",), lambda i: (1 - i,)).astype(F32)
    mixed = hidden.astype(F32) + conv + conv_bias[:, None]
    mixed = (mixed.reshape(96, 4, 256) * mask[None, :, None]).astype(BF)
    return mixed.reshape(96, 1, 4, 2, 128), weight_grad


def solution(mesh):
    cut = Mesh(mesh.devices.reshape(2, 2, 4, 4, 4), ("zh", "co", "zl", "x", "y"))
    ch, ha = ("zh", "co"), ("zl", "x")
    maps = P(ch, "y", None, ha, None)
    placed = (
        maps,
        P("y"),
        P(ch),
        P(ch),
        P(),
        P(),
        P(),
        P(),
        P(ch),
        P(ch),
        P(None, None, None, ch, None),
        P(ch),
        maps,
    )
    return jax.shard_map(
        body,
        mesh=cut,
        in_specs=placed,
        out_specs=(maps, P(None, None, None, ch, None)),
        check_vma=False,
    )
```

```python
import itertools
import jax
import jax.numpy as jnp
from jax import lax
from jax.experimental import pallas as pl
from jax.experimental.pallas import tpu as pltpu
from jax.sharding import Mesh, PartitionSpec as P

EPS = 1e-06
SIZES = {"zh": 2, "co": 2, "zl": 4, "x": 4, "y": 4}
BF, F32 = jnp.bfloat16, jnp.float32
VMEM = 56 * 1024 * 1024


def permute(value, axes, target):
    sizes = [SIZES[a] for a in axes]

    def flat(index):
        at = 0
        for i, n in zip(index, sizes):
            at = at * n + i
        return at

    pairs = []
    for index in itertools.product(*[range(n) for n in sizes]):
        to = target(*index)
        if to is not None:
            pairs.append((flat(index), flat(to)))
    return lax.ppermute(value, axes, pairs)


def ring(value, axis):
    return [value] + [permute(value, (axis,), lambda i: ((i + s) % 4,)) for s in (1, 2, 3)]


def halo(last, first):
    def up(zl, x):
        at = zl * 4 + x + 1
        return (at // 4, at % 4) if at < 16 else None

    def down(zl, x):
        at = zl * 4 + x - 1
        return (at // 4, at % 4) if at >= 0 else None

    return permute(last, ("zl", "x"), up), permute(first, ("zl", "x"), down)


def spread(value, axes, count):
    copies = jnp.broadcast_to(value[None], (count,) + value.shape)
    return lax.all_to_all(copies, axes, 0, 0, tiled=True)


def cost(flops, size):
    return pl.CostEstimate(flops=flops, bytes_accessed=size, transcendentals=0)


def column(rows, place):
    lane = lax.broadcasted_iota(jnp.int32, (96, 128), 1)
    return jnp.sum(jnp.where(lane == place, rows, 0.0), axis=1, keepdims=True)


def pack_kernel(valid, frames, gain, shift, out):
    first = jnp.zeros((96, 128), F32)
    second = jnp.zeros((96, 128), F32)
    for f in range(4):
        data = frames[:, f * 256 : f * 256 + 256]
        out[2 * f, :96] = data
        out[2 * f + 1, :96] = data
        data = jnp.where(f < valid[0], data.astype(F32), 0.0)
        square = data * data
        first += data[:, :128] + data[:, 128:]
        second += square[:, :128] + square[:, 128:]
    row = lax.broadcasted_iota(jnp.int32, (96, 128), 0) // 12
    lane = lax.broadcasted_iota(jnp.int32, (96, 128), 1)
    first = jnp.sum(first, axis=1, keepdims=True)
    second = jnp.sum(second, axis=1, keepdims=True)
    sums = jnp.where(row + 96 == lane, first, jnp.where(row + 104 == lane, second, 0.0))
    sums = jnp.sum(sums, axis=0, keepdims=True)
    left = jnp.concatenate([gain[...], jnp.zeros((1, 32), F32)], axis=1) + sums
    right = jnp.concatenate([shift[...], jnp.zeros((1, 32), F32)], axis=1)
    rest = jnp.concatenate([left, right], axis=1)
    rows = []
    for _ in range(3):
        rounded = rest.astype(BF).astype(F32)
        rows.append(rounded)
        rest = rest - rounded
    rows = jnp.concatenate(rows + [jnp.zeros((13, 256), F32)], axis=0).astype(BF)
    for z in range(8):
        out[z, 96:] = rows


def attend_kernel(
    at,
    own0,
    own1,
    own2,
    own3,
    other0,
    other1,
    other2,
    other3,
    qkv,
    qkv_bias,
    out_weight,
    out_bias,
    piece0,
    piece1,
    piece2,
    piece3,
    tokens,
    scores,
    hidden,
):
    co, slot, valid, frame = at[0], at[1], at[2], at[3]
    count = valid.astype(F32) * (12 * 32 * 128)
    group = lax.broadcasted_iota(jnp.int32, (96, 128), 0) // 12
    entry = lax.broadcasted_iota(jnp.int32, (96, 128), 0)
    for which, parts in ((co, (own0, own1, own2, own3)), (1 - co, (other0, other1, other2, other3))):
        for zh in range(2):
            tables = []
            for s in range(4):
                for zl in range(4):
                    rows = parts[s][zh * 4 + zl, 96:].astype(F32)
                    tables.append(rows[0:1] + rows[1:2] + rows[2:3])
            table = tables[0]
            for other in tables[1:]:
                table = table + other
            left, right = tables[0][:, :128], tables[0][:, 128:]
            mean = column(table[:, :128], group + 96) / count
            var = column(table[:, :128], group + 104) / count - mean * mean
            scale = lax.rsqrt(var + EPS)
            gain = column(left, entry)
            shift = column(right, entry)
            rows = pl.ds(pl.multiple_of((2 * zh + which) * 96, 32), 96)
            for s in range(4):
                for zl in range(4):
                    data = parts[s][zh * 4 + zl, :96].astype(F32)
                    data = (data - mean) * scale * gain + shift
                    to = s * 1024 + zl * 256
                    tokens[rows, to : to + 256] = data.astype(BF)
    lanes = pl.ds(pl.multiple_of(slot * 256, 256), 256)
    queries = lax.dot_general(
        tokens[:, lanes], qkv[:, :384], (((0,), (0,)), ((), ())), preferred_element_type=F32
    )
    queries = (queries + qkv_bias[:, :384]).astype(BF)
    lifted = lax.dot_general(
        queries, qkv[:, 384:768], (((1,), (1,)), ((), ())), preferred_element_type=F32
    ).astype(BF)
    offset = jnp.sum(queries.astype(F32) * qkv_bias[:, 384:768], axis=1, keepdims=True)
    top = jnp.full((256, 128), -jnp.inf, F32)
    for j in range(8):
        piece = jnp.dot(lifted, tokens[:, j * 512 : j * 512 + 512], preferred_element_type=F32)
        piece = (piece + offset) * (384 ** (-0.5))
        scores[:, j * 512 : j * 512 + 512] = piece
        for i in range(4):
            top = jnp.maximum(top, piece[:, i * 128 : i * 128 + 128])
    top = jnp.max(top, axis=1, keepdims=True)
    total = jnp.zeros((256, 128), F32)
    acc = jnp.zeros((256, 384), F32)
    for j in range(8):
        ew = jnp.exp(scores[:, j * 512 : j * 512 + 512] - top)
        for i in range(4):
            total += ew[:, i * 128 : i * 128 + 128]
        acc += lax.dot_general(
            ew.astype(BF),
            tokens[:, j * 512 : j * 512 + 512],
            (((1,), (1,)), ((), ())),
            preferred_element_type=F32,
        )
    total = jnp.sum(total, axis=1, keepdims=True)
    acc = (acc / total).astype(BF)
    attended = jnp.dot(acc, qkv[:, 768:], preferred_element_type=F32)
    attended = (attended + qkv_bias[:, 768:]).astype(BF)
    update = lax.dot_general(
        out_weight[...], attended, (((0,), (1,)), ((), ())), preferred_element_type=F32
    )
    hidden[...] = (update + out_bias[...]).astype(BF)
    for which, part in ((co, own0), (1 - co, other0)):
        for zh in range(2):
            rows = pl.ds(pl.multiple_of((2 * zh + which) * 96, 32), 96)
            raw = part[zh * 4 + slot, :96].astype(F32)
            hidden[rows, :] = (raw + hidden[rows, :].astype(F32)).astype(BF)
    for k, piece in enumerate((piece0, piece1, piece2, piece3)):
        piece[...] = hidden[pl.ds(pl.multiple_of((frame ^ k) * 96, 32), 96), :]


def arrange_kernel(at, piece0, piece1, piece2, piece3, whole, last, leading, sums, held):
    for k, piece in enumerate((piece0, piece1, piece2, piece3)):
        held[at[0] ^ k] = piece[...]
    valid = at[1]
    first = jnp.zeros((96, 128), F32)
    second = jnp.zeros((96, 128), F32)
    for f in range(4):
        data = held[f]
        whole[:, f * 256 : f * 256 + 256] = data
        leading[:, f * 128 : f * 128 + 128] = data[:, :128]
        last[:, f * 128 : f * 128 + 128] = data[:, 128:]
        data = jnp.where(f < valid, data.astype(F32), 0.0)
        square = data * data
        first += data[:, :128] + data[:, 128:]
        second += square[:, :128] + square[:, 128:]
    first = jnp.sum(first, axis=1, keepdims=True)
    second = jnp.sum(second, axis=1, keepdims=True)
    row = lax.broadcasted_iota(jnp.int32, (96, 128), 0) // 12
    lane = lax.broadcasted_iota(jnp.int32, (96, 128), 1)
    table = jnp.where(row == lane, first, jnp.where(row + 8 == lane, second, 0.0))
    table = jnp.sum(table, axis=0, keepdims=True)
    table = table + jnp.where(lane[0:1] == 64, valid.astype(F32) / 16.0, 0.0)
    sums[...] = jnp.broadcast_to(table[None], sums.shape)


def clip_columns(table):
    group = lax.broadcasted_iota(jnp.int32, (96, 128), 0) // 12
    count = column(table, 64) * (12 * 32 * 128)
    mean = column(table, group) / count
    var = column(table, group + 8) / count - mean * mean
    return mean, lax.rsqrt(var + EPS)


def gate(data, columns, gain, shift):
    mean, scale = columns
    u = (data.astype(F32) - mean) * scale * gain[...] + shift[...]
    return u / (1.0 + jnp.exp(-u))


def shifted(g, kx):
    if kx == 1:
        return g
    lane = lax.broadcasted_iota(jnp.int32, g.shape, 1)
    if kx == 0:
        return jnp.where(lane == 0, 0.0, pltpu.roll(g, 1, 1))
    return jnp.where(lane == 127, 0.0, pltpu.roll(g, 127, 1))


def grad_kernel(
    at,
    table,
    clip0,
    clip1,
    clip2,
    clip3,
    near0,
    near1,
    far0,
    far1,
    gain,
    shift,
    out,
    gs,
    cs,
    cot,
    before,
    after,
):
    for i, part in enumerate((near0, near1, far0, far1)):
        cot[i] = part[:, :1024]
        before[i] = part[:, 1024:1536]
        after[i] = part[:, 1536:]
    gs[864:, :] = jnp.zeros((32, 4096), BF)
    for s, hidden in enumerate((clip0, clip1, clip2, clip3)):
        clip = lax.rem(at[0] - s + 4, 4)
        columns = clip_columns(jnp.sum(table[:, clip], axis=0))
        for kt in range(2):
            gs[kt * 288 : kt * 288 + 288, s * 1024 : s * 1024 + (2 - kt) * 256] = jnp.zeros(
                (288, (2 - kt) * 256), BF
            )
        for b in range(8):
            g = gate(hidden[:, b * 128 : b * 128 + 128], columns, gain, shift)
            for kx in range(3):
                piece = shifted(g, kx).astype(BF)
                for kt in range(3):
                    to = b * 128 + (2 - kt) * 256
                    if to < 1024:
                        row = (kt * 3 + kx) * 96
                        gs[row : row + 96, s * 1024 + to : s * 1024 + to + 128] = piece
        k = jnp.where(lax.rem(clip, 2) == at[1], 0, 2) + (clip // 2 ^ at[2])
        cs[96:192, s * 1024 : s * 1024 + 1024] = cot[k]
        for f in range(4):
            to = s * 1024 + f * 256
            cs[0:96, to : to + 128] = cot[k, :, f * 256 + 128 : f * 256 + 256]
            cs[0:96, to + 128 : to + 256] = after[k, :, f * 128 : f * 128 + 128]
            cs[192:288, to : to + 128] = before[k, :, f * 128 : f * 128 + 128]
            cs[192:288, to + 128 : to + 256] = cot[k, :, f * 256 : f * 256 + 128]
    grads = lax.dot_general(
        cs[...], gs[...], (((1,), (1,)), ((), ())), preferred_element_type=F32
    ).astype(BF)
    for t in range(18):
        for l in range(7):
            out[t * 7 + l] = grads[t * 16 : t * 16 + 16, l * 128 : l * 128 + 128]
    out[126:] = jnp.zeros((2, 16, 128), BF)


def join_kernel(at, table0, table1, table2, table3, out, held):
    for s, table in enumerate((table0, table1, table2, table3)):
        held[lax.rem(at[0] - s + 4, 4)] = table[...]
    for ky in range(3):
        for l in range(7):
            blocks = [
                held[j, (ky * 6 + t) * 7 + l] for j in range(4) for t in range(6)
            ]
            flipped = jnp.concatenate(blocks, axis=0).astype(F32).T
            lane = l * 128
            while lane < min(l * 128 + 128, 864):
                block = lane // 96
                end = min((block + 1) * 96, l * 128 + 128)
                row = ((block // 3 * 3 + ky) * 3 + block % 3) * 96 + lane % 96
                out[row : row + end - lane, :] = flipped[lane - l * 128 : end - l * 128, :]
                lane = end


def conv_kernel(at, table, clip, before, after, weight, gain, shift, keep, send, stack, held):
    stack[:, :512] = jnp.zeros((864, 512), BF)
    columns = clip_columns(jnp.sum(table[:, at[2]], axis=0))
    for f in range(4):
        for p in range(4):
            if p == 0:
                g = before[:, f * 128 : f * 128 + 128]
            elif p == 3:
                g = after[:, f * 128 : f * 128 + 128]
            else:
                g = clip[:, f * 256 + p * 128 - 128 : f * 256 + p * 128]
            g = gate(g, columns, gain, shift)
            if p == 0:
                g = jnp.where(at[1] > 0, g, 0.0)
            elif p == 3:
                g = jnp.where(at[1] < 15, g, 0.0)
            for kx in range(3):
                piece = shifted(g, kx).astype(BF)
                for ky in range(3):
                    r = p - ky
                    if 0 <= r < 2:
                        to = 512 + f * 256 + r * 128
                        row = (ky * 3 + kx) * 96
                        stack[row : row + 96, to : to + 128] = piece
    total = jnp.zeros((384, 1024), F32)
    for kt in range(3):
        total = total + jnp.dot(
            weight[kt], stack[:, kt * 256 : kt * 256 + 1024], preferred_element_type=F32
        )
    held[...] = total.astype(BF).reshape(4, 96, 1024)
    for zh in range(2):
        keep[zh] = held[2 * zh + at[0]]
        send[zh] = held[2 * zh + 1 - at[0]]


def body(
    features,
    frame_count,
    norm1_gain,
    norm1_shift,
    qkv_weight,
    qkv_bias,
    out_weight,
    out_bias,
    norm2_gain,
    norm2_shift,
    conv_weight,
    conv_bias,
    cotangent,
):
    zh, co, zl = lax.axis_index("zh"), lax.axis_index("co"), lax.axis_index("zl")
    x, y = lax.axis_index("x"), lax.axis_index("y")
    ch = zh * 2 + co
    params = pltpu.CompilerParams(vmem_limit_bytes=VMEM)
    scalars = pl.BlockSpec(memory_space=pltpu.SMEM)
    whole = pl.BlockSpec(memory_space=pltpu.VMEM)
    valid = frame_count[0]
    mask = (lax.iota(jnp.int32, 4) < valid).astype(F32)

    by_frame = pl.pallas_call(
        pack_kernel,
        out_shape=jax.ShapeDtypeStruct((8, 112, 256), BF),
        in_specs=[scalars, whole, whole, whole],
        out_specs=whole,
        compiler_params=params,
        cost_estimate=cost(10**6, 200000),
        name="pack",
    )(frame_count, features.reshape(96, 1024), norm1_gain[None], norm1_shift[None])
    mine = lax.all_to_all(by_frame, ("zh", "zl"), 0, 0, tiled=True)
    masked = (cotangent.reshape(96, 4, 256) * mask.astype(BF)[None, :, None]).reshape(96, 1024)
    lines = masked.reshape(96, 4, 2, 128)
    before, after = halo(lines[:, :, 1].reshape(96, 512), lines[:, :, 0].reshape(96, 512))
    bundle = jnp.concatenate([masked, before, after], axis=1)
    mine, bundle = lax.optimization_barrier((mine, bundle))
    parts = ring(mine, "x")

    near = [
        permute(
            bundle, ("zh", "co", "y"), lambda zh, co, y: ((y // 2 + k) % 2, y % 2, 2 * zh + co)
        )
        for k in range(2)
    ]

    parts[2], near = lax.optimization_barrier((parts[2], near))
    others = [permute(p, ("co",), lambda i: (1 - i,)) for p in parts]

    frame = 2 * zh + zl // 2
    at = jnp.stack([co, 2 * (zl % 2) + co, valid, frame]).astype(jnp.int32)
    pieces = pl.pallas_call(
        attend_kernel,
        out_shape=[jax.ShapeDtypeStruct((96, 256), BF)] * 4,
        in_specs=[scalars] + [whole] * 12,
        out_specs=[whole] * 4,
        scratch_shapes=[
            pltpu.VMEM((384, 4096), BF),
            pltpu.VMEM((256, 4096), F32),
            pltpu.VMEM((384, 256), BF),
        ],
        compiler_params=params,
        cost_estimate=cost(4 * 10**9, 20 * 10**6),
        name="attention",
    )(
        at,
        *parts,
        *others,
        qkv_weight,
        qkv_bias[None],
        out_weight,
        out_bias[:, None],
    )

    pieces = list(pieces)

    for k in range(4):

        def to_channels(zh, co, zl, k=k):
            c = (2 * zh + zl // 2) ^ k
            return (c // 2, c % 2, 2 * (zl % 2) + co)

        pieces[k] = permute(pieces[k], ("zh", "co", "zl"), to_channels)
    hidden, last, leading, packed = pl.pallas_call(
        arrange_kernel,
        out_shape=(
            jax.ShapeDtypeStruct((96, 1024), BF),
            jax.ShapeDtypeStruct((96, 512), BF),
            jax.ShapeDtypeStruct((96, 512), BF),
            jax.ShapeDtypeStruct((64, 1, 128), F32),
        ),
        in_specs=[scalars] + [whole] * 4,
        out_specs=(whole,) * 4,
        scratch_shapes=[pltpu.VMEM((4, 96, 256), BF)],
        compiler_params=params,
        cost_estimate=cost(10**6, 10**6),
        name="arrange",
    )(jnp.stack([ch, valid]).astype(jnp.int32), *pieces)
    clips = ring(hidden, "y")
    near, _ = lax.optimization_barrier((near, hidden))
    far = [permute(v, ("co",), lambda i: (1 - i,)) for v in near]

    packed = lax.all_to_all(packed, ("zl", "x", "y"), 0, 0, tiled=True)
    packed = packed.reshape(16, 4, 1, 128)
    gain, shift = norm2_gain[:, None], norm2_shift[:, None]

    table = pl.pallas_call(
        grad_kernel,
        out_shape=jax.ShapeDtypeStruct((128, 16, 128), BF),
        in_specs=[scalars] + [whole] * 11,
        out_specs=whole,
        scratch_shapes=[
            pltpu.VMEM((896, 4096), BF),
            pltpu.VMEM((288, 4096), BF),
            pltpu.VMEM((4, 96, 1024), BF),
            pltpu.VMEM((4, 96, 512), BF),
            pltpu.VMEM((4, 96, 512), BF),
        ],
        compiler_params=params,
        cost_estimate=cost(4 * 10**9, 20 * 10**6),
        name="weight_grad",
    )(jnp.stack([y, co, zh]).astype(jnp.int32), packed, *clips, *near, *far, gain, shift)
    table, conv_weight, last, leading = lax.optimization_barrier((table, conv_weight, last, leading))
    above, below = halo(last, leading)
    kernels = conv_weight.transpose(0, 4, 1, 2, 3).reshape(3, 384, 864)
    shares = lax.all_to_all(table.reshape(16, 8, 16, 128), ("zl", "x"), 0, 0, tiled=True)
    keep, send = pl.pallas_call(
        conv_kernel,
        out_shape=(jax.ShapeDtypeStruct((2, 96, 1024), BF),) * 2,
        in_specs=[scalars] + [whole] * 7,
        out_specs=(whole, whole),
        scratch_shapes=[pltpu.VMEM((864, 1536), BF), pltpu.VMEM((4, 96, 1024), BF)],
        compiler_params=params,
        cost_estimate=cost(3 * 10**9, 12 * 10**6),
        name="convolution",
    )(
        jnp.stack([co, zl * 4 + x, y]).astype(jnp.int32),
        packed,
        clips[0],
        above,
        below,
        kernels,
        gain,
        shift,
    )
    send = permute(send, ("co",), lambda i: (1 - i,))
    summed = keep.astype(F32) + send.astype(F32)
    near = lax.dynamic_index_in_dim(summed, zh, 0, keepdims=False)
    far = lax.dynamic_index_in_dim(summed, 1 - zh, 0, keepdims=False).astype(BF)
    shares, near, far = lax.optimization_barrier((shares, near, far))
    share = jnp.sum(shares.astype(F32), axis=0).astype(BF)
    table = spread(share, ("zl", "x"), 16).reshape(128, 16, 128)
    table, near, far = lax.optimization_barrier((table, near, far))
    weight_grad = pl.pallas_call(
        join_kernel,
        out_shape=jax.ShapeDtypeStruct((2592, 384), F32),
        in_specs=[scalars] + [whole] * 4,
        out_specs=whole,
        scratch_shapes=[pltpu.VMEM((4, 128, 16, 128), BF)],
        compiler_params=params,
        cost_estimate=cost(10**6, 6 * 10**6),
        name="join",
    )(y.astype(jnp.int32)[None], *ring(table, "y"))
    weight_grad = weight_grad.reshape(3, 3, 3, 96, 384)

    conv = near + permute(far, ("zh",), lambda i: (1 - i,)).astype(F32)
    mixed = hidden.astype(F32) + conv + conv_bias[:, None]
    mixed = (mixed.reshape(96, 4, 256) * mask[None, :, None]).astype(BF)
    return mixed.reshape(96, 1, 4, 2, 128), weight_grad


def solution(mesh):
    cut = Mesh(mesh.devices.reshape(2, 2, 4, 4, 4), ("zh", "co", "zl", "x", "y"))
    ch, ha = ("zh", "co"), ("zl", "x")
    maps = P(ch, "y", None, ha, None)
    placed = (
        maps,
        P("y"),
        P(ch),
        P(ch),
        P(),
        P(),
        P(),
        P(),
        P(ch),
        P(ch),
        P(None, None, None, ch, None),
        P(ch),
        maps,
    )
    return jax.shard_map(
        body,
        mesh=cut,
        in_specs=placed,
        out_specs=(maps, P(None, None, None, ch, None)),
        check_vma=False,
    )
```

```python
import itertools
import jax
import jax.numpy as jnp
from jax import lax
from jax.experimental import pallas as pl
from jax.experimental.pallas import tpu as pltpu
from jax.sharding import Mesh, PartitionSpec as P

EPS = 1e-06
SIZES = {"zh": 2, "co": 2, "zl": 4, "x": 4, "y": 4}
BF, F32 = jnp.bfloat16, jnp.float32
VMEM = 56 * 1024 * 1024


def permute(value, axes, target):
    sizes = [SIZES[a] for a in axes]

    def flat(index):
        at = 0
        for i, n in zip(index, sizes):
            at = at * n + i
        return at

    pairs = []
    for index in itertools.product(*[range(n) for n in sizes]):
        to = target(*index)
        if to is not None:
            pairs.append((flat(index), flat(to)))
    return lax.ppermute(value, axes, pairs)


def ring(value, axis):
    return [value] + [permute(value, (axis,), lambda i: ((i + s) % 4,)) for s in (1, 2, 3)]


def halo(last, first):
    def up(zl, x):
        at = zl * 4 + x + 1
        return (at // 4, at % 4) if at < 16 else None

    def down(zl, x):
        at = zl * 4 + x - 1
        return (at // 4, at % 4) if at >= 0 else None

    return permute(last, ("zl", "x"), up), permute(first, ("zl", "x"), down)


def spread(value, axes, count):
    copies = jnp.broadcast_to(value[None], (count,) + value.shape)
    return lax.all_to_all(copies, axes, 0, 0, tiled=True)


def cost(flops, size):
    return pl.CostEstimate(flops=flops, bytes_accessed=size, transcendentals=0)


def column(rows, place):
    lane = lax.broadcasted_iota(jnp.int32, (96, 128), 1)
    return jnp.sum(jnp.where(lane == place, rows, 0.0), axis=1, keepdims=True)


def pack_kernel(valid, frames, gain, shift, out):
    first = jnp.zeros((96, 128), F32)
    second = jnp.zeros((96, 128), F32)
    for f in range(4):
        data = frames[:, f * 256 : f * 256 + 256]
        out[2 * f, :96] = data
        out[2 * f + 1, :96] = data
        data = jnp.where(f < valid[0], data.astype(F32), 0.0)
        square = data * data
        first += data[:, :128] + data[:, 128:]
        second += square[:, :128] + square[:, 128:]
    row = lax.broadcasted_iota(jnp.int32, (96, 128), 0) // 12
    lane = lax.broadcasted_iota(jnp.int32, (96, 128), 1)
    first = jnp.sum(first, axis=1, keepdims=True)
    second = jnp.sum(second, axis=1, keepdims=True)
    sums = jnp.where(row + 96 == lane, first, jnp.where(row + 104 == lane, second, 0.0))
    sums = jnp.sum(sums, axis=0, keepdims=True)
    left = jnp.concatenate([gain[...], jnp.zeros((1, 32), F32)], axis=1) + sums
    right = jnp.concatenate([shift[...], jnp.zeros((1, 32), F32)], axis=1)
    rest = jnp.concatenate([left, right], axis=1)
    rows = []
    for _ in range(3):
        rounded = rest.astype(BF).astype(F32)
        rows.append(rounded)
        rest = rest - rounded
    rows = jnp.concatenate(rows + [jnp.zeros((13, 256), F32)], axis=0).astype(BF)
    for z in range(8):
        out[z, 96:] = rows


def attend_kernel(
    at,
    own0,
    own1,
    own2,
    own3,
    other0,
    other1,
    other2,
    other3,
    qkv,
    qkv_bias,
    out_weight,
    out_bias,
    piece0,
    piece1,
    piece2,
    piece3,
    tokens,
    scores,
    hidden,
):
    co, slot, valid, frame = at[0], at[1], at[2], at[3]
    count = valid.astype(F32) * (12 * 32 * 128)
    group = lax.broadcasted_iota(jnp.int32, (96, 128), 0) // 12
    entry = lax.broadcasted_iota(jnp.int32, (96, 128), 0)
    for which, parts in ((co, (own0, own1, own2, own3)), (1 - co, (other0, other1, other2, other3))):
        for zh in range(2):
            tables = []
            for s in range(4):
                for zl in range(4):
                    rows = parts[s][zh * 4 + zl, 96:].astype(F32)
                    tables.append(rows[0:1] + rows[1:2] + rows[2:3])
            table = tables[0]
            for other in tables[1:]:
                table = table + other
            left, right = tables[0][:, :128], tables[0][:, 128:]
            mean = column(table[:, :128], group + 96) / count
            var = column(table[:, :128], group + 104) / count - mean * mean
            scale = lax.rsqrt(var + EPS)
            gain = column(left, entry)
            shift = column(right, entry)
            rows = pl.ds(pl.multiple_of((2 * zh + which) * 96, 32), 96)
            for s in range(4):
                for zl in range(4):
                    data = parts[s][zh * 4 + zl, :96].astype(F32)
                    data = (data - mean) * scale * gain + shift
                    to = s * 1024 + zl * 256
                    tokens[rows, to : to + 256] = data.astype(BF)
    lanes = pl.ds(pl.multiple_of(slot * 256, 256), 256)
    queries = lax.dot_general(
        tokens[:, lanes], qkv[:, :384], (((0,), (0,)), ((), ())), preferred_element_type=F32
    )
    queries = (queries + qkv_bias[:, :384]).astype(BF)
    lifted = lax.dot_general(
        queries, qkv[:, 384:768], (((1,), (1,)), ((), ())), preferred_element_type=F32
    ).astype(BF)
    offset = jnp.sum(queries.astype(F32) * qkv_bias[:, 384:768], axis=1, keepdims=True)
    top = jnp.full((256, 128), -jnp.inf, F32)
    for j in range(8):
        piece = jnp.dot(lifted, tokens[:, j * 512 : j * 512 + 512], preferred_element_type=F32)
        piece = (piece + offset) * (384 ** (-0.5))
        scores[:, j * 512 : j * 512 + 512] = piece
        for i in range(4):
            top = jnp.maximum(top, piece[:, i * 128 : i * 128 + 128])
    top = jnp.max(top, axis=1, keepdims=True)
    total = jnp.zeros((256, 128), F32)
    acc = jnp.zeros((256, 384), F32)
    for j in range(8):
        ew = jnp.exp(scores[:, j * 512 : j * 512 + 512] - top)
        for i in range(4):
            total += ew[:, i * 128 : i * 128 + 128]
        acc += lax.dot_general(
            ew.astype(BF),
            tokens[:, j * 512 : j * 512 + 512],
            (((1,), (1,)), ((), ())),
            preferred_element_type=F32,
        )
    total = jnp.sum(total, axis=1, keepdims=True)
    acc = (acc / total).astype(BF)
    attended = jnp.dot(acc, qkv[:, 768:], preferred_element_type=F32)
    attended = (attended + qkv_bias[:, 768:]).astype(BF)
    update = lax.dot_general(
        out_weight[...], attended, (((0,), (1,)), ((), ())), preferred_element_type=F32
    )
    hidden[...] = (update + out_bias[...]).astype(BF)
    for which, part in ((co, own0), (1 - co, other0)):
        for zh in range(2):
            rows = pl.ds(pl.multiple_of((2 * zh + which) * 96, 32), 96)
            raw = part[zh * 4 + slot, :96].astype(F32)
            hidden[rows, :] = (raw + hidden[rows, :].astype(F32)).astype(BF)
    for k, piece in enumerate((piece0, piece1, piece2, piece3)):
        piece[...] = hidden[pl.ds(pl.multiple_of((frame ^ k) * 96, 32), 96), :]


def arrange_kernel(at, piece0, piece1, piece2, piece3, whole, last, leading, sums, held):
    for k, piece in enumerate((piece0, piece1, piece2, piece3)):
        held[at[0] ^ k] = piece[...]
    valid = at[1]
    first = jnp.zeros((96, 128), F32)
    second = jnp.zeros((96, 128), F32)
    for f in range(4):
        data = held[f]
        whole[:, f * 256 : f * 256 + 256] = data
        leading[:, f * 128 : f * 128 + 128] = data[:, :128]
        last[:, f * 128 : f * 128 + 128] = data[:, 128:]
        data = jnp.where(f < valid, data.astype(F32), 0.0)
        square = data * data
        first += data[:, :128] + data[:, 128:]
        second += square[:, :128] + square[:, 128:]
    first = jnp.sum(first, axis=1, keepdims=True)
    second = jnp.sum(second, axis=1, keepdims=True)
    row = lax.broadcasted_iota(jnp.int32, (96, 128), 0) // 12
    lane = lax.broadcasted_iota(jnp.int32, (96, 128), 1)
    table = jnp.where(row == lane, first, jnp.where(row + 8 == lane, second, 0.0))
    table = jnp.sum(table, axis=0, keepdims=True)
    table = table + jnp.where(lane[0:1] == 64, valid.astype(F32) / 16.0, 0.0)
    sums[...] = jnp.broadcast_to(table[None], sums.shape)


def clip_columns(table):
    group = lax.broadcasted_iota(jnp.int32, (96, 128), 0) // 12
    count = column(table, 64) * (12 * 32 * 128)
    mean = column(table, group) / count
    var = column(table, group + 8) / count - mean * mean
    return mean, lax.rsqrt(var + EPS)


def gate(data, columns, gain, shift):
    mean, scale = columns
    u = (data.astype(F32) - mean) * scale * gain[...] + shift[...]
    return u / (1.0 + jnp.exp(-u))


def shifted(g, kx):
    if kx == 1:
        return g
    lane = lax.broadcasted_iota(jnp.int32, g.shape, 1)
    if kx == 0:
        return jnp.where(lane == 0, 0.0, pltpu.roll(g, 1, 1))
    return jnp.where(lane == 127, 0.0, pltpu.roll(g, 127, 1))


def grad_kernel(
    at,
    table,
    clip0,
    clip1,
    clip2,
    clip3,
    near0,
    near1,
    far0,
    far1,
    gain,
    shift,
    out,
    gs,
    cs,
    cot,
    before,
    after,
):
    for i, part in enumerate((near0, near1, far0, far1)):
        cot[i] = part[:, :1024]
        before[i] = part[:, 1024:1536]
        after[i] = part[:, 1536:]
    gs[864:, :] = jnp.zeros((32, 4096), BF)
    for s, hidden in enumerate((clip0, clip1, clip2, clip3)):
        clip = lax.rem(at[0] - s + 4, 4)
        columns = clip_columns(jnp.sum(table[:, clip], axis=0))
        for kt in range(2):
            gs[kt * 288 : kt * 288 + 288, s * 1024 : s * 1024 + (2 - kt) * 256] = jnp.zeros(
                (288, (2 - kt) * 256), BF
            )
        for b in range(8):
            g = gate(hidden[:, b * 128 : b * 128 + 128], columns, gain, shift)
            for kx in range(3):
                piece = shifted(g, kx).astype(BF)
                for kt in range(3):
                    to = b * 128 + (2 - kt) * 256
                    if to < 1024:
                        row = (kt * 3 + kx) * 96
                        gs[row : row + 96, s * 1024 + to : s * 1024 + to + 128] = piece
        k = jnp.where(lax.rem(clip, 2) == at[1], 0, 2) + (clip // 2 ^ at[2])
        cs[96:192, s * 1024 : s * 1024 + 1024] = cot[k]
        for f in range(4):
            to = s * 1024 + f * 256
            cs[0:96, to : to + 128] = cot[k, :, f * 256 + 128 : f * 256 + 256]
            cs[0:96, to + 128 : to + 256] = after[k, :, f * 128 : f * 128 + 128]
            cs[192:288, to : to + 128] = before[k, :, f * 128 : f * 128 + 128]
            cs[192:288, to + 128 : to + 256] = cot[k, :, f * 256 : f * 256 + 128]
    grads = lax.dot_general(
        cs[...], gs[...], (((1,), (1,)), ((), ())), preferred_element_type=F32
    ).astype(BF)
    for t in range(18):
        for l in range(7):
            out[t * 7 + l] = grads[t * 16 : t * 16 + 16, l * 128 : l * 128 + 128]
    out[126:] = jnp.zeros((2, 16, 128), BF)


def join_kernel(tables, out):
    for ky in range(3):
        for l in range(7):
            tiles = [(ky * 6 + t) * 7 + l for t in range(6)]
            blocks = [tables[j, t] for j in range(4) for t in tiles]
            flipped = jnp.concatenate(blocks, axis=0).astype(F32).T
            lane = l * 128
            while lane < min(l * 128 + 128, 864):
                block = lane // 96
                end = min((block + 1) * 96, l * 128 + 128)
                row = ((block // 3 * 3 + ky) * 3 + block % 3) * 96 + lane % 96
                out[row : row + end - lane, :] = flipped[lane - l * 128 : end - l * 128, :]
                lane = end


def conv_kernel(at, table, clip, before, after, weight, gain, shift, keep, send, stack, held):
    stack[:, :512] = jnp.zeros((864, 512), BF)
    columns = clip_columns(jnp.sum(table[:, at[2]], axis=0))
    for f in range(4):
        for p in range(4):
            if p == 0:
                g = before[:, f * 128 : f * 128 + 128]
            elif p == 3:
                g = after[:, f * 128 : f * 128 + 128]
            else:
                g = clip[:, f * 256 + p * 128 - 128 : f * 256 + p * 128]
            g = gate(g, columns, gain, shift)
            if p == 0:
                g = jnp.where(at[1] > 0, g, 0.0)
            elif p == 3:
                g = jnp.where(at[1] < 15, g, 0.0)
            for kx in range(3):
                piece = shifted(g, kx).astype(BF)
                for ky in range(3):
                    r = p - ky
                    if 0 <= r < 2:
                        to = 512 + f * 256 + r * 128
                        row = (ky * 3 + kx) * 96
                        stack[row : row + 96, to : to + 128] = piece
    total = jnp.zeros((384, 1024), F32)
    for kt in range(3):
        total = total + jnp.dot(
            weight[kt], stack[:, kt * 256 : kt * 256 + 1024], preferred_element_type=F32
        )
    held[...] = total.astype(BF).reshape(4, 96, 1024)
    for zh in range(2):
        keep[zh] = held[2 * zh + at[0]]
        send[zh] = held[2 * zh + 1 - at[0]]


def body(
    features,
    frame_count,
    norm1_gain,
    norm1_shift,
    qkv_weight,
    qkv_bias,
    out_weight,
    out_bias,
    norm2_gain,
    norm2_shift,
    conv_weight,
    conv_bias,
    cotangent,
):
    zh, co, zl = lax.axis_index("zh"), lax.axis_index("co"), lax.axis_index("zl")
    x, y = lax.axis_index("x"), lax.axis_index("y")
    ch = zh * 2 + co
    params = pltpu.CompilerParams(vmem_limit_bytes=VMEM)
    scalars = pl.BlockSpec(memory_space=pltpu.SMEM)
    whole = pl.BlockSpec(memory_space=pltpu.VMEM)
    valid = frame_count[0]
    mask = (lax.iota(jnp.int32, 4) < valid).astype(F32)

    by_frame = pl.pallas_call(
        pack_kernel,
        out_shape=jax.ShapeDtypeStruct((8, 112, 256), BF),
        in_specs=[scalars, whole, whole, whole],
        out_specs=whole,
        compiler_params=params,
        cost_estimate=cost(10**6, 200000),
        name="pack",
    )(frame_count, features.reshape(96, 1024), norm1_gain[None], norm1_shift[None])
    mine = lax.all_to_all(by_frame, ("zh", "zl"), 0, 0, tiled=True)
    masked = (cotangent.reshape(96, 4, 256) * mask.astype(BF)[None, :, None]).reshape(96, 1024)
    lines = masked.reshape(96, 4, 2, 128)
    before, after = halo(lines[:, :, 1].reshape(96, 512), lines[:, :, 0].reshape(96, 512))
    bundle = jnp.concatenate([masked, before, after], axis=1)
    mine, bundle = lax.optimization_barrier((mine, bundle))
    parts = ring(mine, "x")

    near = [
        permute(
            bundle, ("zh", "co", "y"), lambda zh, co, y: ((y // 2 + k) % 2, y % 2, 2 * zh + co)
        )
        for k in range(2)
    ]

    parts[2], near = lax.optimization_barrier((parts[2], near))
    others = [permute(p, ("co",), lambda i: (1 - i,)) for p in parts]

    frame = 2 * zh + zl // 2
    at = jnp.stack([co, 2 * (zl % 2) + co, valid, frame]).astype(jnp.int32)
    pieces = pl.pallas_call(
        attend_kernel,
        out_shape=[jax.ShapeDtypeStruct((96, 256), BF)] * 4,
        in_specs=[scalars] + [whole] * 12,
        out_specs=[whole] * 4,
        scratch_shapes=[
            pltpu.VMEM((384, 4096), BF),
            pltpu.VMEM((256, 4096), F32),
            pltpu.VMEM((384, 256), BF),
        ],
        compiler_params=params,
        cost_estimate=cost(4 * 10**9, 20 * 10**6),
        name="attention",
    )(
        at,
        *parts,
        *others,
        qkv_weight,
        qkv_bias[None],
        out_weight,
        out_bias[:, None],
    )

    pieces = list(pieces)

    for k in range(4):

        def to_channels(zh, co, zl, k=k):
            c = (2 * zh + zl // 2) ^ k
            return (c // 2, c % 2, 2 * (zl % 2) + co)

        pieces[k] = permute(pieces[k], ("zh", "co", "zl"), to_channels)
    hidden, last, leading, packed = pl.pallas_call(
        arrange_kernel,
        out_shape=(
            jax.ShapeDtypeStruct((96, 1024), BF),
            jax.ShapeDtypeStruct((96, 512), BF),
            jax.ShapeDtypeStruct((96, 512), BF),
            jax.ShapeDtypeStruct((64, 1, 128), F32),
        ),
        in_specs=[scalars] + [whole] * 4,
        out_specs=(whole,) * 4,
        scratch_shapes=[pltpu.VMEM((4, 96, 256), BF)],
        compiler_params=params,
        cost_estimate=cost(10**6, 10**6),
        name="arrange",
    )(jnp.stack([ch, valid]).astype(jnp.int32), *pieces)
    clips = ring(hidden, "y")
    near, _ = lax.optimization_barrier((near, hidden))
    far = [permute(v, ("co",), lambda i: (1 - i,)) for v in near]

    packed = lax.all_to_all(packed, ("zl", "x", "y"), 0, 0, tiled=True)
    packed = packed.reshape(16, 4, 1, 128)
    gain, shift = norm2_gain[:, None], norm2_shift[:, None]

    table = pl.pallas_call(
        grad_kernel,
        out_shape=jax.ShapeDtypeStruct((128, 16, 128), BF),
        in_specs=[scalars] + [whole] * 11,
        out_specs=whole,
        scratch_shapes=[
            pltpu.VMEM((896, 4096), BF),
            pltpu.VMEM((288, 4096), BF),
            pltpu.VMEM((4, 96, 1024), BF),
            pltpu.VMEM((4, 96, 512), BF),
            pltpu.VMEM((4, 96, 512), BF),
        ],
        compiler_params=params,
        cost_estimate=cost(4 * 10**9, 20 * 10**6),
        name="weight_grad",
    )(jnp.stack([y, co, zh]).astype(jnp.int32), packed, *clips, *near, *far, gain, shift)
    table, conv_weight, last, leading = lax.optimization_barrier((table, conv_weight, last, leading))
    above, below = halo(last, leading)
    kernels = conv_weight.transpose(0, 4, 1, 2, 3).reshape(3, 384, 864)
    shares = lax.all_to_all(table.reshape(16, 8, 16, 128), ("zl", "x"), 0, 0, tiled=True)
    keep, send = pl.pallas_call(
        conv_kernel,
        out_shape=(jax.ShapeDtypeStruct((2, 96, 1024), BF),) * 2,
        in_specs=[scalars] + [whole] * 7,
        out_specs=(whole, whole),
        scratch_shapes=[pltpu.VMEM((864, 1536), BF), pltpu.VMEM((4, 96, 1024), BF)],
        compiler_params=params,
        cost_estimate=cost(3 * 10**9, 12 * 10**6),
        name="convolution",
    )(
        jnp.stack([co, zl * 4 + x, y]).astype(jnp.int32),
        packed,
        clips[0],
        above,
        below,
        kernels,
        gain,
        shift,
    )
    send = permute(send, ("co",), lambda i: (1 - i,))
    summed = keep.astype(F32) + send.astype(F32)
    near = lax.dynamic_index_in_dim(summed, zh, 0, keepdims=False)
    far = lax.dynamic_index_in_dim(summed, 1 - zh, 0, keepdims=False).astype(BF)
    shares, near, far = lax.optimization_barrier((shares, near, far))
    share = jnp.sum(shares.astype(F32), axis=0).astype(BF)
    table = spread(share, ("zl", "x"), 16).reshape(128, 16, 128)
    table, near, far = lax.optimization_barrier((table, near, far))
    weight_grad = pl.pallas_call(
        join_kernel,
        out_shape=jax.ShapeDtypeStruct((2592, 384), F32),
        compiler_params=params,
        cost_estimate=cost(10**6, 6 * 10**6),
        name="join",
    )(spread(table, ("y",), 4).reshape(4, 128, 16, 128))
    weight_grad = weight_grad.reshape(3, 3, 3, 96, 384)

    conv = near + permute(far, ("zh",), lambda i: (1 - i,)).astype(F32)
    mixed = hidden.astype(F32) + conv + conv_bias[:, None]
    mixed = (mixed.reshape(96, 4, 256) * mask[None, :, None]).astype(BF)
    return mixed.reshape(96, 1, 4, 2, 128), weight_grad


def solution(mesh):
    cut = Mesh(mesh.devices.reshape(2, 2, 4, 4, 4), ("zh", "co", "zl", "x", "y"))
    ch, ha = ("zh", "co"), ("zl", "x")
    maps = P(ch, "y", None, ha, None)
    placed = (
        maps,
        P("y"),
        P(ch),
        P(ch),
        P(),
        P(),
        P(),
        P(),
        P(ch),
        P(ch),
        P(None, None, None, ch, None),
        P(ch),
        maps,
    )
    return jax.shard_map(
        body,
        mesh=cut,
        in_specs=placed,
        out_specs=(maps, P(None, None, None, ch, None)),
        check_vma=False,
    )
```

```python
import itertools
import jax
import jax.numpy as jnp
from jax import lax
from jax.experimental import pallas as pl
from jax.experimental.pallas import tpu as pltpu
from jax.sharding import Mesh, PartitionSpec as P

EPS = 1e-06
SIZES = {"zh": 2, "co": 2, "zl": 4, "x": 4, "y": 4}
BF, F32 = jnp.bfloat16, jnp.float32
VMEM = 56 * 1024 * 1024


def permute(value, axes, target):
    sizes = [SIZES[a] for a in axes]

    def flat(index):
        at = 0
        for i, n in zip(index, sizes):
            at = at * n + i
        return at

    pairs = []
    for index in itertools.product(*[range(n) for n in sizes]):
        to = target(*index)
        if to is not None:
            pairs.append((flat(index), flat(to)))
    return lax.ppermute(value, axes, pairs)


def ring(value, axis):
    return [value] + [permute(value, (axis,), lambda i: ((i + s) % 4,)) for s in (1, 2, 3)]


def halo(last, first):
    def up(zl, x):
        at = zl * 4 + x + 1
        return (at // 4, at % 4) if at < 16 else None

    def down(zl, x):
        at = zl * 4 + x - 1
        return (at // 4, at % 4) if at >= 0 else None

    return permute(last, ("zl", "x"), up), permute(first, ("zl", "x"), down)


def spread(value, axes, count):
    copies = jnp.broadcast_to(value[None], (count,) + value.shape)
    return lax.all_to_all(copies, axes, 0, 0, tiled=True)


def cost(flops, size):
    return pl.CostEstimate(flops=flops, bytes_accessed=size, transcendentals=0)


def column(rows, place):
    lane = lax.broadcasted_iota(jnp.int32, (96, 128), 1)
    return jnp.sum(jnp.where(lane == place, rows, 0.0), axis=1, keepdims=True)


def pack_kernel(valid, frames, gain, shift, out):
    first = jnp.zeros((96, 128), F32)
    second = jnp.zeros((96, 128), F32)
    for f in range(4):
        data = frames[:, f * 256 : f * 256 + 256]
        out[2 * f, :96] = data
        out[2 * f + 1, :96] = data
        data = jnp.where(f < valid[0], data.astype(F32), 0.0)
        square = data * data
        first += data[:, :128] + data[:, 128:]
        second += square[:, :128] + square[:, 128:]
    row = lax.broadcasted_iota(jnp.int32, (96, 128), 0) // 12
    lane = lax.broadcasted_iota(jnp.int32, (96, 128), 1)
    first = jnp.sum(first, axis=1, keepdims=True)
    second = jnp.sum(second, axis=1, keepdims=True)
    sums = jnp.where(row + 96 == lane, first, jnp.where(row + 104 == lane, second, 0.0))
    sums = jnp.sum(sums, axis=0, keepdims=True)
    left = jnp.concatenate([gain[...], jnp.zeros((1, 32), F32)], axis=1) + sums
    right = jnp.concatenate([shift[...], jnp.zeros((1, 32), F32)], axis=1)
    rest = jnp.concatenate([left, right], axis=1)
    rows = []
    for _ in range(3):
        rounded = rest.astype(BF).astype(F32)
        rows.append(rounded)
        rest = rest - rounded
    rows = jnp.concatenate(rows + [jnp.zeros((13, 256), F32)], axis=0).astype(BF)
    for z in range(8):
        out[z, 96:] = rows


def attend_kernel(
    at,
    own0,
    own1,
    own2,
    own3,
    other0,
    other1,
    other2,
    other3,
    qkv,
    qkv_bias,
    out_weight,
    out_bias,
    piece0,
    piece1,
    piece2,
    piece3,
    tokens,
    scores,
    hidden,
):
    co, slot, valid, frame = at[0], at[1], at[2], at[3]
    count = valid.astype(F32) * (12 * 32 * 128)
    group = lax.broadcasted_iota(jnp.int32, (96, 128), 0) // 12
    entry = lax.broadcasted_iota(jnp.int32, (96, 128), 0)
    for which, parts in ((co, (own0, own1, own2, own3)), (1 - co, (other0, other1, other2, other3))):
        for zh in range(2):
            tables = []
            for s in range(4):
                for zl in range(4):
                    rows = parts[s][zh * 4 + zl, 96:].astype(F32)
                    tables.append(rows[0:1] + rows[1:2] + rows[2:3])
            table = tables[0]
            for other in tables[1:]:
                table = table + other
            left, right = tables[0][:, :128], tables[0][:, 128:]
            mean = column(table[:, :128], group + 96) / count
            var = column(table[:, :128], group + 104) / count - mean * mean
            scale = lax.rsqrt(var + EPS)
            gain = column(left, entry)
            shift = column(right, entry)
            rows = pl.ds(pl.multiple_of((2 * zh + which) * 96, 32), 96)
            for s in range(4):
                for zl in range(4):
                    data = parts[s][zh * 4 + zl, :96].astype(F32)
                    data = (data - mean) * scale * gain + shift
                    to = s * 1024 + zl * 256
                    tokens[rows, to : to + 256] = data.astype(BF)
    lanes = pl.ds(pl.multiple_of(slot * 256, 256), 256)
    queries = lax.dot_general(
        tokens[:, lanes], qkv[:, :384], (((0,), (0,)), ((), ())), preferred_element_type=F32
    )
    queries = (queries + qkv_bias[:, :384]).astype(BF)
    lifted = lax.dot_general(
        queries, qkv[:, 384:768], (((1,), (1,)), ((), ())), preferred_element_type=F32
    ).astype(BF)
    offset = jnp.sum(queries.astype(F32) * qkv_bias[:, 384:768], axis=1, keepdims=True)
    top = jnp.full((256, 128), -jnp.inf, F32)
    for j in range(8):
        piece = jnp.dot(lifted, tokens[:, j * 512 : j * 512 + 512], preferred_element_type=F32)
        piece = (piece + offset) * (384 ** (-0.5))
        scores[:, j * 512 : j * 512 + 512] = piece
        for i in range(4):
            top = jnp.maximum(top, piece[:, i * 128 : i * 128 + 128])
    top = jnp.max(top, axis=1, keepdims=True)
    total = jnp.zeros((256, 128), F32)
    acc = jnp.zeros((256, 384), F32)
    for j in range(8):
        ew = jnp.exp(scores[:, j * 512 : j * 512 + 512] - top)
        for i in range(4):
            total += ew[:, i * 128 : i * 128 + 128]
        acc += lax.dot_general(
            ew.astype(BF),
            tokens[:, j * 512 : j * 512 + 512],
            (((1,), (1,)), ((), ())),
            preferred_element_type=F32,
        )
    total = jnp.sum(total, axis=1, keepdims=True)
    acc = (acc / total).astype(BF)
    attended = jnp.dot(acc, qkv[:, 768:], preferred_element_type=F32)
    attended = (attended + qkv_bias[:, 768:]).astype(BF)
    update = lax.dot_general(
        out_weight[...], attended, (((0,), (1,)), ((), ())), preferred_element_type=F32
    )
    hidden[...] = (update + out_bias[...]).astype(BF)
    for which, part in ((co, own0), (1 - co, other0)):
        for zh in range(2):
            rows = pl.ds(pl.multiple_of((2 * zh + which) * 96, 32), 96)
            raw = part[zh * 4 + slot, :96].astype(F32)
            hidden[rows, :] = (raw + hidden[rows, :].astype(F32)).astype(BF)
    for k, piece in enumerate((piece0, piece1, piece2, piece3)):
        piece[...] = hidden[pl.ds(pl.multiple_of((frame ^ k) * 96, 32), 96), :]


def arrange_kernel(at, piece0, piece1, piece2, piece3, whole, last, leading, sums, held):
    for k, piece in enumerate((piece0, piece1, piece2, piece3)):
        held[at[0] ^ k] = piece[...]
    valid = at[1]
    first = jnp.zeros((96, 128), F32)
    second = jnp.zeros((96, 128), F32)
    for f in range(4):
        data = held[f]
        whole[:, f * 256 : f * 256 + 256] = data
        leading[:, f * 128 : f * 128 + 128] = data[:, :128]
        last[:, f * 128 : f * 128 + 128] = data[:, 128:]
        data = jnp.where(f < valid, data.astype(F32), 0.0)
        square = data * data
        first += data[:, :128] + data[:, 128:]
        second += square[:, :128] + square[:, 128:]
    first = jnp.sum(first, axis=1, keepdims=True)
    second = jnp.sum(second, axis=1, keepdims=True)
    row = lax.broadcasted_iota(jnp.int32, (96, 128), 0) // 12
    lane = lax.broadcasted_iota(jnp.int32, (96, 128), 1)
    table = jnp.where(row == lane, first, jnp.where(row + 8 == lane, second, 0.0))
    table = jnp.sum(table, axis=0, keepdims=True)
    table = table + jnp.where(lane[0:1] == 64, valid.astype(F32) / 16.0, 0.0)
    sums[...] = jnp.broadcast_to(table[None], sums.shape)


def clip_columns(table):
    group = lax.broadcasted_iota(jnp.int32, (96, 128), 0) // 12
    count = column(table, 64) * (12 * 32 * 128)
    mean = column(table, group) / count
    var = column(table, group + 8) / count - mean * mean
    return mean, lax.rsqrt(var + EPS)


def gate(data, columns, gain, shift):
    mean, scale = columns
    u = (data.astype(F32) - mean) * scale * gain[...] + shift[...]
    return u / (1.0 + jnp.exp(-u))


def shifted(g, kx):
    if kx == 1:
        return g
    lane = lax.broadcasted_iota(jnp.int32, g.shape, 1)
    if kx == 0:
        return jnp.where(lane == 0, 0.0, pltpu.roll(g, 1, 1))
    return jnp.where(lane == 127, 0.0, pltpu.roll(g, 127, 1))


def grad_kernel(
    at,
    table,
    clip0,
    clip1,
    clip2,
    clip3,
    near0,
    near1,
    far0,
    far1,
    gain,
    shift,
    out,
    gs,
    cs,
    cot,
    before,
    after,
):
    for i, part in enumerate((near0, near1, far0, far1)):
        cot[i] = part[:, :1024]
        before[i] = part[:, 1024:1536]
        after[i] = part[:, 1536:]
    gs[864:, :] = jnp.zeros((32, 4096), BF)
    for s, hidden in enumerate((clip0, clip1, clip2, clip3)):
        clip = lax.rem(at[0] - s + 4, 4)
        columns = clip_columns(jnp.sum(table[:, clip], axis=0))
        for kt in range(2):
            gs[kt * 288 : kt * 288 + 288, s * 1024 : s * 1024 + (2 - kt) * 256] = jnp.zeros(
                (288, (2 - kt) * 256), BF
            )
        for b in range(8):
            g = gate(hidden[:, b * 128 : b * 128 + 128], columns, gain, shift)
            for kx in range(3):
                piece = shifted(g, kx).astype(BF)
                for kt in range(3):
                    to = b * 128 + (2 - kt) * 256
                    if to < 1024:
                        row = (kt * 3 + kx) * 96
                        gs[row : row + 96, s * 1024 + to : s * 1024 + to + 128] = piece
        k = jnp.where(lax.rem(clip, 2) == at[1], 0, 2) + (clip // 2 ^ at[2])
        cs[96:192, s * 1024 : s * 1024 + 1024] = cot[k]
        for f in range(4):
            to = s * 1024 + f * 256
            cs[0:96, to : to + 128] = cot[k, :, f * 256 + 128 : f * 256 + 256]
            cs[0:96, to + 128 : to + 256] = after[k, :, f * 128 : f * 128 + 128]
            cs[192:288, to : to + 128] = before[k, :, f * 128 : f * 128 + 128]
            cs[192:288, to + 128 : to + 256] = cot[k, :, f * 256 : f * 256 + 128]
    grads = lax.dot_general(
        cs[...], gs[...], (((1,), (1,)), ((), ())), preferred_element_type=F32
    ).astype(BF)
    for t in range(18):
        for l in range(7):
            out[t * 7 + l] = grads[t * 16 : t * 16 + 16, l * 128 : l * 128 + 128]
    out[126:] = jnp.zeros((2, 16, 128), BF)


def join_kernel(at, table0, table1, table2, table3, out, held):
    for s, table in enumerate((table0, table1, table2, table3)):
        held[lax.rem(at[0] - s + 4, 4)] = table[...]
    for ky in range(3):
        for l in range(7):
            blocks = [
                held[j, (ky * 6 + t) * 7 + l] for j in range(4) for t in range(6)
            ]
            flipped = jnp.concatenate(blocks, axis=0).astype(F32).T
            lane = l * 128
            while lane < min(l * 128 + 128, 864):
                block = lane // 96
                end = min((block + 1) * 96, l * 128 + 128)
                row = ((block // 3 * 3 + ky) * 3 + block % 3) * 96 + lane % 96
                out[row : row + end - lane, :] = flipped[lane - l * 128 : end - l * 128, :]
                lane = end


def conv_kernel(at, table, clip, before, after, weight, gain, shift, keep, send, stack, held):
    stack[:, :512] = jnp.zeros((864, 512), BF)
    columns = clip_columns(jnp.sum(table[:, at[2]], axis=0))
    for f in range(4):
        for p in range(4):
            if p == 0:
                g = before[:, f * 128 : f * 128 + 128]
            elif p == 3:
                g = after[:, f * 128 : f * 128 + 128]
            else:
                g = clip[:, f * 256 + p * 128 - 128 : f * 256 + p * 128]
            g = gate(g, columns, gain, shift)
            if p == 0:
                g = jnp.where(at[1] > 0, g, 0.0)
            elif p == 3:
                g = jnp.where(at[1] < 15, g, 0.0)
            for kx in range(3):
                piece = shifted(g, kx).astype(BF)
                for ky in range(3):
                    r = p - ky
                    if 0 <= r < 2:
                        to = 512 + f * 256 + r * 128
                        row = (ky * 3 + kx) * 96
                        stack[row : row + 96, to : to + 128] = piece
    total = jnp.zeros((384, 1024), F32)
    for kt in range(3):
        total = total + jnp.dot(
            weight[kt], stack[:, kt * 256 : kt * 256 + 1024], preferred_element_type=F32
        )
    held[...] = total.astype(BF).reshape(4, 96, 1024)
    for zh in range(2):
        keep[zh] = held[2 * zh + at[0]]
        send[zh] = held[2 * zh + 1 - at[0]]


def body(
    features,
    frame_count,
    norm1_gain,
    norm1_shift,
    qkv_weight,
    qkv_bias,
    out_weight,
    out_bias,
    norm2_gain,
    norm2_shift,
    conv_weight,
    conv_bias,
    cotangent,
):
    zh, co, zl = lax.axis_index("zh"), lax.axis_index("co"), lax.axis_index("zl")
    x, y = lax.axis_index("x"), lax.axis_index("y")
    ch = zh * 2 + co
    params = pltpu.CompilerParams(vmem_limit_bytes=VMEM)
    scalars = pl.BlockSpec(memory_space=pltpu.SMEM)
    whole = pl.BlockSpec(memory_space=pltpu.VMEM)
    valid = frame_count[0]
    mask = (lax.iota(jnp.int32, 4) < valid).astype(F32)

    by_frame = pl.pallas_call(
        pack_kernel,
        out_shape=jax.ShapeDtypeStruct((8, 112, 256), BF),
        in_specs=[scalars, whole, whole, whole],
        out_specs=whole,
        compiler_params=params,
        cost_estimate=cost(10**6, 200000),
        name="pack",
    )(frame_count, features.reshape(96, 1024), norm1_gain[None], norm1_shift[None])
    mine = lax.all_to_all(by_frame, ("zh", "zl"), 0, 0, tiled=True)
    masked = (cotangent.reshape(96, 4, 256) * mask.astype(BF)[None, :, None]).reshape(96, 1024)
    lines = masked.reshape(96, 4, 2, 128)
    before, after = halo(lines[:, :, 1].reshape(96, 512), lines[:, :, 0].reshape(96, 512))
    bundle = jnp.concatenate([masked, before, after], axis=1)
    mine, bundle = lax.optimization_barrier((mine, bundle))
    parts = ring(mine, "x")

    near = [
        permute(
            bundle, ("zh", "co", "y"), lambda zh, co, y: ((y // 2 + k) % 2, y % 2, 2 * zh + co)
        )
        for k in range(2)
    ]

    parts[2], near = lax.optimization_barrier((parts[2], near))
    others = [permute(p, ("co",), lambda i: (1 - i,)) for p in parts]

    frame = 2 * zh + zl // 2
    at = jnp.stack([co, 2 * (zl % 2) + co, valid, frame]).astype(jnp.int32)
    pieces = pl.pallas_call(
        attend_kernel,
        out_shape=[jax.ShapeDtypeStruct((96, 256), BF)] * 4,
        in_specs=[scalars] + [whole] * 12,
        out_specs=[whole] * 4,
        scratch_shapes=[
            pltpu.VMEM((384, 4096), BF),
            pltpu.VMEM((256, 4096), F32),
            pltpu.VMEM((384, 256), BF),
        ],
        compiler_params=params,
        cost_estimate=cost(4 * 10**9, 20 * 10**6),
        name="attention",
    )(
        at,
        *parts,
        *others,
        qkv_weight,
        qkv_bias[None],
        out_weight,
        out_bias[:, None],
    )

    pieces = list(pieces)

    for k in range(4):

        def to_channels(zh, co, zl, k=k):
            c = (2 * zh + zl // 2) ^ k
            return (c // 2, c % 2, 2 * (zl % 2) + co)

        pieces[k] = permute(pieces[k], ("zh", "co", "zl"), to_channels)
    hidden, last, leading, packed = pl.pallas_call(
        arrange_kernel,
        out_shape=(
            jax.ShapeDtypeStruct((96, 1024), BF),
            jax.ShapeDtypeStruct((96, 512), BF),
            jax.ShapeDtypeStruct((96, 512), BF),
            jax.ShapeDtypeStruct((64, 1, 128), F32),
        ),
        in_specs=[scalars] + [whole] * 4,
        out_specs=(whole,) * 4,
        scratch_shapes=[pltpu.VMEM((4, 96, 256), BF)],
        compiler_params=params,
        cost_estimate=cost(10**6, 10**6),
        name="arrange",
    )(jnp.stack([ch, valid]).astype(jnp.int32), *pieces)
    clips = ring(hidden, "y")
    near, _ = lax.optimization_barrier((near, hidden))
    far = [permute(v, ("co",), lambda i: (1 - i,)) for v in near]

    packed = lax.all_to_all(packed, ("zl", "x", "y"), 0, 0, tiled=True)
    packed = packed.reshape(16, 4, 1, 128)
    gain, shift = norm2_gain[:, None], norm2_shift[:, None]

    above, below = halo(last, leading)
    clips, above, below = lax.optimization_barrier((clips, above, below))
    table = pl.pallas_call(
        grad_kernel,
        out_shape=jax.ShapeDtypeStruct((128, 16, 128), BF),
        in_specs=[scalars] + [whole] * 11,
        out_specs=whole,
        scratch_shapes=[
            pltpu.VMEM((896, 4096), BF),
            pltpu.VMEM((288, 4096), BF),
            pltpu.VMEM((4, 96, 1024), BF),
            pltpu.VMEM((4, 96, 512), BF),
            pltpu.VMEM((4, 96, 512), BF),
        ],
        compiler_params=params,
        cost_estimate=cost(4 * 10**9, 20 * 10**6),
        name="weight_grad",
    )(jnp.stack([y, co, zh]).astype(jnp.int32), packed, *clips, *near, *far, gain, shift)
    table, conv_weight = lax.optimization_barrier((table, conv_weight))
    kernels = conv_weight.transpose(0, 4, 1, 2, 3).reshape(3, 384, 864)
    shares = lax.all_to_all(table.reshape(16, 8, 16, 128), ("zl", "x"), 0, 0, tiled=True)
    keep, send = pl.pallas_call(
        conv_kernel,
        out_shape=(jax.ShapeDtypeStruct((2, 96, 1024), BF),) * 2,
        in_specs=[scalars] + [whole] * 7,
        out_specs=(whole, whole),
        scratch_shapes=[pltpu.VMEM((864, 1536), BF), pltpu.VMEM((4, 96, 1024), BF)],
        compiler_params=params,
        cost_estimate=cost(3 * 10**9, 12 * 10**6),
        name="convolution",
    )(
        jnp.stack([co, zl * 4 + x, y]).astype(jnp.int32),
        packed,
        clips[0],
        above,
        below,
        kernels,
        gain,
        shift,
    )
    send = permute(send, ("co",), lambda i: (1 - i,))
    summed = keep.astype(F32) + send.astype(F32)
    near = lax.dynamic_index_in_dim(summed, zh, 0, keepdims=False)
    far = lax.dynamic_index_in_dim(summed, 1 - zh, 0, keepdims=False).astype(BF)
    shares, near, far = lax.optimization_barrier((shares, near, far))
    share = jnp.sum(shares.astype(F32), axis=0).astype(BF)
    table = spread(share, ("zl", "x"), 16).reshape(128, 16, 128)
    table, near, far = lax.optimization_barrier((table, near, far))
    weight_grad = pl.pallas_call(
        join_kernel,
        out_shape=jax.ShapeDtypeStruct((2592, 384), F32),
        in_specs=[scalars] + [whole] * 4,
        out_specs=whole,
        scratch_shapes=[pltpu.VMEM((4, 128, 16, 128), BF)],
        compiler_params=params,
        cost_estimate=cost(10**6, 6 * 10**6),
        name="join",
    )(y.astype(jnp.int32)[None], *ring(table, "y"))
    weight_grad = weight_grad.reshape(3, 3, 3, 96, 384)

    conv = near + permute(far, ("zh",), lambda i: (1 - i,)).astype(F32)
    mixed = hidden.astype(F32) + conv + conv_bias[:, None]
    mixed = (mixed.reshape(96, 4, 256) * mask[None, :, None]).astype(BF)
    return mixed.reshape(96, 1, 4, 2, 128), weight_grad


def solution(mesh):
    cut = Mesh(mesh.devices.reshape(2, 2, 4, 4, 4), ("zh", "co", "zl", "x", "y"))
    ch, ha = ("zh", "co"), ("zl", "x")
    maps = P(ch, "y", None, ha, None)
    placed = (
        maps,
        P("y"),
        P(ch),
        P(ch),
        P(),
        P(),
        P(),
        P(),
        P(ch),
        P(ch),
        P(None, None, None, ch, None),
        P(ch),
        maps,
    )
    return jax.shard_map(
        body,
        mesh=cut,
        in_specs=placed,
        out_specs=(maps, P(None, None, None, ch, None)),
        check_vma=False,
    )
```
